32 devices in a mesh: dp: 8 (over z, x), tensor: 4 (over y, core).
Axes of the slice: x: 2, y: 2, z: 4, core: 2. Of those that a mesh axis runs over, the one named last changes fastest.
Arguments:
- frames_input: bfloat16 [8192, 1024], P(('dp', 'tensor')), may hold values from -6 to 6
- out_grad: bfloat16 [8192, 1024], P(('dp', 'tensor')), may hold values from -6 to 6
- lengths: int32 [8], P('dp'), may hold values from 341 to 1024, as said below
- step_count: int32 [1], replicated, may hold values from 2 to 4
- rates: float32 [4], replicated, may hold values from 0.4 to 0.6
- expand_params: float32 [2, 2, 1024, 4096], P(None, None, 'dp', 'tensor'), may hold values from -0.1875 to 0.1875
- expand_first: float32 [2, 1024, 4096], P(None, 'dp', 'tensor'), may hold values from -80 to 80
- expand_second: float32 [2, 1024, 4096], P(None, 'dp', 'tensor'), may hold values from 81.92 to 1310.72
- shrink_params: float32 [2, 2, 4096, 1024], P(None, None, 'tensor', 'dp'), may hold values from -0.1875 to 0.1875
- shrink_first: float32 [2, 4096, 1024], P(None, 'tensor', 'dp'), may hold values from -80 to 80
- shrink_second: float32 [2, 4096, 1024], P(None, 'tensor', 'dp'), may hold values from 81.92 to 1310.72
- project_params: float32 [2, 3, 1024, 1024], P(None, None, 'dp', 'tensor'), may hold values from -0.1875 to 0.1875
- project_first: float32 [3, 1024, 1024], P(None, 'dp', 'tensor'), may hold values from -32 to 32
- project_second: float32 [3, 1024, 1024], P(None, 'dp', 'tensor'), may hold values from 12.288 to 196.608
- mixing_params: float32 [2, 1024, 1024], P(None, 'tensor', 'dp'), may hold values from -0.5 to 0.5
- mixing_first: float32 [1024, 1024], P('tensor', 'dp'), may hold values from -56 to 56
- mixing_second: float32 [1024, 1024], P('tensor', 'dp'), may hold values from 40.96 to 655.36
- gating_params: float32 [2, 2, 1024, 1024], P(None, None, 'dp', 'tensor'), may hold values from -0.1875 to 0.1875
- gating_first: float32 [2, 1024, 1024], P(None, 'dp', 'tensor'), may hold values from -56 to 56
- gating_second: float32 [2, 1024, 1024], P(None, 'dp', 'tensor'), may hold values from 40.96 to 655.36
- kernel_params: float32 [2, 31, 1024], P(None, None, 'tensor'), may hold values from -1 to 1
- kernel_first: float32 [31, 1024], P(None, 'tensor'), may hold values from -56 to 56
- kernel_second: float32 [31, 1024], P(None, 'tensor'), may hold values from 40.96 to 655.36
- merging_params: float32 [2, 1024, 1024], P(None, 'tensor', 'dp'), may hold values from -0.375 to 0.375
- merging_first: float32 [1024, 1024], P('tensor', 'dp'), may hold values from -56 to 56
- merging_second: float32 [1024, 1024], P('tensor', 'dp'), may hold values from 40.96 to 655.36
- gains_params: float32 [2, 5, 1024], replicated, may hold values from 0.5 to 1.5
- gains_first: float32 [5, 1024], replicated, may hold values from -256 to 256
- gains_second: float32 [5, 1024], replicated, may hold values from 819.2 to 13107.2
Outputs:
- frames_out: bfloat16 [8192, 1024], P(('dp', 'tensor'))
- input_grad: bfloat16 [8192, 1024], P(('dp', 'tensor'))
- expand_grad: float32 [2, 1024, 4096], P(None, 'dp', 'tensor')
- expand_mean: float32 [2, 1024, 4096], P(None, 'dp', 'tensor')
- expand_square: float32 [2, 1024, 4096], P(None, 'dp', 'tensor')
- expand_weights: float32 [2, 2, 1024, 4096], P(None, None, 'dp', 'tensor')
- expand_copies: bfloat16 [2, 2, 1024, 4096], P(None, None, 'dp', 'tensor')
- shrink_grad: float32 [2, 4096, 1024], P(None, 'tensor', 'dp')
- shrink_mean: float32 [2, 4096, 1024], P(None, 'tensor', 'dp')
- shrink_square: float32 [2, 4096, 1024], P(None, 'tensor', 'dp')
- shrink_weights: float32 [2, 2, 4096, 1024], P(None, None, 'tensor', 'dp')
- shrink_copies: bfloat16 [2, 2, 4096, 1024], P(None, None, 'tensor', 'dp')
- project_grad: float32 [3, 1024, 1024], P(None, 'dp', 'tensor')
- project_mean: float32 [3, 1024, 1024], P(None, 'dp', 'tensor')
- project_square: float32 [3, 1024, 1024], P(None, 'dp', 'tensor')
- project_weights: float32 [2, 3, 1024, 1024], P(None, None, 'dp', 'tensor')
- project_copies: bfloat16 [2, 3, 1024, 1024], P(None, None, 'dp', 'tensor')
- mixing_grad: float32 [1024, 1024], P('tensor', 'dp')
- mixing_mean: float32 [1024, 1024], P('tensor', 'dp')
- mixing_square: float32 [1024, 1024], P('tensor', 'dp')
- mixing_weights: float32 [2, 1024, 1024], P(None, 'tensor', 'dp')
- mixing_copies: bfloat16 [2, 1024, 1024], P(None, 'tensor', 'dp')
- gating_grad: float32 [2, 1024, 1024], P(None, 'dp', 'tensor')
- gating_mean: float32 [2, 1024, 1024], P(None, 'dp', 'tensor')
- gating_square: float32 [2, 1024, 1024], P(None, 'dp', 'tensor')
- gating_weights: float32 [2, 2, 1024, 1024], P(None, None, 'dp', 'tensor')
- gating_copies: bfloat16 [2, 2, 1024, 1024], P(None, None, 'dp', 'tensor')
- kernel_grad: float32 [31, 1024], P(None, 'tensor')
- kernel_mean: float32 [31, 1024], P(None, 'tensor')
- kernel_square: float32 [31, 1024], P(None, 'tensor')
- kernel_weights: float32 [2, 31, 1024], P(None, None, 'tensor')
- kernel_copies: bfloat16 [2, 31, 1024], P(None, None, 'tensor')
- merging_grad: float32 [1024, 1024], P('tensor', 'dp')
- merging_mean: float32 [1024, 1024], P('tensor', 'dp')
- merging_square: float32 [1024, 1024], P('tensor', 'dp')
- merging_weights: float32 [2, 1024, 1024], P(None, 'tensor', 'dp')
- merging_copies: bfloat16 [2, 1024, 1024], P(None, 'tensor', 'dp')
- gains_grad: float32 [5, 1024], replicated
- gains_mean: float32 [5, 1024], replicated
- gains_square: float32 [5, 1024], replicated
- gains_weights: float32 [2, 5, 1024], replicated
- gains_copies: bfloat16 [2, 5, 1024], replicated
- trust_norms: float32 [17, 2], replicated
The draws below stay inside these ranges and needn't reach their ends.
Inputs may be any that keep to these rules, and one draw needn't show every extreme that they name: `lengths`: each item's length lies between 341 and 1024; some item fills its whole slot.
All inputs are finite; a program needn't handle non-finite values.
Results may differ from the reference program's by a relative error of at most 0.014.
Values may be sent and summed in bfloat16 or wider, within the bound.
A program may use at most 192 MiB of HBM per device.

```python
import math
import jax
import jax.numpy as jnp
from jax import lax

D = 1024
HEADS = 16
HEAD_DIM = 64
FF = 4096
CONV = 1024
KERNEL = 31
SLOT = 1024
BLOCK = 512
ITEMS = 8
FRAMES = 8192


def draw_lengths(key, part):
    long_lengths = jax.random.randint(jax.random.fold_in(key, 11), (ITEMS,), SLOT * 7 // 8, SLOT + 1)
    short_flags = jax.random.randint(jax.random.fold_in(key, 12), (ITEMS,), 0, 8) == 0
    lengths = jnp.where(short_flags, SLOT // 3, long_lengths)
    picked = jax.random.randint(jax.random.fold_in(key, 13), (), 0, ITEMS)
    lengths = jnp.where(jnp.arange(ITEMS) == picked, SLOT, lengths)
    return lengths.astype(jnp.int32)


def shard_levels(own_key, extent, shards, least, high):
    def one(dim, shards_of):
        steps = jax.random.uniform(jax.random.fold_in(jax.random.fold_in(own_key, 6), dim), (shards_of,), jnp.float32, least / len(shards), high / len(shards))
        return jnp.repeat(jnp.exp(steps), extent[dim] // shards_of).reshape((-1,) + (1,) * (len(extent) - dim - 1))

    gain = one(*shards[0])
    for cut in shards[1:]:
        gain = gain * one(*cut)
    return gain


def normal_values(key, extent, scale, limit, pieces=(), kind=jnp.bfloat16):
    gain = shard_levels(key, extent, pieces, -0.22, 0.18) if pieces else 1.0
    array = jax.random.normal(key, extent, jnp.float32) * scale * gain
    return jnp.minimum(jnp.maximum(array, -limit), limit).astype(kind)


def setup_inputs(seed: int = 0) -> dict:
    key_of = jax.random.split(jax.random.key(seed), 30)
    frames_input = normal_values(key_of[0], (FRAMES, D), 1.0, 6.0, ((0, 32),))
    out_grad = normal_values(key_of[1], (FRAMES, D), 1.0, 6.0, ((0, 32),))
    lengths = draw_lengths(jax.random.fold_in(key_of[29], 71), 0)
    step_count = jax.random.randint(key_of[3], (1,), 2, 5).astype(jnp.int32)
    rates = jnp.clip(jax.random.uniform(key_of[4], (4,), jnp.float32, 0.4, 0.6), 0.4, 0.6)
    expand_params = normal_values(key_of[5], (2, 2, D, FF), D ** -0.5, 0.1875, ((2, 8), (3, 4)), jnp.float32)
    expand_first = normal_values(key_of[6], (2, D, FF), ((0.02 * FRAMES) ** 0.5), 80.0, ((1, 8), (2, 4)), jnp.float32)
    expand_second = jnp.clip(jnp.exp(math.log(1310.72) - 2.7725887 * jax.random.uniform(key_of[7], (2, D, FF), jnp.float32) ** shard_levels(key_of[7], (2, D, FF), ((1, 8), (2, 4)), -0.2, 0.2)), 81.92, 1310.72)
    shrink_params = normal_values(key_of[8], (2, 2, FF, D), (FF // 4) ** -0.5, 0.1875, ((2, 4), (3, 8)), jnp.float32)
    shrink_first = normal_values(key_of[9], (2, FF, D), ((0.02 * FRAMES) ** 0.5), 80.0, ((1, 4), (2, 8)), jnp.float32)
    shrink_second = jnp.clip(jnp.exp(math.log(1310.72) - 2.7725887 * jax.random.uniform(key_of[10], (2, FF, D), jnp.float32) ** shard_levels(key_of[10], (2, FF, D), ((1, 4), (2, 8)), -0.2, 0.2)), 81.92, 1310.72)
    project_params = normal_values(key_of[11], (2, 3, D, D), D ** -0.5, 0.1875, ((2, 8), (3, 4)), jnp.float32)
    project_first = normal_values(key_of[12], (3, D, D), ((0.003 * FRAMES) ** 0.5), 32.0, ((1, 8), (2, 4)), jnp.float32)
    project_second = jnp.clip(jnp.exp(math.log(196.608) - 2.7725887 * jax.random.uniform(key_of[13], (3, D, D), jnp.float32) ** shard_levels(key_of[13], (3, D, D), ((1, 8), (2, 4)), -0.2, 0.2)), 12.288, 196.608)
    mixing_params = normal_values(key_of[14], (2, D, D), (D // 8) ** -0.5, 0.5, ((1, 4), (2, 8)), jnp.float32)
    mixing_first = normal_values(key_of[15], (D, D), ((0.01 * FRAMES) ** 0.5), 56.0, ((0, 4), (1, 8)), jnp.float32)
    mixing_second = jnp.clip(jnp.exp(math.log(655.36) - 2.7725887 * jax.random.uniform(key_of[16], (D, D), jnp.float32) ** shard_levels(key_of[16], (D, D), ((0, 4), (1, 8)), -0.2, 0.2)), 40.96, 655.36)
    gating_params = normal_values(key_of[17], (2, 2, D, CONV), D ** -0.5, 0.1875, ((2, 8), (3, 4)), jnp.float32)
    gating_first = normal_values(key_of[18], (2, D, CONV), ((0.01 * FRAMES) ** 0.5), 56.0, ((1, 8), (2, 4)), jnp.float32)
    gating_second = jnp.clip(jnp.exp(math.log(655.36) - 2.7725887 * jax.random.uniform(key_of[19], (2, D, CONV), jnp.float32) ** shard_levels(key_of[19], (2, D, CONV), ((1, 8), (2, 4)), -0.2, 0.2)), 40.96, 655.36)
    kernel_params = normal_values(key_of[20], (2, KERNEL, CONV), KERNEL ** -0.5, 1.0, ((2, 4),), jnp.float32)
    kernel_first = normal_values(key_of[21], (KERNEL, CONV), ((0.01 * FRAMES) ** 0.5), 56.0, ((1, 4),), jnp.float32)
    kernel_second = jnp.clip(jnp.exp(math.log(655.36) - 2.7725887 * jax.random.uniform(key_of[22], (KERNEL, CONV), jnp.float32) ** shard_levels(key_of[22], (KERNEL, CONV), ((1, 4),), -0.2, 0.2)), 40.96, 655.36)
    merging_params = normal_values(key_of[23], (2, CONV, D), (CONV // 4) ** -0.5, 0.375, ((1, 4), (2, 8)), jnp.float32)
    merging_first = normal_values(key_of[24], (CONV, D), ((0.01 * FRAMES) ** 0.5), 56.0, ((0, 4), (1, 8)), jnp.float32)
    merging_second = jnp.clip(jnp.exp(math.log(655.36) - 2.7725887 * jax.random.uniform(key_of[25], (CONV, D), jnp.float32) ** shard_levels(key_of[25], (CONV, D), ((0, 4), (1, 8)), -0.2, 0.2)), 40.96, 655.36)
    gains_params = jnp.clip(1.0 + 0.1 * jax.random.normal(key_of[26], (2, 5, D), jnp.float32), 0.5, 1.5)
    gains_first = normal_values(key_of[27], (5, D), ((0.2 * FRAMES) ** 0.5), 256.0, (), jnp.float32)
    gains_second = jnp.clip(jnp.exp(jax.random.uniform(key_of[28], (5, D), jnp.float32, math.log(819.2), math.log(13107.2))), 819.2, 13107.2)
    return {"frames_input": frames_input, "out_grad": out_grad, "lengths": lengths, "step_count": step_count, "rates": rates, "expand_params": expand_params, "expand_first": expand_first, "expand_second": expand_second, "shrink_params": shrink_params, "shrink_first": shrink_first, "shrink_second": shrink_second, "project_params": project_params, "project_first": project_first, "project_second": project_second, "mixing_params": mixing_params, "mixing_first": mixing_first, "mixing_second": mixing_second, "gating_params": gating_params, "gating_first": gating_first, "gating_second": gating_second, "kernel_params": kernel_params, "kernel_first": kernel_first, "kernel_second": kernel_second, "merging_params": merging_params, "merging_first": merging_first, "merging_second": merging_second, "gains_params": gains_params, "gains_first": gains_first, "gains_second": gains_second}


EPSILON = 1e-05
ADAM_EPS = 1e-06
DECAY_RATE = 0.01
MASKED = -1000000000.0
HIGH = lax.Precision.HIGHEST

@jax.custom_vjp
def low(v):
    return lax.optimization_barrier(v.astype(jnp.bfloat16)).astype(jnp.float32)

@jax.custom_vjp
def low_back(v):
    return v

def low_keep(v):
    return (low(v), None)

def low_pass(kept, grad):
    return (grad,)

def back_keep(v):
    return (v, None)

def back_low(kept, grad):
    return (low(grad),)
low.defvjp(low_keep, low_pass)
low_back.defvjp(back_keep, back_low)

def normalize(hidden, gain_row):
    center = hidden - lax.optimization_barrier(jnp.mean(hidden, axis=-1, keepdims=True))
    spread = lax.optimization_barrier(jnp.mean(center * center, axis=-1, keepdims=True))
    return center * lax.rsqrt(spread + EPSILON) * gain_row

def feed_forward(normed, expand_matrix, shrink_matrix):
    before = low_back(jnp.dot(normed, expand_matrix, precision=HIGH))
    hidden = low(jax.nn.silu(before))
    return low_back(jnp.dot(hidden, shrink_matrix, precision=HIGH))

def attention(normed, project_matrix, mixing_matrix, live_keys):
    packed = low(low_back(jnp.einsum('sd,kde->kse', normed, project_matrix, precision=HIGH)))
    queries = packed[0].reshape(SLOT, HEADS, HEAD_DIM)
    keys_all = packed[1].reshape(SLOT, HEADS, HEAD_DIM)
    values_all = packed[2].reshape(SLOT, HEADS, HEAD_DIM)
    score_scale = HEAD_DIM ** (-0.5)

    def one_block(query_block):
        scores = low_back(jnp.einsum('bhe,khe->hbk', query_block, keys_all, precision=HIGH) * score_scale)
        scores = jnp.where(live_keys[None, None, :], scores, MASKED)
        weights = low(jax.nn.softmax(scores, axis=-1))
        return jnp.einsum('hbk,khe->bhe', weights, values_all, precision=HIGH)
    blocks = lax.map(jax.checkpoint(one_block), queries.reshape(SLOT // BLOCK, BLOCK, HEADS, HEAD_DIM))
    mixed_heads = low(low_back(blocks.reshape(SLOT, D)))
    return low_back(jnp.dot(mixed_heads, mixing_matrix, precision=HIGH))

def convolve(normed, gating_matrix, kernel_taps, merging_matrix, live_frames):
    gated_pair = low_back(jnp.einsum('sd,kdc->ksc', normed, gating_matrix, precision=HIGH))
    glu_values = gated_pair[0] * jax.nn.sigmoid(gated_pair[1]) * live_frames[:, None]
    margin = (KERNEL - 1) // 2
    padded = jnp.pad(glu_values, ((margin, margin), (0, 0)))
    mixed_time = padded[0:SLOT] * kernel_taps[0]
    for offset in range(1, KERNEL):
        mixed_time = mixed_time + padded[offset:offset + SLOT] * kernel_taps[offset]
    hidden = low(jax.nn.silu(mixed_time))
    return low_back(jnp.dot(hidden, merging_matrix, precision=HIGH))

def item_forward(frames, live_frames, weights):
    expand_matrix, shrink_matrix, project_matrix, mixing_matrix, gating_matrix, kernel_taps, merging_matrix, gain_rows = weights
    live_keys = live_frames > 0.5
    hidden = frames + 0.5 * feed_forward(low(normalize(frames, gain_rows[0])), expand_matrix[0], shrink_matrix[0])
    hidden = hidden + attention(low(normalize(hidden, gain_rows[1])), project_matrix, mixing_matrix, live_keys)
    hidden = hidden + convolve(low(normalize(hidden, gain_rows[2])), gating_matrix, kernel_taps, merging_matrix, live_frames)
    hidden = hidden + 0.5 * feed_forward(low(normalize(hidden, gain_rows[3])), expand_matrix[1], shrink_matrix[1])
    return normalize(hidden, gain_rows[4])

def rounded(master):
    return master.astype(jnp.bfloat16).astype(jnp.float32)

def add_pair(former, latter):
    return former + latter

def piece_squares(numbers, stacked):
    pieces_count = numbers.shape[0] if stacked else 1
    return lax.optimization_barrier(jnp.sum(jnp.reshape(numbers * numbers, (pieces_count, -1)), axis=1))

def reference(frames_input, out_grad, lengths, step_count, rates, expand_params, expand_first, expand_second, shrink_params, shrink_first, shrink_second, project_params, project_first, project_second, mixing_params, mixing_first, mixing_second, gating_params, gating_first, gating_second, kernel_params, kernel_first, kernel_second, merging_params, merging_first, merging_second, gains_params, gains_first, gains_second):
    weights = (rounded(expand_params[0]), rounded(shrink_params[0]), rounded(project_params[0]), rounded(mixing_params[0]), rounded(gating_params[0]), kernel_params[0], rounded(merging_params[0]), gains_params[0])
    frames = frames_input.astype(jnp.float32).reshape(ITEMS, SLOT, D)
    cotangent = out_grad.astype(jnp.float32).reshape(ITEMS, SLOT, D)
    live = (jnp.arange(SLOT, dtype=jnp.int32)[None, :] < lengths[:, None]).astype(jnp.float32)

    def one_item(totals, inputs):
        frames_item, cotangent_item, live_item = inputs

        def forward(frames_arg, weights_arg):
            return item_forward(frames_arg, live_item, weights_arg)
        outputs, pullback = jax.vjp(forward, frames_item, weights)
        frames_grad, weight_grads = pullback(cotangent_item * live_item[:, None])
        return (jax.tree.map(add_pair, totals, weight_grads), (outputs, frames_grad))
    zeroed = jax.tree.map(jnp.zeros_like, weights)
    totals, (outputs, frame_grads) = lax.scan(one_item, zeroed, (frames, cotangent, live))
    frames_out = outputs.reshape(FRAMES, D).astype(jnp.bfloat16)
    input_grad = frame_grads.reshape(FRAMES, D).astype(jnp.bfloat16)
    beta_one = rates[0]
    beta_two = rates[1]
    average_rate = rates[2]
    learn_rate = rates[3]
    steps_done = step_count[0].astype(jnp.float32)
    bias_one = 1.0 - beta_one ** steps_done
    bias_two = 1.0 - beta_two ** steps_done
    entries = [(totals[0], expand_params, expand_first, expand_second, True, DECAY_RATE), (totals[1], shrink_params, shrink_first, shrink_second, True, DECAY_RATE), (totals[2], project_params, project_first, project_second, True, DECAY_RATE), (totals[3], mixing_params, mixing_first, mixing_second, False, DECAY_RATE), (totals[4], gating_params, gating_first, gating_second, True, DECAY_RATE), (totals[5], kernel_params, kernel_first, kernel_second, False, DECAY_RATE), (totals[6], merging_params, merging_first, merging_second, False, DECAY_RATE), (totals[7], gains_params, gains_first, gains_second, True, 0.0)]
    results = []
    weight_norms = []
    update_norms = []
    for gradient, params, first, second, stacked, decay_weight in entries:
        mean_new = beta_one * first + (1.0 - beta_one) * gradient
        square_new = beta_two * second + (1.0 - beta_two) * gradient * gradient
        direction = mean_new / bias_one / (jnp.sqrt(square_new / bias_two) + ADAM_EPS) + decay_weight * params[0]
        weight_norm = jnp.sqrt(piece_squares(params[0], stacked))
        update_norm = jnp.sqrt(piece_squares(direction, stacked))
        master = params[0]
        if stacked:
            broadcast_shape = (master.shape[0],) + (1,) * (master.ndim - 1)
        else:
            broadcast_shape = (1,) * master.ndim
        trust_ratio = (weight_norm / update_norm).reshape(broadcast_shape)
        master_new = master - learn_rate * trust_ratio * direction
        average_new = average_rate * params[1] + (1.0 - average_rate) * master_new
        weights_new = jnp.stack([master_new, average_new])
        results.extend([gradient, mean_new, square_new, weights_new, weights_new.astype(jnp.bfloat16)])
        weight_norms.append(weight_norm)
        update_norms.append(update_norm)
    trust_norms = jnp.stack([jnp.concatenate(weight_norms), jnp.concatenate(update_norms)], axis=1)
    return (frames_out, input_grad, results[0], results[1], results[2], results[3], results[4], results[5], results[6], results[7], results[8], results[9], results[10], results[11], results[12], results[13], results[14], results[15], results[16], results[17], results[18], results[19], results[20], results[21], results[22], results[23], results[24], results[25], results[26], results[27], results[28], results[29], results[30], results[31], results[32], results[33], results[34], results[35], results[36], results[37], results[38], results[39], trust_norms)
```

```python
import functools
import math
from types import SimpleNamespace

import jax
import jax.numpy as jnp
from jax import lax
from jax.experimental import pallas as pl
from jax.experimental.pallas import tpu as pltpu
from jax.sharding import PartitionSpec as P

HEAD_DIM = 64
KERNEL = 31
BLOCK = 512

EPSILON = 1e-05
ADAM_EPS = 1e-06
DECAY_RATE = 0.01
MASKED = -1000000000.0

F32 = jnp.float32
BF16 = jnp.bfloat16
MESH = pl.DeviceIdType.MESH
STEP = 16
TILE = 256
GRANT = 50 * 1024 * 1024


class Spot:
    def __init__(self, dims):
        self.dims = dims
        self.d = lax.axis_index("dp")
        self.t = lax.axis_index("tensor")
        self.y = lax.div(self.t, 2)
        self.c = lax.rem(self.t, 2)
        self.a = lax.div(self.d, dims.nb)
        self.b = lax.rem(self.d, dims.nb)

    def sibling(self):
        return (self.d, self.y * 2 + 1 - self.c)

    def across(self, j):
        return (self.d, lax.rem(self.y + j, self.dims.ny) * 2 + self.c)

    def slow(self, j):
        return (lax.rem(self.a + j, self.dims.na) * self.dims.nb + self.b, self.t)

    def fast(self, j):
        return (self.a * self.dims.nb + lax.rem(self.b + j, self.dims.nb), self.t)

    def tensor_peers(self):
        return [self.sibling()] + [self.across(j) for j in range(1, self.dims.ny)]

    def data_peers(self):
        return [self.slow(j) for j in range(1, self.dims.na)] + [
            self.fast(j) for j in range(1, self.dims.nb)
        ]


def greet(peers):
    barrier = pltpu.get_barrier_semaphore()
    for peer in peers:
        pl.semaphore_signal(barrier, 1, device_id=peer, device_id_type=MESH)
    pl.semaphore_wait(barrier, len(peers))


def remote(source, target, send, recv, peer):
    return pltpu.make_async_remote_copy(
        src_ref=source,
        dst_ref=target,
        send_sem=send,
        recv_sem=recv,
        device_id=peer,
        device_id_type=MESH,
    )


def loop(count, body, unroll=1):
    def step(i, carry):
        body(i)
        return carry

    lax.fori_loop(0, count, step, 0, unroll=unroll)


def rows_of(i, step=STEP):
    return pl.ds(pl.multiple_of(i * step, step), step)


def call(body, ins, outs, scratch, cid, flops=0, moved=0):
    in_names, out_names, scratch_names = list(ins), list(outs), list(scratch)

    def kernel(*refs):
        names = in_names + out_names + scratch_names
        body(SimpleNamespace(**dict(zip(names, refs))))

    results = pl.pallas_call(
        kernel,
        out_shape=[jax.ShapeDtypeStruct(shape, kind) for shape, kind, _ in outs.values()],
        in_specs=[pl.BlockSpec(memory_space=space) for _, space in ins.values()],
        out_specs=[pl.BlockSpec(memory_space=space) for _, _, space in outs.values()],
        scratch_shapes=list(scratch.values()),
        compiler_params=pltpu.CompilerParams(
            collective_id=cid, has_side_effects=cid is not None, vmem_limit_bytes=GRANT
        ),
        cost_estimate=pl.CostEstimate(flops=flops, bytes_accessed=moved, transcendentals=0),
    )(*[array for array, _ in ins.values()])
    return dict(zip(out_names, results))


VM = pltpu.VMEM
HB = pl.ANY
SM = pltpu.SMEM
SEMS = pltpu.SemaphoreType.DMA


def tagged(prefix, tag, specs):
    return {prefix + name + tag: spec for name, spec in specs.items()}


def bound(refs, prefix, tag, specs):
    return SimpleNamespace(**{name: getattr(refs, prefix + name + tag) for name in specs})


class Gather:
    def __init__(self, tag, dims):
        self.tag, self.dims = tag, dims
        na, nb = dims.na, dims.nb
        m, k = max(nb - 1, 1), max(na - 1, 1)
        self.specs = dict(
            loc=SEMS,
            xs=SEMS((m,)),
            xr=SEMS((m,)),
            us=SEMS((k,)),
            ur=SEMS((k,)),
            ds=SEMS((k,)),
            dr=SEMS((k,)),
            fs=SEMS((2, k, m)),
            fr=SEMS((2, k, m)),
        )
        self.stage = 0

    def scratch(self):
        return tagged("g", self.tag, self.specs)

    def bind(self, refs, spot, source, whole):
        self.sem = bound(refs, "g", self.tag, self.specs)
        self.spot, self.source, self.whole = spot, source, whole
        return self

    def rows(self, d):
        shard = self.source.shape[0]
        return self.whole.at[pl.ds(pl.multiple_of(d * shard, shard), shard)]

    def block(self, a):
        return self.rows(a * self.dims.nb + self.spot.b)

    def hop(self, way, s):
        spot, sem = self.spot, self.sem
        step = 1 if way == 0 else -1
        target = self.block(spot.a - step * (s - 1))
        source = self.source if s == 1 else target
        send, recv = (sem.us, sem.ur) if way == 0 else (sem.ds, sem.dr)
        peer = ((spot.a + step) * self.dims.nb + spot.b, spot.t)
        return remote(source, target, send.at[s - 1], recv.at[s - 1], peer)

    def sends(self, way, s):
        spot, na = self.spot, self.dims.na
        if way == 0:
            return jnp.logical_and(spot.a - (s - 1) >= 0, spot.a + 1 < na)
        return jnp.logical_and(spot.a + (s - 1) < na, spot.a - 1 >= 0)

    def has(self, way, s):
        return self.spot.a - s >= 0 if way == 0 else self.spot.a + s < self.dims.na

    def hand(self, way, s, i):
        block = self.block(self.spot.a - s if way == 0 else self.spot.a + s)
        sem = self.sem
        return remote(
            block, block, sem.fs.at[way, s - 1, i - 1], sem.fr.at[way, s - 1, i - 1], self.spot.fast(i)
        )

    def start(self):
        spot, dims, sem = self.spot, self.dims, self.sem
        mine = self.rows(spot.d)
        if dims.na > 1:
            for way in range(2):

                @pl.when(self.sends(way, 1))
                def _(way=way):
                    self.hop(way, 1).start()

        self.own = [
            remote(self.source, mine, sem.xs.at[j - 1], sem.xr.at[j - 1], spot.fast(j))
            for j in range(1, dims.nb)
        ]
        for copy in self.own:
            copy.start()
        self.local = pltpu.make_async_copy(self.source, mine, sem.loc)
        self.local.start()

    def advance(self):
        dims = self.dims
        self.stage += 1
        s = self.stage
        if s >= dims.na:
            return False
        for way in range(2):

            @pl.when(self.has(way, s))
            def _(way=way):
                self.hop(way, s).wait_recv()
                for i in range(1, dims.nb):
                    self.hand(way, s, i).start()

            if s + 1 < dims.na:

                @pl.when(self.sends(way, s + 1))
                def _(way=way):
                    self.hop(way, s + 1).start()

        return True

    def finish(self):
        dims = self.dims
        while self.advance():
            pass
        self.local.wait()
        for copy in self.own:
            copy.wait()
        for s in range(1, dims.na):
            for way in range(2):

                @pl.when(self.sends(way, s))
                def _(way=way, s=s):
                    self.hop(way, s).wait_send()

                @pl.when(self.has(way, s))
                def _(way=way, s=s):
                    for i in range(1, dims.nb):
                        self.hand(way, s, i).wait()


class Scatter:
    def __init__(self, tag, dims, rows, first, columns):
        self.tag, self.dims, self.size = tag, dims, (rows, columns)
        self.columns = pl.ds(first, columns)
        na, nb = dims.na, dims.nb
        m, k = max(nb - 1, 1), max(na - 1, 1)
        self.specs = dict(
            held=VM((na, rows, columns), BF16),
            one=VM((m, na, rows, columns), BF16),
            two=VM((k, rows, columns), BF16),
            loc=SEMS,
            xs=SEMS((m,)),
            xr=SEMS((m,)),
            zs=SEMS((k,)),
            zr=SEMS((k,)),
        )
        self.stage = 0

    def scratch(self):
        return tagged("s", self.tag, self.specs)

    def bind(self, refs, spot, source, result):
        self.r = bound(refs, "s", self.tag, self.specs)
        self.spot, self.source, self.result = spot, source, result
        return self

    def start(self):
        spot, dims, r = self.spot, self.dims, self.r
        self.first = []
        for j in range(1, dims.nb):
            block = lax.rem(spot.b + j, dims.nb)
            copy = remote(
                self.source.at[:, block, :, self.columns],
                r.one.at[j - 1],
                r.xs.at[j - 1],
                r.xr.at[j - 1],
                spot.fast(j),
            )
            copy.start()
            self.first.append(copy)
        self.local = pltpu.make_async_copy(
            self.source.at[:, spot.b, :, self.columns], r.held, r.loc
        )
        self.local.start()

    def advance(self):
        if self.stage:
            return False
        self.stage = 1
        spot, dims, r = self.spot, self.dims, self.r
        rows, columns = self.size
        self.local.wait()
        for copy in self.first:
            copy.wait_recv()
        if dims.nb > 1:
            for a in range(dims.na):

                def add(i, a=a):
                    rs = rows_of(i)
                    total = r.held[a, rs, :].astype(F32)
                    for j in range(dims.nb - 1):
                        total = total + r.one[j, a, rs, :].astype(F32)
                    r.held[a, rs, :] = total.astype(BF16)

                loop(rows // STEP, add, 2)
        self.second = []
        for j in range(1, dims.na):
            copy = remote(
                r.held.at[lax.rem(spot.a + j, dims.na)],
                r.two.at[j - 1],
                r.zs.at[j - 1],
                r.zr.at[j - 1],
                spot.slow(j),
            )
            copy.start()
            self.second.append(copy)
        return True

    def finish(self):
        self.advance()
        dims, r = self.dims, self.r
        rows, columns = self.size
        for copy in self.second:
            copy.wait_recv()

        def add(i):
            rs = rows_of(i)
            total = r.held[self.spot.a, rs, :].astype(F32)
            for j in range(dims.na - 1):
                total = total + r.two[j, rs, :].astype(F32)
            self.result[rs, self.columns] = total

        loop(rows // STEP, add, 2)
        for copy in self.first + self.second:
            copy.wait_send()


class Edge:
    def __init__(self, dims, gather=True, owner_only=False):
        self.dims, self.gather, self.owner_only = dims, gather, owner_only

    def scratch(self):
        ny, L, D = self.dims.ny, self.dims.L, self.dims.D
        m = max(ny - 1, 1)
        return dict(
            e_own=VM((ny, L, D), F32),
            e_give=VM((ny, L, D), BF16),
            e_take=VM((ny, L, D), BF16),
            e_sum=VM((ny, L, D), BF16),
            e_far=VM((m, ny, L, D), BF16),
            e_ds=SEMS((ny,)),
            e_dr=SEMS((ny,)),
            e_ys=SEMS((m, ny)),
            e_yr=SEMS((m, ny)),
            e_ns=SEMS((ny,)),
            e_nr=SEMS((ny,)),
        )

    def bind(self, refs, spot, normed=None):
        self.refs, self.spot, self.normed = refs, spot, normed
        self.near, self.far, self.handed = {}, {}, {}
        return self

    def put(self, k, columns, part):
        L, refs = self.dims.L, self.refs
        low, high = part[:L], part[L:]
        first = self.spot.c == 0
        refs.e_own[k, :, columns] = jnp.where(first, low, high)
        refs.e_give[k, :, columns] = jnp.where(first, high, low).astype(BF16)

    def start(self, k):
        refs = self.refs
        copy = remote(
            refs.e_give.at[k], refs.e_take.at[k], refs.e_ds.at[k], refs.e_dr.at[k], self.spot.sibling()
        )
        copy.start()
        self.near[k] = copy

    def cross(self, k):
        refs, dims = self.refs, self.dims
        self.near[k].wait_recv()

        def add(i):
            rs = rows_of(i)
            total = refs.e_own[k, rs, :] + refs.e_take[k, rs, :].astype(F32)
            refs.e_own[k, rs, :] = total
            refs.e_sum[k, rs, :] = total.astype(BF16)

        loop(dims.L // STEP, add, 2)
        if not self.owner_only:
            self.far[k] = []
            for j in range(1, dims.ny):
                copy = remote(
                    refs.e_sum.at[k],
                    refs.e_far.at[j - 1, k],
                    refs.e_ys.at[j - 1, k],
                    refs.e_yr.at[j - 1, k],
                    self.spot.across(j),
                )
                copy.start()
                self.far[k].append(copy)

    def cross_owner(self):
        refs, dims = self.refs, self.dims
        copies = []
        for j in range(1, dims.ny):
            copy = remote(
                refs.e_sum.at[lax.rem(self.spot.y + j, dims.ny)],
                refs.e_far.at[j - 1, 0],
                refs.e_ys.at[j - 1, 0],
                refs.e_yr.at[j - 1, 0],
                self.spot.across(j),
            )
            copy.start()
            copies.append(copy)
        self.far[0] = copies

    def total(self, k, rs, slot=None):
        refs = self.refs
        total = refs.e_own[k, rs, :]
        for j in range(self.dims.ny - 1):
            total = total + refs.e_far[j, k if slot is None else slot, rs, :].astype(F32)
        return total

    def settle(self, k, row_fn):
        refs, dims, spot = self.refs, self.dims, self.spot
        for copy in self.far[k]:
            copy.wait_recv()
        base = (k * 2 + spot.c) * dims.L

        def body(i):
            rs = rows_of(i)
            rows = row_fn(self.total(k, rs), k, rs)
            if self.gather:
                target = pl.ds(pl.multiple_of(base + i * STEP, STEP), STEP)
                self.normed[target, :] = rows

        loop(dims.L // STEP, body, 2)
        if self.gather:
            block = self.normed.at[pl.ds(pl.multiple_of(base, dims.L), dims.L)]
            copy = remote(block, block, refs.e_ns.at[k], refs.e_nr.at[k], spot.sibling())
            copy.start()
            self.handed[k] = copy

    def arrived(self, k):
        self.handed[k].wait_recv()

    def drain(self):
        for copy in self.near.values():
            copy.wait_send()
        for copies in self.far.values():
            for copy in copies:
                copy.wait_send()
        for copy in self.handed.values():
            copy.wait_send()


def unit(hidden):
    center = hidden - jnp.mean(hidden, axis=-1, keepdims=True)
    spread = jnp.mean(center * center, axis=-1, keepdims=True)
    inverse = lax.rsqrt(spread + EPSILON)
    return center * inverse, inverse


def unit_back(upstream, xhat, inverse, gain):
    scaled = upstream * gain
    return inverse * (
        scaled
        - jnp.mean(scaled, axis=-1, keepdims=True)
        - xhat * jnp.mean(scaled * xhat, axis=-1, keepdims=True)
    )


def fold(rows):
    return rows[:8] + rows[8:]


def head_kernel(dims, cid, frames, cotangent, gain, expand_shard, shrink_shard):
    ny, L, D = dims.ny, dims.L, dims.D
    beside = Beside(dims, [expand_shard, shrink_shard])
    m = max(ny - 1, 1)
    scratch = dict(
        xs=SEMS((m,)), xr=SEMS((m,)), os=SEMS((m,)), orr=SEMS((m,)), ns=SEMS((ny,)), nr=SEMS((ny,))
    )

    def body(r):
        spot = Spot(dims)
        greet(spot.tensor_peers() + spot.data_peers())
        beside.start(r, spot)
        moves = []
        for j in range(1, ny):
            copy = remote(r.x, r.xh.at[spot.y], r.xs.at[j - 1], r.xr.at[j - 1], spot.across(j))
            copy.start()
            other = remote(r.og, r.ogh.at[spot.y], r.os.at[j - 1], r.orr.at[j - 1], spot.across(j))
            other.start()
            moves.append((copy, other))

        def own_rows(i):
            rs = rows_of(i)
            r.xh[spot.y, rs, :] = r.x[rs, :]
            r.ogh[spot.y, rs, :] = r.og[rs, :]

        loop(L // STEP, own_rows)
        handed = []

        def normalize(y, slot):
            base = (y * 2 + spot.c) * L

            def rows(i):
                xhat, _ = unit(r.xh[y, rows_of(i), :].astype(F32))
                target = pl.ds(pl.multiple_of(base + i * STEP, STEP), STEP)
                r.n[target, :] = (xhat * r.g[...]).astype(BF16)

            loop(L // STEP, rows, 2)
            block = r.n.at[pl.ds(pl.multiple_of(base, L), L)]
            copy = remote(block, block, r.ns.at[slot], r.nr.at[slot], spot.sibling())
            copy.start()
            handed.append(copy)

        normalize(spot.y, 0)
        for j in range(1, ny):
            moves[j - 1][0].wait_recv()
            normalize(lax.rem(spot.y + ny - j, ny), j)
        beside.advance()
        for copy in handed:
            copy.wait()
        for copy, other in moves:
            copy.wait_send()
            other.wait()
        beside.finish()

    return call(
        body,
        dict(
            x=(frames, VM),
            og=(cotangent, VM),
            g=(gain, VM),
        )
        | beside.ins(),
        dict(
            xh=((ny, L, D), BF16, VM),
            ogh=((ny, L, D), BF16, VM),
            n=((dims.S, D), BF16, VM),
        )
        | beside.outs(),
        scratch | beside.scratch(),
        cid,
    )


class Beside:
    def __init__(self, dims, gathers=(), scatters=(), pieces=2):
        self.dims = dims
        self.arrays = list(gathers) + list(scatters)
        self.gathers = len(gathers)
        self.jobs = [(i, Gather(str(i), dims)) for i in range(len(gathers))]
        for i, source in enumerate(scatters):
            rows, width = source.shape[2:]
            count = pieces if width % (pieces * 128) == 0 else 1
            for piece in range(count):
                tag = str(len(self.jobs))
                part = width // count
                self.jobs.append(
                    (self.gathers + i, Scatter(tag, dims, rows, piece * part, part))
                )

    def peers(self, spot):
        return spot.data_peers() if self.jobs else []

    def ins(self):
        return {"bi" + str(i): (source, HB) for i, source in enumerate(self.arrays)}

    def outs(self):
        named = {}
        for i, source in enumerate(self.arrays):
            if i < self.gathers:
                rows, columns = source.shape
                shape = ((rows * self.dims.na * self.dims.nb, columns), BF16, HB)
            else:
                shape = (source.shape[2:], F32, VM)
            named["bo" + str(i)] = shape
        return named

    def scratch(self):
        named = {}
        for _, job in self.jobs:
            named |= job.scratch()
        return named

    def start(self, refs, spot):
        for i, job in self.jobs:
            job.bind(refs, spot, getattr(refs, "bi" + str(i)), getattr(refs, "bo" + str(i))).start()

    def advance(self):
        for _, job in self.jobs:
            job.advance()

    def finish(self):
        for _, job in self.jobs:
            job.finish()


def up_products(r, dims, k):
    m = 2 * dims.L

    def column(j):
        rows, cs = pl.ds(k * m, m), rows_of(j, TILE)
        before = jnp.dot(r.n[rows, :], r.e[:, cs], preferred_element_type=F32)
        gate = jax.nn.sigmoid(before)
        r.u[rows, cs] = (before * gate).astype(BF16)
        r.slope[rows, cs] = (gate * (1.0 + before * (1.0 - gate))).astype(BF16)

    loop(dims.F // TILE, column)


def down_products(edge, k, operand, matrix, dims, width):
    m = 2 * dims.L

    def column(j):
        cs = rows_of(j, TILE)
        part = lax.dot_general(
            operand[pl.ds(k * m, m), :],
            matrix[cs, :],
            (((1,), (1,)), ((), ())),
            preferred_element_type=F32,
        )
        edge.put(k, cs, part)

    loop(width // TILE, column)


def weight_product(result, rows_side, columns_side, dims):
    def block(i):
        cs = rows_of(i, TILE)
        result[cs, :] = lax.dot_general(
            rows_side[:, cs],
            columns_side[...],
            (((0,), (0,)), ((), ())),
            preferred_element_type=F32,
        ).astype(BF16)

    loop(dims.D // TILE, block)


def forward_rows(r, scale):
    def rows(total, k, rs):
        hidden = r.h[k, rs, :].astype(F32) + scale * total
        r.hn[k, rs, :] = hidden
        xhat, _ = unit(hidden)
        return (xhat * r.g[...]).astype(BF16)

    return rows


def backward_rows(r, scale, spot):
    def rows(total, k, rs):
        xhat, inverse = unit(r.h[k, rs, :].astype(F32))
        own = jnp.where(spot.y == k, 1.0, 0.0)
        r.dg[...] += fold(total * xhat) * own
        grad = r.gh[k, rs, :] + unit_back(total, xhat, inverse, r.g[...])
        r.ghn[k, rs, :] = grad
        return (scale * grad).astype(BF16)

    return rows


def ff_forward(dims, cid, normed, expand, shrink, hidden, gain, beside):
    ny, L, D, S, F = dims.ny, dims.L, dims.D, dims.S, dims.F
    edge = Edge(dims)

    def body(r):
        spot = Spot(dims)
        greet(spot.tensor_peers() + beside.peers(spot))
        beside.start(r, spot)
        edge.bind(r, spot, r.nn)
        for k in range(ny):
            up_products(r, dims, k)
            down_products(edge, k, r.u, r.rt, dims, D)
            edge.start(k)
            edge.cross(k)
        beside.advance()
        for k in range(ny):
            edge.settle(k, forward_rows(r, 0.5))
            beside.advance()
        for k in range(ny):
            edge.arrived(k)
        edge.drain()
        beside.finish()

    return call(
        body,
        dict(
            n=(normed, VM),
            e=(expand, VM),
            rt=(shrink, VM),
            h=(hidden, VM),
            g=(gain, VM),
        )
        | beside.ins(),
        dict(
            u=((S, F), BF16, VM),
            slope=((S, F), BF16, VM),
            hn=((ny, L, D), F32, VM),
            nn=((S, D), BF16, VM),
        )
        | beside.outs(),
        edge.scratch() | beside.scratch(),
        cid,
    )


def ff_turn(dims, cid, normed, expand, shrink, hidden, gain, cotangent, beside):
    ny, L, D, S, F = dims.ny, dims.L, dims.D, dims.S, dims.F
    edge = Edge(dims)

    def body(r):
        spot = Spot(dims)
        greet(spot.tensor_peers() + beside.peers(spot))
        beside.start(r, spot)
        edge.bind(r, spot, r.w)
        r.dg[...] = jnp.zeros_like(r.dg)

        def rows(total, k, rs):
            xhat, inverse = unit(r.h[k, rs, :] + 0.5 * total)
            r.fo[k, rs, :] = (xhat * r.g[...]).astype(BF16)
            upstream = r.og[k, rs, :].astype(F32)
            own = jnp.where(spot.y == k, 1.0, 0.0)
            r.dg[...] += fold(upstream * xhat) * own
            grad = unit_back(upstream, xhat, inverse, r.g[...])
            r.ghn[k, rs, :] = grad
            return (0.5 * grad).astype(BF16)

        for k in range(ny):
            up_products(r, dims, k)
            down_products(edge, k, r.u, r.rt, dims, D)
            edge.start(k)
            edge.cross(k)
        beside.advance()
        for k in range(ny):
            edge.settle(k, rows)
        for k in range(ny):
            edge.arrived(k)
        edge.drain()
        beside.finish()

    return call(
        body,
        dict(
            n=(normed, VM),
            e=(expand, VM),
            rt=(shrink, VM),
            h=(hidden, VM),
            g=(gain, VM),
            og=(cotangent, VM),
        )
        | beside.ins(),
        dict(
            u=((S, F), BF16, VM),
            slope=((S, F), BF16, VM),
            fo=((ny, L, D), BF16, VM),
            ghn=((ny, L, D), F32, VM),
            w=((S, D), BF16, VM),
            dg=((8, D), F32, VM),
        )
        | beside.outs(),
        edge.scratch() | beside.scratch(),
        cid,
    )


def ff_back(dims, cid, upstream, expand, shrink, slope, inner, normed, grad, hidden, gain, beside, last):
    ny, L, D, S, F = dims.ny, dims.L, dims.D, dims.S, dims.F
    edge = Edge(dims, gather=not last, owner_only=last)
    m = 2 * L

    def body(r):
        spot = Spot(dims)
        greet(spot.tensor_peers() + beside.peers(spot))
        beside.start(r, spot)
        edge.bind(r, spot, None if last else r.wn)
        r.dg[...] = jnp.zeros_like(r.dg)
        for k in range(ny):

            def column(j, k=k):
                rows, cs = pl.ds(k * m, m), rows_of(j, TILE)
                back = jnp.dot(r.w[rows, :], r.rt[:, cs], preferred_element_type=F32)
                r.db[rows, cs] = (back * r.slope[rows, cs].astype(F32)).astype(BF16)

            loop(F // TILE, column)
            down_products(edge, k, r.db, r.e, dims, D)
            edge.start(k)
            edge.cross(k)
        if last:
            edge.cross_owner()
        weight_product(r.de, r.n, r.db, dims)
        weight_product(r.dr, r.w, r.u, dims)
        beside.advance()
        if last:
            for copy in edge.far[0]:
                copy.wait_recv()

            def rows(i):
                rs = rows_of(i)
                total = edge.total(spot.y, rs, 0)
                xhat, inverse = unit(r.h[spot.y, rs, :].astype(F32))
                r.dg[...] += fold(total * xhat)
                back = r.gh[spot.y, rs, :] + unit_back(total, xhat, inverse, r.g[...])
                r.gin[rs, :] = back.astype(BF16)

            loop(L // STEP, rows, 2)
        else:
            for k in range(ny):
                edge.settle(k, backward_rows(r, 1.0, spot))
            for k in range(ny):
                edge.arrived(k)
        edge.drain()
        beside.finish()

    if last:
        outs = dict(gin=((L, D), BF16, VM))
    else:
        outs = dict(ghn=((ny, L, D), F32, VM), wn=((S, D), BF16, VM))
    return call(
        body,
        dict(
            w=(upstream, VM),
            e=(expand, VM),
            rt=(shrink, VM),
            slope=(slope, VM),
            u=(inner, VM),
            n=(normed, VM),
            gh=(grad, VM),
            h=(hidden, VM),
            g=(gain, VM),
        )
        | beside.ins(),
        outs
        | dict(
            de=((D, F), BF16, VM),
            dr=((D, F), BF16, VM),
            dg=((8, D), F32, VM),
        )
        | beside.outs(),
        dict(db=VM((S, F), BF16)) | edge.scratch() | beside.scratch(),
        cid,
    )


def edge_forward(dims, cid, part, hidden, gain, beside):
    ny, L, D, S = dims.ny, dims.L, dims.D, dims.S
    edge = Edge(dims)

    def body(r):
        spot = Spot(dims)
        greet(spot.tensor_peers() + beside.peers(spot))
        beside.start(r, spot)
        edge.bind(r, spot, r.nn)
        for k in range(ny):
            loop(
                D // TILE,
                lambda j, k=k: edge.put(
                    k, rows_of(j, TILE), r.p[pl.ds(k * 2 * L, 2 * L), rows_of(j, TILE)]
                ),
            )
            edge.start(k)
            edge.cross(k)
        beside.advance()
        for k in range(ny):
            edge.settle(k, forward_rows(r, 1.0))
            beside.advance()
        for k in range(ny):
            edge.arrived(k)
        edge.drain()
        beside.finish()

    return call(
        body,
        dict(p=(part, VM), h=(hidden, VM), g=(gain, VM)) | beside.ins(),
        dict(hn=((ny, L, D), F32, VM), nn=((S, D), BF16, VM)) | beside.outs(),
        edge.scratch() | beside.scratch(),
        cid,
    )


def edge_back(dims, cid, part, grad, hidden, gain, scale, beside):
    ny, L, D, S = dims.ny, dims.L, dims.D, dims.S
    edge = Edge(dims)

    def body(r):
        spot = Spot(dims)
        greet(spot.tensor_peers() + beside.peers(spot))
        beside.start(r, spot)
        edge.bind(r, spot, r.wn)
        r.dg[...] = jnp.zeros_like(r.dg)
        for k in range(ny):
            loop(
                D // TILE,
                lambda j, k=k: edge.put(
                    k, rows_of(j, TILE), r.p[pl.ds(k * 2 * L, 2 * L), rows_of(j, TILE)]
                ),
            )
            edge.start(k)
            edge.cross(k)
        beside.advance()
        for k in range(ny):
            edge.settle(k, backward_rows(r, scale, spot))
        for k in range(ny):
            edge.arrived(k)
        edge.drain()
        beside.finish()

    return call(
        body,
        dict(p=(part, VM), gh=(grad, VM), h=(hidden, VM), g=(gain, VM)) | beside.ins(),
        dict(
            ghn=((ny, L, D), F32, VM),
            wn=((S, D), BF16, VM),
            dg=((8, D), F32, VM),
        )
        | beside.outs(),
        edge.scratch() | beside.scratch(),
        cid,
    )


def direction_of(mean, square, master, rates, decay):
    return mean * rates[4] / (jnp.sqrt(square * rates[5]) + ADAM_EPS) + decay * master


def moments_of(grad, mean, square, rates):
    return (
        rates[0] * mean + (1.0 - rates[0]) * grad,
        rates[1] * square + (1.0 - rates[1]) * grad * grad,
    )


def tile_rows(shape):
    rows, columns = shape[-2:]
    step = min(rows, max(8, 16384 // max(columns, 128)))
    return step if rows % step == 0 and step % 8 == 0 else rows


def eighths(tile):
    rows, columns = tile.shape
    return tile.reshape(rows // 8, 8, columns).sum(axis=0) if rows % 8 == 0 else tile


def flip(result, source, dims):
    def part(j):
        cs = rows_of(j, 128)
        result[cs, :] = source[:, cs].T

    loop(source.shape[1] // 128, part)


PLACES = (0, 1, 2, 3, 4, 6, 5, 7)


def piece_rows(shapes):
    rows, total = {}, 0
    for i in PLACES:
        rows[i] = total
        total += shapes[i][0]
    return rows


class Relay:
    def __init__(self, tag, count, shape):
        self.tag, self.count = tag, count
        k = max(count - 1, 1)
        self.specs = dict(slots=VM((count,) + shape, F32), s=SEMS((k,)), r=SEMS((k,)))

    def scratch(self):
        return tagged("r", self.tag, self.specs)

    def start(self, refs, place, peers, value):
        self.r = bound(refs, "r", self.tag, self.specs)
        r = self.r
        r.slots[place] = value
        self.copies = []
        for j, peer in enumerate(peers):
            copy = remote(r.slots.at[place], r.slots.at[place], r.s.at[j], r.r.at[j], peer)
            copy.start()
            self.copies.append(copy)

    def finish(self):
        for copy in self.copies:
            copy.wait()
        total = self.r.slots[0]
        for i in range(1, self.count):
            total = total + self.r.slots[i]
        return total


def gradient_kernel(dims, cid, rates, entries, scatter, sums, gain_parts, kernel_part):
    D, F, H, C = dims.D, dims.F, dims.H, dims.C
    beside = Beside(dims, scatters=scatter)
    shard = scatter[0].shape[2]
    count_t, count_d = dims.ny * 2, dims.na * dims.nb
    gains_relays = [
        Relay("0", 2, (8, D)), Relay("1", dims.ny, (8, D)),
        Relay("2", dims.na, (8, D)), Relay("3", dims.nb, (8, D)),
    ]
    taps_relays = [Relay("4", dims.na, (KERNEL, C)), Relay("5", dims.nb, (KERNEL, C))]
    norm_relays = [Relay("6", count_t, (24, 128)), Relay("7", count_d, (24, 128))]
    relays = gains_relays + taps_relays + norm_relays
    count = len(entries)
    shapes = [entry[0].shape[1:] for entry in entries]
    scratch = dict(
        nrm=VM((24, 128), F32),
        gains=VM((8, D), F32),
        shr0=VM((shard, F), F32),
        shr1=VM((shard, F), F32),
        mix=VM((shard, H), F32),
        mer=VM((shard, C), F32),
        gsem=SEMS((8 + dims.ny,)),
        isem=SEMS((count, 3)),
    )
    ins = dict(rates=(rates, SM), kp=(kernel_part, VM))
    outs = dict(norms=((24, 128), F32, VM))
    for i, (params, mean, square, _) in enumerate(entries):
        tag = str(i)
        ins |= {"p" + tag: (params, HB), "m" + tag: (mean, HB), "v" + tag: (square, HB)}
        scratch |= {"w" + tag: VM(shapes[i], F32), "n" + tag: VM(shapes[i], F32)}
        scratch |= {"q" + tag: VM(shapes[i], F32)}
        outs |= {"g" + tag: (shapes[i], F32, VM)}
    for i, part in enumerate(gain_parts):
        ins |= {"d" + str(i): (part, VM)}
    for i, array in enumerate(sums):
        ins |= {"s" + str(i): (array, HB)}
    for relay in relays:
        scratch |= relay.scratch()

    def body(r):
        spot = Spot(dims)
        everyone = [(spot.d, lax.rem(spot.t + j, count_t)) for j in range(1, count_t)]
        items = [(lax.rem(spot.d + j, count_d), spot.t) for j in range(1, count_d)]
        greet(everyone + items)
        get = lambda name, i: getattr(r, name + str(i))
        for k, (i, job) in enumerate(beside.jobs):
            target = r.shr0 if i else r.g0.at[0]
            job.bind(r, spot, get("bi", i), target).start()
        loads = []
        for i in range(count):
            triple = [
                pltpu.make_async_copy(get("p", i).at[0], get("w", i), r.isem.at[i, 0]),
                pltpu.make_async_copy(get("m", i), get("n", i), r.isem.at[i, 1]),
                pltpu.make_async_copy(get("v", i), get("q", i), r.isem.at[i, 2]),
            ]
            for copy in triple:
                copy.start()
            loads.append(triple)
        grads = [
            pltpu.make_async_copy(r.s0, r.g0.at[1], r.gsem.at[0]),
            pltpu.make_async_copy(r.s1, r.shr1, r.gsem.at[1]),
            pltpu.make_async_copy(r.s2.at[:, pl.ds(3 * H, H)], r.mix, r.gsem.at[2]),
            pltpu.make_async_copy(r.s3.at[:, pl.ds(2 * C, C)], r.mer, r.gsem.at[3]),
        ]
        grads += [
            pltpu.make_async_copy(r.s2.at[:, pl.ds(k * H, H)], r.g2.at[k], r.gsem.at[4 + k])
            for k in range(3)
        ]
        sides = [
            pltpu.make_async_copy(r.s3.at[:, pl.ds(k * C, C)], r.g4.at[k], r.gsem.at[7 + k])
            for k in range(2)
        ]
        for copy in grads + sides:
            copy.start()

        r.nrm[...] = jnp.zeros_like(r.nrm)
        row = lax.broadcasted_iota(jnp.int32, (24, 128), 0)
        lane = lax.broadcasted_iota(jnp.int32, (24, 128), 1)
        first_piece = piece_rows(shapes)
        loaded = set()

        def norm(i, p, weight=None):
            if i not in loaded:
                loaded.add(i)
                for copy in loads[i]:
                    copy.wait()
            step = tile_rows(shapes[i])
            columns = shapes[i][-1]
            acc_rows = 8 if step % 8 == 0 else step
            zero = jnp.zeros((acc_rows, columns), F32)

            def tile(j, carry):
                rs = pl.ds(pl.multiple_of(j * step, step), step)
                master = get("w", i)[p, rs, :]
                mean, square = moments_of(
                    get("g", i)[p, rs, :], get("n", i)[p, rs, :], get("q", i)[p, rs, :], r.rates
                )
                step_of = direction_of(mean, square, master, r.rates, entries[i][3])
                return (
                    carry[0] + eighths(master * master),
                    carry[1] + eighths(step_of * step_of),
                )

            totals = lax.fori_loop(0, shapes[i][-2] // step, tile, (zero, zero))
            here = row == first_piece[i] + p
            for column, total in enumerate(totals):
                value = jnp.sum(jnp.sum(total, axis=0, keepdims=True), axis=1, keepdims=True)
                if weight is not None:
                    value = value * weight
                r.nrm[...] += jnp.where(jnp.logical_and(here, lane == column), value, 0.0)

        r.gains[...] = jnp.zeros_like(r.gains)
        for k in range(5):
            r.gains[k : k + 1, :] = jnp.sum(get("d", k)[...], axis=0, keepdims=True)
        gains_relays[0].start(r, spot.c, [spot.sibling()], r.gains[...])
        slow = [spot.slow(j) for j in range(1, dims.na)]
        fast = [spot.fast(j) for j in range(1, dims.nb)]
        taps_relays[0].start(r, spot.a, slow, r.kp[...])
        total = gains_relays[0].finish()
        gains_relays[1].start(r, spot.y, [spot.across(j) for j in range(1, dims.ny)], total)
        for copy in grads + sides:
            copy.wait()
        flip(r.g3.at[0], r.mix, dims)
        flip(r.g5.at[0], r.mer, dims)
        total = gains_relays[1].finish()
        gains_relays[2].start(r, spot.a, slow, total)
        for i in (2, 3, 4, 5):
            for p in range(shapes[i][0]):
                norm(i, p)
        jobs = [job for _, job in beside.jobs]
        half = len(jobs) // 2
        jobs[0].advance()
        norm(0, 1)
        for job in jobs[1:half]:
            job.advance()
        flip(r.g1.at[1], r.shr1, dims)
        norm(1, 1)
        total = taps_relays[0].finish()
        taps_relays[1].start(r, spot.b, fast, total)
        total = gains_relays[2].finish()
        gains_relays[3].start(r, spot.b, fast, total)
        for job in jobs[half:]:
            job.advance()
        r.g6[0] = taps_relays[1].finish()
        owner = jnp.where(spot.d == 0, 1.0, 0.0)
        norm(6, 0, owner)
        r.gains[...] = gains_relays[3].finish()
        owner = jnp.where(spot.t == 0, owner, 0.0)
        for k in range(5):
            r.g7[k] = r.gains[k : k + 1, :]
            norm(7, k, owner)
        for job in jobs[:half]:
            job.finish()
        norm(0, 0)
        for job in jobs[half:]:
            job.finish()
        flip(r.g1.at[0], r.shr0, dims)
        norm(1, 0)
        norm_relays[0].start(r, spot.t, everyone, r.nrm[...])
        total = norm_relays[0].finish()
        norm_relays[1].start(r, spot.d, items, total)
        r.norms[...] = norm_relays[1].finish()

    return call(body, ins | beside.ins(), outs, scratch | beside.scratch(), cid)


def update_kernel(dims, rates, norms, entries, grads):
    count = len(entries)
    shapes = [entry[1].shape for entry in entries]
    ins = dict(rates=(rates, SM), norms=(norms, VM))
    outs = dict(trust=((17, 2), F32, VM))
    scratch = dict(isem=SEMS((count, 5)), osem=SEMS((count, 5)))
    for i, (params, mean, square, _) in enumerate(entries):
        tag = str(i)
        shape = shapes[i]
        pair = (2,) + shape
        ins |= {"p" + tag: (params, HB), "m" + tag: (mean, HB), "v" + tag: (square, HB)}
        ins |= {"g" + tag: (grads[i], HB)}
        scratch |= {"w" + tag: VM(pair, F32), "n" + tag: VM(shape, F32)}
        scratch |= {"q" + tag: VM(shape, F32), "h" + tag: VM(shape, F32)}
        scratch |= {"b" + tag: VM(pair, BF16)}
        outs |= {"og" + tag: (shape, F32, HB), "om" + tag: (shape, F32, HB)}
        outs |= {"ov" + tag: (shape, F32, HB), "ow" + tag: (pair, F32, HB)}
        outs |= {"ob" + tag: (pair, BF16, HB)}
    order = [7, 6] + list(range(2, 6)) + [0, 1]

    def body(r):
        get = lambda name, i: getattr(r, name + str(i))
        loads, stores = {}, []
        for i in order:
            moves = (("g", "h"), ("m", "n"), ("v", "q"), ("p", "w"))
            loads[i] = [
                pltpu.make_async_copy(get(source, i), get(target, i), r.isem.at[i, k])
                for k, (source, target) in enumerate(moves)
            ]
            for copy in loads[i]:
                copy.start()
        norms = jnp.sqrt(r.norms[...])
        r.trust[...] = norms[:17, :2]
        ratio = r.rates[3] * norms[:, 0:1] / norms[:, 1:2]

        def send(i, name, target, k):
            copy = pltpu.make_async_copy(get(name, i), get(target, i), r.osem.at[i, k])
            copy.start()
            stores.append(copy)

        for i in order:
            for copy in loads[i]:
                copy.wait()
            send(i, "h", "og", 0)
            step = tile_rows(shapes[i])
            offset = piece_rows(shapes)[i]
            for p in range(shapes[i][0]):
                scale = ratio[offset + p : offset + p + 1, :]

                def tile(j, p=p, i=i, step=step, scale=scale):
                    rs = pl.ds(pl.multiple_of(j * step, step), step)
                    master = get("w", i)[0, p, rs, :]
                    mean, square = moments_of(
                        get("h", i)[p, rs, :], get("n", i)[p, rs, :], get("q", i)[p, rs, :], r.rates
                    )
                    move = direction_of(mean, square, master, r.rates, entries[i][3])
                    master = master - scale * move
                    average = get("w", i)[1, p, rs, :]
                    average = r.rates[2] * average + (1.0 - r.rates[2]) * master
                    get("n", i)[p, rs, :] = mean
                    get("q", i)[p, rs, :] = square
                    get("w", i)[0, p, rs, :] = master
                    get("w", i)[1, p, rs, :] = average
                    get("b", i)[0, p, rs, :] = master.astype(BF16)
                    get("b", i)[1, p, rs, :] = average.astype(BF16)

                loop(shapes[i][-2] // step, tile)
            send(i, "n", "om", 1)
            send(i, "q", "ov", 2)
            send(i, "w", "ow", 3)
            send(i, "b", "ob", 4)
        for copy in stores:
            copy.wait()

    return call(body, ins, outs, scratch, None)


def product(operand, another):
    return jnp.dot(operand, another, preferred_element_type=F32)


def product_left(operand, another):
    return lax.dot_general(
        operand, another, (((0,), (0,)), ((), ())), preferred_element_type=F32
    )


def product_right(operand, another):
    return lax.dot_general(
        operand, another, (((1,), (1,)), ((), ())), preferred_element_type=F32
    )


def silu_slope(before):
    sigmoid_of = jax.nn.sigmoid(before)
    return sigmoid_of * (1.0 + before * (1.0 - sigmoid_of))


def attend(queries, keys_all, values_all, live_keys):
    score_scale = HEAD_DIM ** (-0.5)
    slot, heads_local = queries.shape[:2]
    blocks = queries.reshape(slot // BLOCK, BLOCK, heads_local, HEAD_DIM)

    def one_block(query_block):
        scores = (
            jnp.einsum("bhe,khe->hbk", query_block, keys_all, preferred_element_type=F32)
            * score_scale
        )
        scores = jnp.where(live_keys[None, None, :], scores, MASKED)
        row_peak = jnp.max(scores, axis=-1, keepdims=True)
        exponent = jnp.exp(scores - row_peak)
        row_total = jnp.sum(exponent, axis=-1, keepdims=True)
        weights = (exponent / row_total).astype(BF16)
        output = jnp.einsum("hbk,khe->bhe", weights, values_all, preferred_element_type=F32)
        return (output, (row_peak + jnp.log(row_total))[..., 0])

    outputs, logsum = lax.map(one_block, blocks)
    return (outputs.reshape(slot, heads_local, HEAD_DIM), logsum)


def attend_back(queries, keys_all, values_all, live_keys, logsum, grad_out):
    score_scale = HEAD_DIM ** (-0.5)
    slot, heads_local = queries.shape[:2]
    blocks = queries.reshape(slot // BLOCK, BLOCK, heads_local, HEAD_DIM)
    grad_blocks = grad_out.reshape(slot // BLOCK, BLOCK, heads_local, HEAD_DIM)

    def one_block(carried, inputs):
        key_grad, value_grad = carried
        query_block, grad_block, logsum_block = inputs
        scores = (
            jnp.einsum("bhe,khe->hbk", query_block, keys_all, preferred_element_type=F32)
            * score_scale
        )
        scores = jnp.where(live_keys[None, None, :], scores, MASKED)
        probability = jnp.exp(scores - logsum_block[..., None])
        weights = probability.astype(BF16)
        value_grad = value_grad + jnp.einsum(
            "hbk,bhe->khe", weights, grad_block, preferred_element_type=F32
        )
        prob_grad = jnp.einsum(
            "bhe,khe->hbk", grad_block, values_all, preferred_element_type=F32
        )
        row_inner = jnp.sum(probability * prob_grad, axis=-1, keepdims=True)
        score_grad = (probability * (prob_grad - row_inner)).astype(BF16)
        query_grad = (
            jnp.einsum("hbk,khe->bhe", score_grad, keys_all, preferred_element_type=F32)
            * score_scale
        )
        key_grad = (
            key_grad
            + jnp.einsum("hbk,bhe->khe", score_grad, query_block, preferred_element_type=F32)
            * score_scale
        )
        return ((key_grad, value_grad), query_grad)

    zeroed = jnp.zeros((slot, heads_local, HEAD_DIM), F32)
    (key_grad, value_grad), query_grad = lax.scan(
        one_block, (zeroed, zeroed), (blocks, grad_blocks, logsum)
    )
    return (query_grad.reshape(slot, heads_local, HEAD_DIM), key_grad, value_grad)


def attention_forward(dims, normed, matrices, live_keys):
    S, H = dims.S, dims.H
    packed = product(normed, matrices[:, : 3 * H]).astype(BF16)
    queries, keys_all, values_all = (
        packed[:, i * H : (i + 1) * H].reshape(S, H // HEAD_DIM, HEAD_DIM) for i in range(3)
    )
    output, logsum = attend(queries, keys_all, values_all, live_keys)
    mixed_heads = output.reshape(S, H).astype(BF16)
    part = product_right(mixed_heads, matrices[:, 3 * H :])
    return part, (queries, keys_all, values_all, mixed_heads, logsum)


def attention_back(dims, normed, matrices, live_keys, kept, upstream):
    S, H = dims.S, dims.H
    queries, keys_all, values_all, mixed_heads, logsum = kept
    mixing_grad = product_left(upstream, mixed_heads)
    mixed_grad = product(upstream, matrices[:, 3 * H :]).astype(BF16)
    grads = attend_back(
        queries,
        keys_all,
        values_all,
        live_keys,
        logsum,
        mixed_grad.reshape(S, H // HEAD_DIM, HEAD_DIM),
    )
    packed_grad = jnp.concatenate([grad.reshape(S, H).astype(BF16) for grad in grads], axis=1)
    project_grad = product_left(normed, packed_grad)
    part = product_right(packed_grad, matrices[:, : 3 * H])
    return part, jnp.concatenate([project_grad, mixing_grad], axis=1).astype(BF16)


def conv_forward(dims, normed, matrices, taps, live):
    S, C = dims.S, dims.C
    pair = product(normed, matrices[:, : 2 * C])
    values, gate = pair[:, :C], jax.nn.sigmoid(pair[:, C:])
    glu_values = values * gate * live
    margin = (KERNEL - 1) // 2
    padded = jnp.pad(glu_values, ((margin, margin), (0, 0)))
    mixed_time = padded[0:S] * taps[0]
    for offset in range(1, KERNEL):
        mixed_time = mixed_time + padded[offset : offset + S] * taps[offset]
    hidden = jax.nn.silu(mixed_time).astype(BF16)
    part = product_right(hidden, matrices[:, 2 * C :])
    return part, (values, gate, padded, mixed_time, hidden)


def conv_back(dims, normed, matrices, taps, live, kept, upstream):
    S, C = dims.S, dims.C
    values, gate, padded, mixed_time, hidden = kept
    merging_grad = product_left(upstream, hidden)
    time_grad = product(upstream, matrices[:, 2 * C :]) * silu_slope(mixed_time)
    margin = (KERNEL - 1) // 2
    kernel_grad = jnp.stack(
        [jnp.sum(padded[offset : offset + S] * time_grad, axis=0) for offset in range(KERNEL)]
    )
    slope_padded = jnp.pad(time_grad, ((margin, margin), (0, 0)))
    glu_grad = slope_padded[2 * margin : 2 * margin + S] * taps[0]
    for offset in range(1, KERNEL):
        first = 2 * margin - offset
        glu_grad = glu_grad + slope_padded[first : first + S] * taps[offset]
    glu_grad = glu_grad * live
    pair_grad = jnp.concatenate(
        [glu_grad * gate, glu_grad * values * gate * (1.0 - gate)], axis=1
    ).astype(BF16)
    gating_grad = product_left(normed, pair_grad)
    part = product_right(pair_grad, matrices[:, : 2 * C])
    return part, jnp.concatenate([gating_grad, merging_grad], axis=1).astype(BF16), kernel_grad


def shards(
    dims,
    frames_input,
    out_grad,
    lengths,
    step_count,
    rates,
    expand_params,
    expand_first,
    expand_second,
    shrink_params,
    shrink_first,
    shrink_second,
    project_params,
    project_first,
    project_second,
    mixing_params,
    mixing_first,
    mixing_second,
    gating_params,
    gating_first,
    gating_second,
    kernel_params,
    kernel_first,
    kernel_second,
    merging_params,
    merging_first,
    merging_second,
    gains_params,
    gains_first,
    gains_second,
):
    local_rows, width = frames_input.shape
    shard_rows = expand_params.shape[2]
    dims = SimpleNamespace(
        L=local_rows,
        D=width,
        S=local_rows * dims.ny * 2,
        F=expand_params.shape[3],
        H=project_params.shape[3],
        C=gating_params.shape[3],
        **vars(dims),
    )
    tensor_rank = lax.axis_index("tensor")
    data_rank = lax.axis_index("dp")
    block_y = tensor_rank // 2
    live_keys = jnp.arange(dims.S, dtype=jnp.int32) < lengths[0]
    live = live_keys.astype(F32).reshape(-1, 1)
    live_local = lax.dynamic_slice_in_dim(live, tensor_rank * local_rows, local_rows, 0)
    taps = kernel_params[0]
    gain = [gains_params[0, i : i + 1] for i in range(5)]

    expand_shard = expand_params[0].astype(BF16)
    shrink_shard = jnp.swapaxes(shrink_params[0].astype(BF16), 1, 2)
    attention_shard = jnp.concatenate(
        [project_params[0, 0], project_params[0, 1], project_params[0, 2], mixing_params[0].T], axis=1
    ).astype(BF16)
    conv_shard = jnp.concatenate(
        [gating_params[0, 0], gating_params[0, 1], merging_params[0].T], axis=1
    ).astype(BF16)
    cotangent = (out_grad.astype(F32) * live_local).astype(BF16)

    head = head_kernel(
        dims, 0, frames_input, cotangent, gain[0], expand_shard[0], shrink_shard[0]
    )
    n1, h0, expand0, shrink0 = head["n"], head["xh"], head["bo0"], head["bo1"]
    one = ff_forward(
        dims, 1, n1, expand0, shrink0, h0, gain[1], Beside(dims, [attention_shard, conv_shard])
    )
    n2, h1 = one["nn"], one["hn"]
    attention_matrices, conv_matrices = one["bo0"], one["bo1"]
    part, kept_two = attention_forward(dims, n2, attention_matrices, live_keys)
    two = edge_forward(
        dims, 2, part, h1, gain[2], Beside(dims, [expand_shard[1]])
    )
    n3, h2, expand1 = two["nn"], two["hn"], two["bo0"]
    part, kept_three = conv_forward(dims, n3, conv_matrices, taps, live)
    three = edge_forward(dims, 3, part, h2, gain[3], Beside(dims, [shrink_shard[1]]))
    n4, h3, shrink1 = three["nn"], three["hn"], three["bo0"]
    four = ff_turn(
        dims, 4, n4, expand1, shrink1, h3, gain[4], head["ogh"], Beside(dims)
    )
    five = ff_back(
        dims, 5, four["w"], expand1, shrink1, four["slope"], four["u"], n4, four["ghn"], h3,
        gain[3], Beside(dims), False,
    )
    def blocks(array):
        return array.reshape(dims.na, dims.nb, shard_rows, array.shape[1])

    part, conv_grad, kernel_grad = conv_back(
        dims, n3, conv_matrices, taps, live, kept_three, five["wn"]
    )
    six = edge_back(
        dims, 6, part, five["ghn"], h2, gain[2], 1.0,
        Beside(dims, scatters=[blocks(conv_grad), blocks(five["dr"])]),
    )
    part, attention_grad = attention_back(
        dims, n2, attention_matrices, live_keys, kept_two, six["wn"]
    )
    seven = edge_back(
        dims, 7, part, six["ghn"], h1, gain[1], 0.5, Beside(dims, scatters=[blocks(five["de"])])
    )
    eight = ff_back(
        dims, 8, seven["wn"], expand0, shrink0, one["slope"], one["u"], n1, seven["ghn"], h0,
        gain[0], Beside(dims, scatters=[blocks(attention_grad)]), True,
    )
    frames_out = lax.dynamic_index_in_dim(four["fo"], block_y, 0, False)

    steps_done = step_count[0].astype(F32)
    scalars = jnp.concatenate(
        [rates, 1.0 / (1.0 - rates[:2] ** steps_done), jnp.zeros((2,), F32)]
    )
    entries = []
    triples = (
        (expand_params, expand_first, expand_second),
        (shrink_params, shrink_first, shrink_second),
        (project_params, project_first, project_second),
        (mixing_params, mixing_first, mixing_second),
        (gating_params, gating_first, gating_second),
        (kernel_params, kernel_first, kernel_second),
        (merging_params, merging_first, merging_second),
        (gains_params, gains_first, gains_second),
    )
    for place in PLACES:
        params, first, second = triples[place]
        if first.ndim == 2:
            at = 1 if place == 7 else 0
            params = jnp.expand_dims(params, at + 1)
            first, second = jnp.expand_dims(first, at), jnp.expand_dims(second, at)
        entries.append((params, first, second, 0.0 if place == 7 else DECAY_RATE))
    summed = gradient_kernel(
        dims, 9, scalars, entries, [blocks(eight["de"]), blocks(eight["dr"])],
        [seven["bo0"], six["bo1"], eight["bo0"], six["bo0"]],
        [kernel["dg"] for kernel in (eight, seven, six, five, four)], kernel_grad,
    )
    updated = update_kernel(
        dims, scalars, summed["norms"], entries, [summed["g" + str(i)] for i in range(8)]
    )
    results = []
    for place in range(8):
        tag = str(PLACES.index(place))
        like = triples[place][1].shape
        results += [updated[name + tag].reshape(like) for name in ("og", "om", "ov")]
        results += [updated[name + tag].reshape((2,) + like) for name in ("ow", "ob")]
    return (frames_out, eight["gin"], *results, updated["trust"])


def solution(mesh):
    slow = math.gcd(mesh.shape["dp"], 4)
    dims = SimpleNamespace(na=slow, nb=mesh.shape["dp"] // slow, ny=mesh.shape["tensor"] // 2)
    return jax.shard_map(
        functools.partial(shards, dims),
        mesh=mesh,
        in_specs=(
            P(("dp", "tensor"), None),
            P(("dp", "tensor"), None),
            P("dp"),
            P(),
            P(),
            P(None, None, "dp", "tensor"),
            P(None, "dp", "tensor"),
            P(None, "dp", "tensor"),
            P(None, None, "tensor", "dp"),
            P(None, "tensor", "dp"),
            P(None, "tensor", "dp"),
            P(None, None, "dp", "tensor"),
            P(None, "dp", "tensor"),
            P(None, "dp", "tensor"),
            P(None, "tensor", "dp"),
            P("tensor", "dp"),
            P("tensor", "dp"),
            P(None, None, "dp", "tensor"),
            P(None, "dp", "tensor"),
            P(None, "dp", "tensor"),
            P(None, None, "tensor"),
            P(None, "tensor"),
            P(None, "tensor"),
            P(None, "tensor", "dp"),
            P("tensor", "dp"),
            P("tensor", "dp"),
            P(),
            P(),
            P(),
        ),
        out_specs=(
            P(("dp", "tensor"), None),
            P(("dp", "tensor"), None),
            P(None, "dp", "tensor"),
            P(None, "dp", "tensor"),
            P(None, "dp", "tensor"),
            P(None, None, "dp", "tensor"),
            P(None, None, "dp", "tensor"),
            P(None, "tensor", "dp"),
            P(None, "tensor", "dp"),
            P(None, "tensor", "dp"),
            P(None, None, "tensor", "dp"),
            P(None, None, "tensor", "dp"),
            P(None, "dp", "tensor"),
            P(None, "dp", "tensor"),
            P(None, "dp", "tensor"),
            P(None, None, "dp", "tensor"),
            P(None, None, "dp", "tensor"),
            P("tensor", "dp"),
            P("tensor", "dp"),
            P("tensor", "dp"),
            P(None, "tensor", "dp"),
            P(None, "tensor", "dp"),
            P(None, "dp", "tensor"),
            P(None, "dp", "tensor"),
            P(None, "dp", "tensor"),
            P(None, None, "dp", "tensor"),
            P(None, None, "dp", "tensor"),
            P(None, "tensor"),
            P(None, "tensor"),
            P(None, "tensor"),
            P(None, None, "tensor"),
            P(None, None, "tensor"),
            P("tensor", "dp"),
            P("tensor", "dp"),
            P("tensor", "dp"),
            P(None, "tensor", "dp"),
            P(None, "tensor", "dp"),
            P(),
            P(),
            P(),
            P(),
            P(),
            P(),
        ),
        check_vma=False,
    )
```

```python
import functools
import math
from types import SimpleNamespace

import jax
import jax.numpy as jnp
from jax import lax
from jax.experimental import pallas as pl
from jax.experimental.pallas import tpu as pltpu
from jax.sharding import PartitionSpec as P

HEAD_DIM = 64
KERNEL = 31

EPSILON = 1e-05
ADAM_EPS = 1e-06
DECAY_RATE = 0.01
MASKED = -1000000000.0

F32 = jnp.float32
BF16 = jnp.bfloat16
MESH = pl.DeviceIdType.MESH
STEP = 16
TILE = 256
GRANT = 60 * 1024 * 1024


class Spot:
    def __init__(self, dims):
        self.dims = dims
        self.d = lax.axis_index("dp")
        self.t = lax.axis_index("tensor")
        self.y = lax.div(self.t, 2)
        self.c = lax.rem(self.t, 2)
        self.a = lax.div(self.d, dims.nb)
        self.b = lax.rem(self.d, dims.nb)

    def sibling(self):
        return (self.d, self.y * 2 + 1 - self.c)

    def across(self, j):
        return (self.d, lax.rem(self.y + j, self.dims.ny) * 2 + self.c)

    def slow(self, j):
        return (lax.rem(self.a + j, self.dims.na) * self.dims.nb + self.b, self.t)

    def fast(self, j):
        return (self.a * self.dims.nb + lax.rem(self.b + j, self.dims.nb), self.t)

    def tensor_peers(self):
        return [self.sibling()] + [self.across(j) for j in range(1, self.dims.ny)]

    def data_peers(self):
        return [self.slow(j) for j in range(1, self.dims.na)] + [
            self.fast(j) for j in range(1, self.dims.nb)
        ]


def greet(peers):
    barrier = pltpu.get_barrier_semaphore()
    for peer in peers:
        pl.semaphore_signal(barrier, 1, device_id=peer, device_id_type=MESH)
    pl.semaphore_wait(barrier, len(peers))


def remote(source, target, send, recv, peer):
    return pltpu.make_async_remote_copy(
        src_ref=source,
        dst_ref=target,
        send_sem=send,
        recv_sem=recv,
        device_id=peer,
        device_id_type=MESH,
    )


def loop(count, body, unroll=1):
    def step(i, carry):
        body(i)
        return carry

    lax.fori_loop(0, count, step, 0, unroll=unroll)


def rows_of(i, step=STEP):
    return pl.ds(pl.multiple_of(i * step, step), step)


class Refs(SimpleNamespace):
    def need(self, *names):
        for name in names:
            if name in self.pending:
                self.pending.pop(name).wait()

    def done(self, *names):
        for name in names:
            copy = self.unsent.pop(name)
            copy.start()
            self.leaving.append(copy)

    def close(self):
        self.need(*list(self.pending))
        self.done(*list(self.unsent))
        for copy in self.leaving:
            copy.wait()


def call(body, ins, outs, scratch, cid):
    in_names, out_names, scratch_names = list(ins), list(outs), list(scratch)
    loads = [name for name in in_names if ins[name][1] is LD]
    stores = [name for name in out_names if outs[name][2] is ST]
    copies = [VM(ins[name][0].shape, ins[name][0].dtype) for name in loads]
    copies += [VM(outs[name][0], outs[name][1]) for name in stores]
    sems = [SEMS((max(len(copies), 1),))]

    def place(space):
        return pl.BlockSpec(memory_space=HB if space in (LD, ST) else space)

    def kernel(*refs):
        names = in_names + out_names + scratch_names
        given = dict(zip(names, refs))
        held = refs[len(names) : -1]
        r = Refs(**given, pending={}, unsent={}, leaving=[])
        for i, name in enumerate(loads):
            r.pending[name] = pltpu.make_async_copy(given[name], held[i], refs[-1].at[i])
            setattr(r, name, held[i])
        for i, name in enumerate(stores, len(loads)):
            r.unsent[name] = pltpu.make_async_copy(held[i], given[name], refs[-1].at[i])
            setattr(r, name, held[i])
        for copy in r.pending.values():
            copy.start()
        body(r)
        r.close()

    results = pl.pallas_call(
        kernel,
        out_shape=[jax.ShapeDtypeStruct(shape, kind) for shape, kind, _ in outs.values()],
        in_specs=[place(space) for _, space in ins.values()],
        out_specs=[place(space) for _, _, space in outs.values()],
        scratch_shapes=list(scratch.values()) + copies + sems,
        compiler_params=pltpu.CompilerParams(
            collective_id=cid, has_side_effects=cid is not None, vmem_limit_bytes=GRANT
        ),
    )(*[array for array, _ in ins.values()])
    return dict(zip(out_names, results))


LD, ST = object(), object()
VM = pltpu.VMEM
HB = pl.ANY
SM = pltpu.SMEM
SEMS = pltpu.SemaphoreType.DMA


def tagged(prefix, tag, specs):
    return {prefix + name + tag: spec for name, spec in specs.items()}


def bound(refs, prefix, tag, specs):
    return SimpleNamespace(**{name: getattr(refs, prefix + name + tag) for name in specs})


class Gather:
    def __init__(self, tag, dims):
        self.tag, self.dims = tag, dims
        na, nb = dims.na, dims.nb
        m, k = max(nb - 1, 1), max(na - 1, 1)
        self.specs = dict(
            loc=SEMS,
            xs=SEMS((m,)),
            xr=SEMS((m,)),
            us=SEMS((k,)),
            ur=SEMS((k,)),
            ds=SEMS((k,)),
            dr=SEMS((k,)),
            fs=SEMS((2, k, m)),
            fr=SEMS((2, k, m)),
        )
        self.stage = 0

    def scratch(self):
        return tagged("g", self.tag, self.specs)

    def bind(self, refs, spot, source, whole):
        self.sem = bound(refs, "g", self.tag, self.specs)
        self.spot, self.source, self.whole = spot, source, whole
        return self

    def rows(self, d):
        shard = self.source.shape[0]
        return self.whole.at[pl.ds(pl.multiple_of(d * shard, shard), shard)]

    def block(self, a):
        return self.rows(a * self.dims.nb + self.spot.b)

    def hop(self, way, s):
        spot, sem = self.spot, self.sem
        step = 1 if way == 0 else -1
        target = self.block(spot.a - step * (s - 1))
        source = self.source if s == 1 else target
        send, recv = (sem.us, sem.ur) if way == 0 else (sem.ds, sem.dr)
        peer = ((spot.a + step) * self.dims.nb + spot.b, spot.t)
        return remote(source, target, send.at[s - 1], recv.at[s - 1], peer)

    def sends(self, way, s):
        spot, na = self.spot, self.dims.na
        if way == 0:
            return jnp.logical_and(spot.a - (s - 1) >= 0, spot.a + 1 < na)
        return jnp.logical_and(spot.a + (s - 1) < na, spot.a - 1 >= 0)

    def has(self, way, s):
        return self.spot.a - s >= 0 if way == 0 else self.spot.a + s < self.dims.na

    def hand(self, way, s, i):
        block = self.block(self.spot.a - s if way == 0 else self.spot.a + s)
        sem = self.sem
        return remote(
            block, block, sem.fs.at[way, s - 1, i - 1], sem.fr.at[way, s - 1, i - 1], self.spot.fast(i)
        )

    def start(self):
        spot, dims, sem = self.spot, self.dims, self.sem
        mine = self.rows(spot.d)
        if dims.na > 1:
            for way in range(2):

                @pl.when(self.sends(way, 1))
                def _(way=way):
                    self.hop(way, 1).start()

        self.own = [
            remote(self.source, mine, sem.xs.at[j - 1], sem.xr.at[j - 1], spot.fast(j))
            for j in range(1, dims.nb)
        ]
        for copy in self.own:
            copy.start()
        self.local = pltpu.make_async_copy(self.source, mine, sem.loc)
        self.local.start()

    def advance(self):
        dims = self.dims
        self.stage += 1
        s = self.stage
        if s >= dims.na:
            return False
        for way in range(2):

            @pl.when(self.has(way, s))
            def _(way=way):
                self.hop(way, s).wait_recv()
                for i in range(1, dims.nb):
                    self.hand(way, s, i).start()

            if s + 1 < dims.na:

                @pl.when(self.sends(way, s + 1))
                def _(way=way):
                    self.hop(way, s + 1).start()

        return True

    def finish(self):
        dims = self.dims
        while self.advance():
            pass
        self.local.wait()
        for copy in self.own:
            copy.wait()
        for s in range(1, dims.na):
            for way in range(2):

                @pl.when(self.sends(way, s))
                def _(way=way, s=s):
                    self.hop(way, s).wait_send()

                @pl.when(self.has(way, s))
                def _(way=way, s=s):
                    for i in range(1, dims.nb):
                        self.hand(way, s, i).wait()


class Scatter:
    def __init__(self, tag, dims, rows, first, columns):
        self.tag, self.dims, self.size = tag, dims, (rows, columns)
        self.columns = pl.ds(first, columns)
        na, nb = dims.na, dims.nb
        m, k = max(nb - 1, 1), max(na - 1, 1)
        self.specs = dict(
            held=VM((na, rows, columns), BF16),
            one=VM((m, na, rows, columns), BF16),
            two=VM((k, rows, columns), BF16),
            loc=SEMS,
            xs=SEMS((m,)),
            xr=SEMS((m,)),
            zs=SEMS((k,)),
            zr=SEMS((k,)),
        )
        self.stage = 0

    def scratch(self):
        return tagged("s", self.tag, self.specs)

    def bind(self, refs, spot, source, result):
        self.r = bound(refs, "s", self.tag, self.specs)
        self.spot, self.source, self.result = spot, source, result
        return self

    def start(self):
        spot, dims, r = self.spot, self.dims, self.r
        self.first = []
        for j in range(1, dims.nb):
            block = lax.rem(spot.b + j, dims.nb)
            copy = remote(
                self.source.at[:, block, :, self.columns],
                r.one.at[j - 1],
                r.xs.at[j - 1],
                r.xr.at[j - 1],
                spot.fast(j),
            )
            copy.start()
            self.first.append(copy)
        self.local = pltpu.make_async_copy(
            self.source.at[:, spot.b, :, self.columns], r.held, r.loc
        )
        self.local.start()

    def advance(self):
        if self.stage:
            return False
        self.stage = 1
        spot, dims, r = self.spot, self.dims, self.r
        rows, columns = self.size
        self.local.wait()
        for copy in self.first:
            copy.wait_recv()
        if dims.nb > 1:
            for a in range(dims.na):

                def add(i, a=a):
                    rs = rows_of(i)
                    total = r.held[a, rs, :].astype(F32)
                    for j in range(dims.nb - 1):
                        total = total + r.one[j, a, rs, :].astype(F32)
                    r.held[a, rs, :] = total.astype(BF16)

                loop(rows // STEP, add, 2)
        self.second = []
        for j in range(1, dims.na):
            copy = remote(
                r.held.at[lax.rem(spot.a + j, dims.na)],
                r.two.at[j - 1],
                r.zs.at[j - 1],
                r.zr.at[j - 1],
                spot.slow(j),
            )
            copy.start()
            self.second.append(copy)
        return True

    def finish(self):
        self.advance()
        dims, r = self.dims, self.r
        rows, columns = self.size
        for copy in self.second:
            copy.wait_recv()

        def add(i):
            rs = rows_of(i)
            total = r.held[self.spot.a, rs, :].astype(F32)
            for j in range(dims.na - 1):
                total = total + r.two[j, rs, :].astype(F32)
            self.result[rs, self.columns] = total

        loop(rows // STEP, add, 2)
        for copy in self.first + self.second:
            copy.wait_send()


class Edge:
    def __init__(self, dims, count):
        self.dims, self.count = dims, count

    def scratch(self):
        ny, L, D, count = self.dims.ny, self.dims.L, self.dims.D, self.count
        m = max(ny - 1, 1)
        return dict(
            e_own=VM((ny, L, D), F32),
            e_give=VM((ny, L, D), BF16),
            e_take=VM((ny, L, D), BF16),
            e_sum=VM((ny, L, D), BF16),
            e_far=VM((min(count, 2), m, ny, L, D), BF16),
            e_ds=SEMS((count, ny)),
            e_dr=SEMS((count, ny)),
            e_ys=SEMS((count, m, ny)),
            e_yr=SEMS((count, m, ny)),
            e_ns=SEMS((count, ny)),
            e_nr=SEMS((count, ny)),
        )

    def bind(self, refs, spot):
        self.refs, self.spot = refs, spot
        self.near, self.far, self.handed = {}, {}, {}
        return self

    def open(self, i, k):
        if i > 0:
            self.near.pop((i - 1, k)).wait_send()

    def put(self, k, columns, part):
        L, refs = self.dims.L, self.refs
        low, high = part[:L], part[L:]
        first = self.spot.c == 0
        refs.e_own[k, :, columns] = jnp.where(first, low, high)
        refs.e_give[k, :, columns] = jnp.where(first, high, low).astype(BF16)

    def start(self, i, k):
        refs = self.refs
        copy = remote(
            refs.e_give.at[k],
            refs.e_take.at[k],
            refs.e_ds.at[i, k],
            refs.e_dr.at[i, k],
            self.spot.sibling(),
        )
        copy.start()
        self.near[i, k] = copy

    def cross(self, i, k, send=True):
        refs, dims = self.refs, self.dims
        self.near[i, k].wait_recv()
        if i > 0:
            for copy in self.far.pop((i - 1, k)):
                copy.wait_send()

        def add(j):
            rs = rows_of(j)
            total = refs.e_own[k, rs, :] + refs.e_take[k, rs, :].astype(F32)
            refs.e_own[k, rs, :] = total
            refs.e_sum[k, rs, :] = total.astype(BF16)

        loop(dims.L // STEP, add, 2)
        if send:
            self.far[i, k] = []
            for j in range(1, dims.ny):
                copy = remote(
                    refs.e_sum.at[k],
                    refs.e_far.at[i % 2, j - 1, k],
                    refs.e_ys.at[i, j - 1, k],
                    refs.e_yr.at[i, j - 1, k],
                    self.spot.across(j),
                )
                copy.start()
                self.far[i, k].append(copy)

    def cross_owner(self, i):
        refs, dims = self.refs, self.dims
        self.far[i, 0] = []
        for j in range(1, dims.ny):
            copy = remote(
                refs.e_sum.at[lax.rem(self.spot.y + j, dims.ny)],
                refs.e_far.at[i % 2, j - 1, 0],
                refs.e_ys.at[i, j - 1, 0],
                refs.e_yr.at[i, j - 1, 0],
                self.spot.across(j),
            )
            copy.start()
            self.far[i, 0].append(copy)

    def total(self, i, k, rs, slot):
        refs = self.refs
        total = refs.e_own[k, rs, :]
        for j in range(self.dims.ny - 1):
            total = total + refs.e_far[i % 2, j, slot, rs, :].astype(F32)
        return total

    def settle(self, i, k, row_fn, target):
        refs, dims, spot = self.refs, self.dims, self.spot
        for copy in self.far[i, k]:
            copy.wait_recv()
        base = (k * 2 + spot.c) * dims.L

        def body(j):
            rs = rows_of(j)
            rows = row_fn(self.total(i, k, rs, k), k, rs)
            target[pl.ds(pl.multiple_of(base + j * STEP, STEP), STEP), :] = rows

        loop(dims.L // STEP, body, 2)
        block = target.at[pl.ds(pl.multiple_of(base, dims.L), dims.L)]
        copy = remote(block, block, refs.e_ns.at[i, k], refs.e_nr.at[i, k], spot.sibling())
        copy.start()
        self.handed[i, k] = copy

    def arrived(self, i, k):
        self.handed[i, k].wait_recv()

    def drain(self):
        for copy in list(self.near.values()) + list(self.handed.values()):
            copy.wait_send()
        for copies in self.far.values():
            for copy in copies:
                copy.wait_send()


def unit(hidden):
    center = hidden - jnp.mean(hidden, axis=-1, keepdims=True)
    spread = jnp.mean(center * center, axis=-1, keepdims=True)
    inverse = lax.rsqrt(spread + EPSILON)
    return center * inverse, inverse


def unit_back(upstream, xhat, inverse, gain):
    scaled = upstream * gain
    return inverse * (
        scaled
        - jnp.mean(scaled, axis=-1, keepdims=True)
        - xhat * jnp.mean(scaled * xhat, axis=-1, keepdims=True)
    )


def fold(rows):
    return rows[:8] + rows[8:]


def head_kernel(dims, cid, frames, cotangent, gain, expand_shard, shrink_shard):
    ny, L, D = dims.ny, dims.L, dims.D
    beside = Beside(dims, [expand_shard, shrink_shard])
    m = max(ny - 1, 1)
    scratch = dict(
        xs=SEMS((m,)), xr=SEMS((m,)), os=SEMS((m,)), orr=SEMS((m,)), ns=SEMS((ny,)), nr=SEMS((ny,))
    )

    def body(r):
        spot = Spot(dims)
        greet(spot.tensor_peers() + spot.data_peers())
        beside.start(r, spot)
        moves = []
        for j in range(1, ny):
            copy = remote(r.x, r.xh.at[spot.y], r.xs.at[j - 1], r.xr.at[j - 1], spot.across(j))
            copy.start()
            other = remote(r.og, r.ogh.at[spot.y], r.os.at[j - 1], r.orr.at[j - 1], spot.across(j))
            other.start()
            moves.append((copy, other))

        def own_rows(i):
            rs = rows_of(i)
            r.xh[spot.y, rs, :] = r.x[rs, :]
            r.ogh[spot.y, rs, :] = r.og[rs, :]

        loop(L // STEP, own_rows)
        handed = []

        def normalize(y, slot):
            base = (y * 2 + spot.c) * L

            def rows(i):
                xhat, _ = unit(r.xh[y, rows_of(i), :].astype(F32))
                target = pl.ds(pl.multiple_of(base + i * STEP, STEP), STEP)
                r.n[target, :] = (xhat * r.g[...]).astype(BF16)

            loop(L // STEP, rows, 2)
            block = r.n.at[pl.ds(pl.multiple_of(base, L), L)]
            copy = remote(block, block, r.ns.at[slot], r.nr.at[slot], spot.sibling())
            copy.start()
            handed.append(copy)

        normalize(spot.y, 0)
        beside.advance()
        for j in range(1, ny):
            moves[j - 1][0].wait_recv()
            normalize(lax.rem(spot.y + ny - j, ny), j)
        beside.advance()
        for copy in handed:
            copy.wait()
        for copy, other in moves:
            copy.wait_send()
            other.wait()
        beside.finish()

    return call(
        body,
        dict(
            x=(frames, VM),
            og=(cotangent, VM),
            g=(gain, VM),
        )
        | beside.ins(),
        dict(
            xh=((ny, L, D), BF16, VM),
            ogh=((ny, L, D), BF16, VM),
            n=((dims.S, D), BF16, VM),
        )
        | beside.outs(),
        scratch | beside.scratch(),
        cid,
    )


class Beside:
    def __init__(self, dims, gathers=(), scatters=(), pieces=2):
        self.dims = dims
        self.arrays = list(gathers) + list(scatters)
        self.gathers = len(gathers)
        self.jobs = [(i, Gather(str(i), dims)) for i in range(len(gathers))]
        for i, source in enumerate(scatters):
            rows, width = source.shape[2:]
            count = pieces if width % (pieces * 128) == 0 else 1
            for piece in range(count):
                tag = str(len(self.jobs))
                part = width // count
                self.jobs.append(
                    (self.gathers + i, Scatter(tag, dims, rows, piece * part, part))
                )

    def peers(self, spot):
        return spot.data_peers() if self.jobs else []

    def ins(self):
        return {"bi" + str(i): (source, HB) for i, source in enumerate(self.arrays)}

    def outs(self):
        named = {}
        for i, source in enumerate(self.arrays):
            if i < self.gathers:
                rows, columns = source.shape
                shape = ((rows * self.dims.na * self.dims.nb, columns), BF16, HB)
            else:
                shape = (source.shape[2:], F32, VM)
            named["bo" + str(i)] = shape
        return named

    def scratch(self):
        named = {}
        for _, job in self.jobs:
            named |= job.scratch()
        return named

    def start(self, refs, spot):
        for i, job in self.jobs:
            job.bind(refs, spot, getattr(refs, "bi" + str(i)), getattr(refs, "bo" + str(i))).start()

    def advance(self):
        for _, job in self.jobs:
            job.advance()

    def finish(self):
        for _, job in self.jobs:
            job.finish()


def chunk_rows(dims, k):
    return pl.ds(k * 2 * dims.L, 2 * dims.L)


def up_products(dims, k, normed, expand, inner, slope):
    rows = chunk_rows(dims, k)

    def column(j):
        cs = rows_of(j, TILE)
        before = jnp.dot(normed[rows, :], expand[:, cs], preferred_element_type=F32)
        gate = jax.nn.sigmoid(before)
        inner[rows, cs] = (before * gate).astype(BF16)
        slope[rows, cs] = (gate * (1.0 + before * (1.0 - gate))).astype(BF16)

    loop(dims.F // TILE, column, True)


def back_products(dims, k, upstream, shrink, slope, back):
    rows = chunk_rows(dims, k)

    def column(j):
        cs = rows_of(j, TILE)
        part = jnp.dot(upstream[rows, :], shrink[:, cs], preferred_element_type=F32)
        back[rows, cs] = (part * slope[rows, cs].astype(F32)).astype(BF16)

    loop(dims.F // TILE, column, True)


def part_product(edge, i, k, operand, matrix, first, dims):
    width = operand.shape[1]
    edge.open(i, k)

    def column(j):
        cs = rows_of(j, TILE)
        edge.put(
            k,
            cs,
            lax.dot_general(
                operand[chunk_rows(dims, k), :],
                matrix[cs, pl.ds(first, width)],
                (((1,), (1,)), ((), ())),
                preferred_element_type=F32,
            ),
        )

    loop(dims.D // TILE, column, True)
    edge.start(i, k)


def weight_part(result, first, rows_side, columns_side, dims):
    width = columns_side.shape[1]
    shard = result.shape[2]
    for i in range(dims.D // TILE):
        part = lax.dot_general(
            rows_side[:, pl.ds(i * TILE, TILE)],
            columns_side[...],
            (((0,), (0,)), ((), ())),
            preferred_element_type=F32,
        ).astype(BF16)
        for j in range(TILE // shard):
            d = i * (TILE // shard) + j
            result[d // dims.nb, d % dims.nb, :, pl.ds(first, width)] = part[
                j * shard : (j + 1) * shard
            ]


def forward_rows(hidden, scale, gain, kept):
    def rows(total, k, rs):
        after = hidden[k, rs, :].astype(F32) + scale * total
        kept[k, rs, :] = after
        xhat, _ = unit(after)
        return (xhat * gain[...]).astype(BF16)

    return rows


def backward_rows(hidden, scale, gain, grad, sums, spot):
    def rows(total, k, rs):
        xhat, inverse = unit(hidden[k, rs, :].astype(F32))
        own = jnp.where(spot.y == k, 1.0, 0.0)
        sums[...] += fold(total * xhat) * own
        after = grad[k, rs, :] + unit_back(total, xhat, inverse, gain[...])
        grad[k, rs, :] = after
        return (scale * after).astype(BF16)

    return rows


QUERIES = 256
BAND = 64
MARGIN = 16


def slide(padded, base, taps):
    window = padded[pl.ds(pl.multiple_of(base, BAND), BAND + 2 * MARGIN), :]
    total = None
    for residue in range(8):
        shifted = window[residue : residue + BAND + 24]
        for eighth in range(4):
            tap = 8 * eighth + residue - 1
            if 0 <= tap < KERNEL:
                term = shifted[8 * eighth : 8 * eighth + BAND] * taps[tap : tap + 1, :]
                total = term if total is None else total + term
    return total


def clear_margins(padded, S):
    edge = jnp.zeros((MARGIN, padded.shape[1]), F32)
    padded[pl.ds(0, MARGIN), :] = edge
    padded[pl.ds(MARGIN + S, MARGIN), :] = edge


def attend(dims, k, r):
    H, m = dims.H, 2 * dims.L
    heads = H // HEAD_DIM
    blocks = m // min(QUERIES, m)
    size = m // blocks

    def one(i):
        head = lax.div(i, blocks)
        at = pl.ds(pl.multiple_of(k * m + lax.rem(i, blocks) * size, size), size)
        scores = lax.dot_general(
            r.k[head], r.q[head, at, :], (((1,), (1,)), ((), ())), preferred_element_type=F32
        )
        scores = scores + r.bias[...]
        peak = jnp.max(scores, axis=0, keepdims=True)
        exponent = jnp.exp(scores - peak)
        total = jnp.sum(exponent, axis=0, keepdims=True)
        output = jnp.dot(r.vt[head], exponent.astype(BF16), preferred_element_type=F32)
        r.lse[head, :, at] = peak + jnp.log(total)
        r.ot[pl.ds(pl.multiple_of(head * HEAD_DIM, HEAD_DIM), HEAD_DIM), at] = output / total

    loop(heads * blocks, one)
    rows = chunk_rows(dims, k)
    r.oh[rows, :] = r.ot[:, rows].T.astype(BF16)


def front_kernel(
    dims, cid, normed, expand, shrink, hidden, gain_one, gain_two, bias, attention_shard, conv_shard,
    expand_shard,
):
    ny, L, D, S, F, H = dims.ny, dims.L, dims.D, dims.S, dims.F, dims.H
    heads = H // HEAD_DIM
    edge = Edge(dims, 2)
    gathers = [Gather(str(i), dims) for i in range(3)]
    scratch = edge.scratch() | dict(vt=VM((heads, HEAD_DIM, S), BF16), ot=VM((H, S), F32))
    for gather in gathers:
        scratch |= gather.scratch()

    def body(r):
        spot = Spot(dims)
        greet(spot.tensor_peers() + spot.data_peers())
        edge.bind(r, spot)
        gathers[0].bind(r, spot, r.sa, r.wa).start()
        gathers[1].bind(r, spot, r.sc, r.wc)
        gathers[2].bind(r, spot, r.se, r.e1)
        for k in range(ny):
            if k == 0:
                r.need("n", "e")
            up_products(dims, k, r.n, r.e, r.u, r.slope)
            r.need("rt")
            part_product(edge, 0, k, r.u, r.rt, 0, dims)
            edge.cross(0, k)
            gathers[0].advance()
        r.done("u", "slope")
        gathers[0].advance()
        gathers[1].start()
        r.need("h")
        for k in range(ny):
            edge.settle(0, k, forward_rows(r.h, 0.5, r.g1, r.h1), r.n2)
            if k == 0:
                gathers[0].finish()
                gathers[1].advance()
                gathers[2].start()
            edge.arrived(0, k)
            rows = chunk_rows(dims, k)
            for i, target in enumerate((r.q, r.k, r.v)):
                packed = jnp.dot(
                    r.n2[rows, :], r.wa[:, pl.ds(i * H, H)], preferred_element_type=F32
                ).astype(BF16).astype(F32)
                if i == 0:
                    packed = packed * HEAD_DIM**-0.5
                for j in range(heads):
                    part = packed[:, j * HEAD_DIM : (j + 1) * HEAD_DIM]
                    target[j, rows, :] = part.astype(BF16)
                    if i == 2:
                        r.vt[j, :, rows] = part.T.astype(BF16)
        r.done("n2", "h1", "q", "k", "v", "wa")
        r.need("bias")
        for k in range(ny):
            attend(dims, k, r)
            part_product(edge, 1, k, r.oh, r.wa, 3 * H, dims)
            edge.cross(1, k)
            gathers[1].advance()
            gathers[2].advance()
        r.done("oh", "lse")
        gathers[1].advance()
        gathers[2].advance()
        for k in range(ny):
            edge.settle(1, k, forward_rows(r.h1, 1.0, r.g2, r.h2), r.n3)
        r.done("h2")
        for k in range(ny):
            edge.arrived(1, k)
        r.done("n3")
        edge.drain()
        gathers[1].finish()
        gathers[2].finish()

    triple = (heads, S, HEAD_DIM)
    rows_all, held = (S, D), (ny, L, D)
    return call(
        body,
        dict(
            n=(normed, LD),
            e=(expand, LD),
            rt=(shrink, LD),
            h=(hidden, LD),
            bias=(bias, LD),
            g1=(gain_one, VM),
            g2=(gain_two, VM),
            sa=(attention_shard, HB),
            sc=(conv_shard, HB),
            se=(expand_shard, HB),
        ),
        dict(
            u=((S, F), BF16, ST),
            slope=((S, F), BF16, ST),
            h1=(held, F32, ST),
            n2=(rows_all, BF16, ST),
            q=(triple, BF16, ST),
            k=(triple, BF16, ST),
            v=(triple, BF16, ST),
            oh=((S, H), BF16, ST),
            lse=((heads, 1, S), F32, ST),
            h2=(held, F32, ST),
            n3=(rows_all, BF16, ST),
            wa=((D, 4 * H), BF16, ST),
            wc=((D, conv_shard.shape[1]), BF16, HB),
            e1=((D, F), BF16, HB),
        ),
        scratch,
        cid,
    )


def middle_kernel(dims, cid, kept, taps, live, cotangent, gains, shrink_shard, shard):
    ny, L, D, S, F, C = dims.ny, dims.L, dims.D, dims.S, dims.F, dims.C
    m = 2 * L
    edge = Edge(dims, 4)
    gather = Gather("0", dims)
    pieces = 2 if F % 256 == 0 else 1
    scatters = [
        Scatter(str(2 * i + j), dims, shard, j * (F // pieces), F // pieces)
        for i in range(2)
        for j in range(pieces)
    ]
    four = (dims.na, dims.nb, shard)
    scratch = edge.scratch() | gather.scratch()
    scratch |= dict(
        rt=VM((D, F), BF16),
        n4=VM((S, D), BF16),
        h3=VM((ny, L, D), F32),
        u=VM((S, F), BF16),
        slope=VM((S, F), BF16),
        w4=VM((S, D), BF16),
        db=VM((S, F), BF16),
        de=VM(four + (F,), BF16),
        dr=VM(four + (F,), BF16),
        w3=VM((S, D), BF16),
        z=VM((S, C), BF16),
        zslope=VM((S, C), F32),
        ga=VM((S, C), F32),
        gb=VM((S, C), F32),
        glu=VM((S + 2 * MARGIN, C), F32),
        back=VM((S + 2 * MARGIN, C), F32),
        pair=VM((S, 2 * C), BF16),
        sums=VM((KERNEL, 8, C), F32),
    )
    for scatter in scatters:
        scratch |= scatter.scratch()

    def body(r):
        spot = Spot(dims)
        greet(spot.tensor_peers() + spot.data_peers())
        edge.bind(r, spot)
        gather.bind(r, spot, r.sr, r.rt).start()
        for i, scatter in enumerate(scatters):
            early = i < pieces
            scatter.bind(r, spot, r.dr if early else r.de, r.outr if early else r.oute)
        for sums in (r.dg2, r.dg3, r.dg4):
            sums[...] = jnp.zeros_like(sums)

        clear_margins(r.glu, S)
        clear_margins(r.back, S)
        r.need("n", "wc", "live")

        def gated(i):
            rows = rows_of(i, 256)
            values = jnp.dot(r.n[rows, :], r.wc[:, pl.ds(0, C)], preferred_element_type=F32)
            gate = jax.nn.sigmoid(
                jnp.dot(r.n[rows, :], r.wc[:, pl.ds(C, C)], preferred_element_type=F32)
            )
            open_gate = gate * r.live[rows, :]
            product = values * open_gate
            r.ga[rows, :] = open_gate
            r.gb[rows, :] = product * (1.0 - gate)
            r.glu[pl.ds(pl.multiple_of(i * 256 + MARGIN, MARGIN), 256), :] = product

        loop(S // 256, gated)
        for k in range(ny):

            def band(i, k=k):
                base = k * m + i * BAND
                mixed = slide(r.glu, base, r.taps)
                gate = jax.nn.sigmoid(mixed)
                rows = pl.ds(pl.multiple_of(base, BAND), BAND)
                r.z[rows, :] = (mixed * gate).astype(BF16)
                r.zslope[rows, :] = gate * (1.0 + mixed * (1.0 - gate))

            loop(m // BAND, band)
            part_product(edge, 0, k, r.z, r.wc, 2 * C, dims)
            edge.cross(0, k)
            gather.advance()
        gather.advance()

        r.need("h", "e")
        for k in range(ny):
            edge.settle(0, k, forward_rows(r.h, 1.0, r.g3, r.h3), r.n4)
            if k == 0:
                gather.finish()
            edge.arrived(0, k)
            up_products(dims, k, r.n4, r.e, r.u, r.slope)
            part_product(edge, 1, k, r.u, r.rt, 0, dims)
            edge.cross(1, k)

        def turn(total, k, rs):
            xhat, inverse = unit(r.h3[k, rs, :] + 0.5 * total)
            r.fo[k, rs, :] = (xhat * r.g4[...]).astype(BF16)
            upstream = r.og[k, rs, :].astype(F32)
            own = jnp.where(spot.y == k, 1.0, 0.0)
            r.dg4[...] += fold(upstream * xhat) * own
            grad = unit_back(upstream, xhat, inverse, r.g4[...])
            r.gh[k, rs, :] = grad
            return (0.5 * grad).astype(BF16)

        r.need("og")
        for k in range(ny):
            edge.settle(1, k, turn, r.w4)
            edge.arrived(1, k)
            back_products(dims, k, r.w4, r.rt, r.slope, r.db)
            part_product(edge, 2, k, r.db, r.e, 0, dims)
            edge.cross(2, k)
        r.done("fo")
        weight_part(r.dr, 0, r.w4, r.u, dims)
        for scatter in scatters[:pieces]:
            scatter.start()
        weight_part(r.de, 0, r.n4, r.db, dims)
        for scatter in scatters[pieces:]:
            scatter.start()

        finished = 0
        for k in range(ny):
            edge.settle(2, k, backward_rows(r.h3, 1.0, r.g3, r.gh, r.dg3, spot), r.w3)
            edge.arrived(2, k)
            rows = chunk_rows(dims, k)
            inner = jnp.dot(r.w3[rows, :], r.wc[:, pl.ds(2 * C, C)], preferred_element_type=F32)
            r.back[pl.ds(k * m + MARGIN, m), :] = inner * r.zslope[rows, :]
            until = (k + 1) * m // BAND - (1 if k < ny - 1 else 0)

            def band(i, finished=finished):
                base = (i + finished) * BAND
                rows = pl.ds(pl.multiple_of(base, BAND), BAND)
                mixed = slide(r.back, base, r.flipped)
                r.pair[rows, pl.ds(0, C)] = (mixed * r.ga[rows, :]).astype(BF16)
                r.pair[rows, pl.ds(C, C)] = (mixed * r.gb[rows, :]).astype(BF16)

            loop(until - finished, band)
            finished = until
            if k > 0:
                part_product(edge, 3, k - 1, r.pair, r.wc, 0, dims)
                edge.cross(3, k - 1)
        part_product(edge, 3, ny - 1, r.pair, r.wc, 0, dims)
        edge.cross(3, ny - 1)
        for scatter in scatters[:pieces]:
            scatter.advance()
        weight_part(r.dw, 0, r.n, r.pair, dims)
        weight_part(r.dw, 2 * C, r.w3, r.z, dims)
        r.done("dw")
        r.sums[...] = jnp.zeros_like(r.sums)

        def tap_sums(i):
            base = i * BAND
            window = r.glu[pl.ds(pl.multiple_of(base, BAND), BAND + 2 * MARGIN), :]
            slope = r.back[pl.ds(pl.multiple_of(base + MARGIN, MARGIN), BAND), :]
            for residue in range(8):
                shifted = window[residue : residue + BAND + 24]
                for eighth in range(4):
                    tap = 8 * eighth + residue - 1
                    if 0 <= tap < KERNEL:
                        term = shifted[8 * eighth : 8 * eighth + BAND] * slope
                        r.sums[tap] += term.reshape(BAND // 8, 8, C).sum(axis=0)

        loop(S // BAND, tap_sums)
        for tap in range(KERNEL):
            r.dk[tap : tap + 1, :] = jnp.sum(r.sums[tap], axis=0, keepdims=True)
        for k in range(ny):
            edge.settle(3, k, backward_rows(r.h, 1.0, r.g2, r.gh, r.dg2, spot), r.w2)
            if k == 0:
                for scatter in scatters[pieces:]:
                    scatter.advance()
        r.done("gh")
        for k in range(ny):
            edge.arrived(3, k)
        r.done("w2")
        edge.drain()
        for scatter in scatters:
            scatter.finish()

    return call(
        body,
        dict(
            n=(kept["n3"], LD),
            wc=(kept["wc"], LD),
            live=(live, LD),
            e=(kept["e1"], LD),
            h=(kept["h2"], LD),
            og=(cotangent, LD),
            taps=(taps, VM),
            flipped=(taps[::-1], VM),
            g2=(gains[0], VM),
            g3=(gains[1], VM),
            g4=(gains[2], VM),
            sr=(shrink_shard, HB),
        ),
        dict(
            fo=((ny, L, D), BF16, ST),
            gh=((ny, L, D), F32, ST),
            w2=((S, D), BF16, ST),
            dw=(four + (3 * C,), BF16, ST),
            outr=((shard, F), F32, VM),
            oute=((shard, F), F32, VM),
            dk=((KERNEL, C), F32, VM),
            dg2=((8, D), F32, VM),
            dg3=((8, D), F32, VM),
            dg4=((8, D), F32, VM),
        ),
        scratch,
        cid,
    )


def last_kernel(dims, cid, kept, middle, normed, expand, shrink, hidden, bias, gains, shard):
    ny, L, D, S, F, H, C = dims.ny, dims.L, dims.D, dims.S, dims.F, dims.H, dims.C
    heads = H // HEAD_DIM
    edge = Edge(dims, 2)
    four = (dims.na, dims.nb, shard)
    scatters = [Scatter("0", dims, shard, 0, 3 * C)]
    half = 2 * H if H % 128 == 0 else 4 * H
    scatters += [
        Scatter(str(1 + j), dims, shard, j * half, half) for j in range(4 * H // half)
    ]
    triple = (heads, S, HEAD_DIM)
    scratch = edge.scratch() | dict(
        da=VM(triple, BF16),
        kt=VM((heads, HEAD_DIM, S), BF16),
        delta=VM((heads, 1, S), F32),
        gk=VM(triple, F32),
        gv=VM(triple, F32),
        dqt=VM((H, S), F32),
        pack=VM((S, 3 * H), BF16),
        dw=VM(four + (4 * H,), BF16),
        db=VM((S, F), BF16),
        w1=VM((S, D), BF16),
    )
    for scatter in scatters:
        scratch |= scatter.scratch()

    def body(r):
        spot = Spot(dims)
        greet(spot.tensor_peers() + spot.data_peers())
        edge.bind(r, spot)
        scatters[0].bind(r, spot, r.cw, r.sc).start()
        for scatter in scatters[1:]:
            scatter.bind(r, spot, r.dw, r.sa)
        for sums in (r.dg0, r.dg1, r.gk, r.gv):
            sums[...] = jnp.zeros_like(sums)

        r.need("w", "wa", "oh", "k")
        mixed = jnp.dot(r.w[...], r.wa[:, pl.ds(3 * H, H)], preferred_element_type=F32).astype(BF16)
        inner = (mixed.astype(F32) * r.oh[...].astype(F32)).T
        for j in range(heads):
            some = slice(j * HEAD_DIM, (j + 1) * HEAD_DIM)
            r.da[j] = mixed[:, some]
            r.delta[j] = jnp.sum(inner[some], axis=0, keepdims=True)
            r.kt[j] = r.k[j].astype(F32).T.astype(BF16)
        blocks = S // min(QUERIES, S)
        size = S // blocks
        r.need("q", "v", "bias", "lse")

        def one(i):
            head = lax.div(i, blocks)
            at = pl.ds(pl.multiple_of(lax.rem(i, blocks) * size, size), size)
            query, outer = r.q[head, at, :], r.da[head, at, :]
            scores = lax.dot_general(
                r.k[head], query, (((1,), (1,)), ((), ())), preferred_element_type=F32
            )
            prob = jnp.exp(scores + (r.bias[...] - r.lse[head, :, at]))
            r.gv[head] += jnp.dot(prob.astype(BF16), outer, preferred_element_type=F32)
            back = lax.dot_general(
                r.v[head], outer, (((1,), (1,)), ((), ())), preferred_element_type=F32
            )
            slope = (prob * (back - r.delta[head, :, at])).astype(BF16)
            r.gk[head] += jnp.dot(slope, query, preferred_element_type=F32)
            r.dqt[pl.ds(pl.multiple_of(head * HEAD_DIM, HEAD_DIM), HEAD_DIM), at] = (
                jnp.dot(r.kt[head], slope, preferred_element_type=F32) * HEAD_DIM**-0.5
            )

        loop(heads * blocks, one)
        r.pack[:, pl.ds(0, H)] = r.dqt[...].T.astype(BF16)
        for j, source in ((1, r.gk), (2, r.gv)):
            r.pack[:, pl.ds(j * H, H)] = jnp.concatenate(
                [source[i] for i in range(heads)], axis=1
            ).astype(BF16)
        for k in range(ny):
            part_product(edge, 0, k, r.pack, r.wa, 0, dims)
            edge.cross(0, k)
        scatters[0].advance()
        r.need("n2")
        weight_part(r.dw, 0, r.n2, r.pack, dims)
        weight_part(r.dw, 3 * H, r.w, r.oh, dims)
        for scatter in scatters[1:]:
            scatter.start()

        r.need("gh", "h1", "rt", "slope", "e")
        for k in range(ny):
            edge.settle(0, k, backward_rows(r.h1, 0.5, r.g1, r.gh, r.dg1, spot), r.w1)
            edge.arrived(0, k)
            back_products(dims, k, r.w1, r.rt, r.slope, r.db)
            part_product(edge, 1, k, r.db, r.e, 0, dims)
            edge.cross(1, k, send=False)
        edge.cross_owner(1)
        for scatter in scatters[1:]:
            scatter.advance()
        r.need("n1", "u", "h0")
        weight_part(r.de, 0, r.n1, r.db, dims)
        r.done("de")
        weight_part(r.dr, 0, r.w1, r.u, dims)
        r.done("dr")
        for copy in edge.far[1, 0]:
            copy.wait_recv()

        def rows(i):
            rs = rows_of(i)
            total = edge.total(1, spot.y, rs, 0)
            xhat, inverse = unit(r.h0[spot.y, rs, :].astype(F32))
            r.dg0[...] += fold(total * xhat)
            back = r.gh[spot.y, rs, :] + unit_back(total, xhat, inverse, r.g0[...])
            r.gin[rs, :] = back.astype(BF16)

        loop(L // STEP, rows, 2)
        edge.drain()
        for scatter in scatters:
            scatter.finish()

    return call(
        body,
        dict(
            w=(middle["w2"], LD),
            wa=(kept["wa"], LD),
            oh=(kept["oh"], LD),
            k=(kept["k"], LD),
            q=(kept["q"], LD),
            v=(kept["v"], LD),
            bias=(bias, LD),
            lse=(kept["lse"], LD),
            n2=(kept["n2"], LD),
            gh=(middle["gh"], LD),
            h1=(kept["h1"], LD),
            rt=(shrink, LD),
            slope=(kept["slope"], LD),
            e=(expand, LD),
            n1=(normed, LD),
            u=(kept["u"], LD),
            h0=(hidden, LD),
            g0=(gains[0], VM),
            g1=(gains[1], VM),
            cw=(middle["dw"], HB),
        ),
        dict(
            gin=((L, D), BF16, VM),
            de=(four + (F,), BF16, ST),
            dr=(four + (F,), BF16, ST),
            sc=((shard, 3 * C), F32, VM),
            sa=((shard, 4 * H), F32, VM),
            dg0=((8, D), F32, VM),
            dg1=((8, D), F32, VM),
        ),
        scratch,
        cid,
    )


def direction_of(mean, square, master, rates, decay):
    return mean * rates[4] / (jnp.sqrt(square * rates[5]) + ADAM_EPS) + decay * master


def moments_of(grad, mean, square, rates):
    return (
        rates[0] * mean + (1.0 - rates[0]) * grad,
        rates[1] * square + (1.0 - rates[1]) * grad * grad,
    )


def tile_rows(shape):
    rows, columns = shape[-2:]
    step = min(rows, max(8, 16384 // max(columns, 128)))
    return step if rows % step == 0 and step % 8 == 0 else rows


def eighths(tile):
    rows, columns = tile.shape
    return tile.reshape(rows // 8, 8, columns).sum(axis=0) if rows % 8 == 0 else tile


def flip(result, source, dims):
    def part(j):
        cs = rows_of(j, 128)
        result[cs, :] = source[:, cs].T

    loop(source.shape[1] // 128, part)


PLACES = (0, 1, 2, 3, 4, 6, 5, 7)


def piece_rows(shapes):
    rows, total = {}, 0
    for i in PLACES:
        rows[i] = total
        total += shapes[i][0]
    return rows


class Relay:
    def __init__(self, tag, count, shape):
        self.tag, self.count = tag, count
        k = max(count - 1, 1)
        self.specs = dict(slots=VM((count,) + shape, F32), s=SEMS((k,)), r=SEMS((k,)))

    def scratch(self):
        return tagged("r", self.tag, self.specs)

    def start(self, refs, place, peers, value):
        self.r = bound(refs, "r", self.tag, self.specs)
        r = self.r
        r.slots[place] = value
        self.copies = []
        for j, peer in enumerate(peers):
            copy = remote(r.slots.at[place], r.slots.at[place], r.s.at[j], r.r.at[j], peer)
            copy.start()
            self.copies.append(copy)

    def finish(self):
        for copy in self.copies:
            copy.wait()
        total = self.r.slots[0]
        for i in range(1, self.count):
            total = total + self.r.slots[i]
        return total


def gradient_kernel(dims, cid, rates, entries, scatter, sums, gain_parts, kernel_part):
    D, F, H, C = dims.D, dims.F, dims.H, dims.C
    beside = Beside(dims, scatters=scatter)
    shard = scatter[0].shape[2]
    count_t, count_d = dims.ny * 2, dims.na * dims.nb
    gains_relays = [
        Relay("0", 2, (8, D)), Relay("1", dims.ny, (8, D)),
        Relay("2", dims.na, (8, D)), Relay("3", dims.nb, (8, D)),
    ]
    taps_relays = [Relay("4", dims.na, (KERNEL, C)), Relay("5", dims.nb, (KERNEL, C))]
    norm_relays = [Relay("6", count_t, (24, 128)), Relay("7", count_d, (24, 128))]
    relays = gains_relays + taps_relays + norm_relays
    count = len(entries)
    shapes = [entry[0].shape[1:] for entry in entries]
    scratch = dict(
        nrm=VM((24, 128), F32),
        gains=VM((8, D), F32),
        shr0=VM((shard, F), F32),
        shr1=VM((shard, F), F32),
        mix=VM((shard, H), F32),
        mer=VM((shard, C), F32),
        gsem=SEMS((8 + dims.ny,)),
        isem=SEMS((count, 3)),
    )
    ins = dict(rates=(rates, SM), kp=(kernel_part, VM))
    outs = dict(norms=((24, 128), F32, VM))
    for i, (params, mean, square, _) in enumerate(entries):
        tag = str(i)
        ins |= {"p" + tag: (params, HB), "m" + tag: (mean, HB), "v" + tag: (square, HB)}
        scratch |= {"w" + tag: VM(shapes[i], F32), "n" + tag: VM(shapes[i], F32)}
        scratch |= {"q" + tag: VM(shapes[i], F32)}
        outs |= {"g" + tag: (shapes[i], F32, VM)}
    for i, part in enumerate(gain_parts):
        ins |= {"d" + str(i): (part, VM)}
    for i, array in enumerate(sums):
        ins |= {"s" + str(i): (array, HB)}
    for relay in relays:
        scratch |= relay.scratch()

    def body(r):
        spot = Spot(dims)
        everyone = [(spot.d, lax.rem(spot.t + j, count_t)) for j in range(1, count_t)]
        items = [(lax.rem(spot.d + j, count_d), spot.t) for j in range(1, count_d)]
        greet(everyone + items)
        get = lambda name, i: getattr(r, name + str(i))
        for k, (i, job) in enumerate(beside.jobs):
            target = r.shr0 if i else r.g0.at[0]
            job.bind(r, spot, get("bi", i), target).start()
        loads = []
        for i in range(count):
            triple = [
                pltpu.make_async_copy(get("p", i).at[0], get("w", i), r.isem.at[i, 0]),
                pltpu.make_async_copy(get("m", i), get("n", i), r.isem.at[i, 1]),
                pltpu.make_async_copy(get("v", i), get("q", i), r.isem.at[i, 2]),
            ]
            for copy in triple:
                copy.start()
            loads.append(triple)
        grads = [
            pltpu.make_async_copy(r.s0, r.g0.at[1], r.gsem.at[0]),
            pltpu.make_async_copy(r.s1, r.shr1, r.gsem.at[1]),
            pltpu.make_async_copy(r.s2.at[:, pl.ds(3 * H, H)], r.mix, r.gsem.at[2]),
            pltpu.make_async_copy(r.s3.at[:, pl.ds(2 * C, C)], r.mer, r.gsem.at[3]),
        ]
        grads += [
            pltpu.make_async_copy(r.s2.at[:, pl.ds(k * H, H)], r.g2.at[k], r.gsem.at[4 + k])
            for k in range(3)
        ]
        sides = [
            pltpu.make_async_copy(r.s3.at[:, pl.ds(k * C, C)], r.g4.at[k], r.gsem.at[7 + k])
            for k in range(2)
        ]
        for copy in grads + sides:
            copy.start()

        r.nrm[...] = jnp.zeros_like(r.nrm)
        row = lax.broadcasted_iota(jnp.int32, (24, 128), 0)
        lane = lax.broadcasted_iota(jnp.int32, (24, 128), 1)
        first_piece = piece_rows(shapes)
        loaded = set()

        def norm(i, p, weight=None):
            if i not in loaded:
                loaded.add(i)
                for copy in loads[i]:
                    copy.wait()
            step = tile_rows(shapes[i])
            columns = shapes[i][-1]
            acc_rows = 8 if step % 8 == 0 else step
            zero = jnp.zeros((acc_rows, columns), F32)

            def tile(j, carry):
                rs = pl.ds(pl.multiple_of(j * step, step), step)
                master = get("w", i)[p, rs, :]
                mean, square = moments_of(
                    get("g", i)[p, rs, :], get("n", i)[p, rs, :], get("q", i)[p, rs, :], r.rates
                )
                step_of = direction_of(mean, square, master, r.rates, entries[i][3])
                return (
                    carry[0] + eighths(master * master),
                    carry[1] + eighths(step_of * step_of),
                )

            totals = lax.fori_loop(0, shapes[i][-2] // step, tile, (zero, zero))
            here = row == first_piece[i] + p
            for column, total in enumerate(totals):
                value = jnp.sum(jnp.sum(total, axis=0, keepdims=True), axis=1, keepdims=True)
                if weight is not None:
                    value = value * weight
                r.nrm[...] += jnp.where(jnp.logical_and(here, lane == column), value, 0.0)

        r.gains[...] = jnp.zeros_like(r.gains)
        for k in range(5):
            r.gains[k : k + 1, :] = jnp.sum(get("d", k)[...], axis=0, keepdims=True)
        gains_relays[0].start(r, spot.c, [spot.sibling()], r.gains[...])
        slow = [spot.slow(j) for j in range(1, dims.na)]
        fast = [spot.fast(j) for j in range(1, dims.nb)]
        taps_relays[0].start(r, spot.a, slow, r.kp[...])
        total = gains_relays[0].finish()
        gains_relays[1].start(r, spot.y, [spot.across(j) for j in range(1, dims.ny)], total)
        for copy in grads + sides:
            copy.wait()
        flip(r.g3.at[0], r.mix, dims)
        flip(r.g5.at[0], r.mer, dims)
        total = gains_relays[1].finish()
        gains_relays[2].start(r, spot.a, slow, total)
        for i in (2, 3, 4, 5):
            for p in range(shapes[i][0]):
                norm(i, p)
        jobs = [job for _, job in beside.jobs]
        half = len(jobs) // 2
        jobs[0].advance()
        norm(0, 1)
        for job in jobs[1:half]:
            job.advance()
        flip(r.g1.at[1], r.shr1, dims)
        norm(1, 1)
        total = taps_relays[0].finish()
        taps_relays[1].start(r, spot.b, fast, total)
        total = gains_relays[2].finish()
        gains_relays[3].start(r, spot.b, fast, total)
        for job in jobs[half:]:
            job.advance()
        r.g6[0] = taps_relays[1].finish()
        owner = jnp.where(spot.d == 0, 1.0, 0.0)
        norm(6, 0, owner)
        r.gains[...] = gains_relays[3].finish()
        owner = jnp.where(spot.t == 0, owner, 0.0)
        for k in range(5):
            r.g7[k] = r.gains[k : k + 1, :]
            norm(7, k, owner)
        for job in jobs[:half]:
            job.finish()
        norm(0, 0)
        for job in jobs[half:]:
            job.finish()
        flip(r.g1.at[0], r.shr0, dims)
        norm(1, 0)
        norm_relays[0].start(r, spot.t, everyone, r.nrm[...])
        total = norm_relays[0].finish()
        norm_relays[1].start(r, spot.d, items, total)
        r.norms[...] = norm_relays[1].finish()

    return call(body, ins | beside.ins(), outs, scratch | beside.scratch(), cid)


def update_kernel(dims, rates, norms, entries, grads):
    count = len(entries)
    shapes = [entry[1].shape for entry in entries]
    ins = dict(rates=(rates, SM), norms=(norms, VM))
    outs = dict(trust=((17, 2), F32, VM))
    scratch = dict(isem=SEMS((count, 5)), osem=SEMS((count, 5)))
    for i, (params, mean, square, _) in enumerate(entries):
        tag = str(i)
        shape = shapes[i]
        pair = (2,) + shape
        ins |= {"p" + tag: (params, HB), "m" + tag: (mean, HB), "v" + tag: (square, HB)}
        ins |= {"g" + tag: (grads[i], HB)}
        scratch |= {"w" + tag: VM(pair, F32), "n" + tag: VM(shape, F32)}
        scratch |= {"q" + tag: VM(shape, F32), "h" + tag: VM(shape, F32)}
        scratch |= {"b" + tag: VM(pair, BF16)}
        outs |= {"og" + tag: (shape, F32, HB), "om" + tag: (shape, F32, HB)}
        outs |= {"ov" + tag: (shape, F32, HB), "ow" + tag: (pair, F32, HB)}
        outs |= {"ob" + tag: (pair, BF16, HB)}
    order = [7, 6] + list(range(2, 6)) + [0, 1]

    def body(r):
        get = lambda name, i: getattr(r, name + str(i))
        loads, stores = {}, []
        for i in order:
            moves = (("g", "h"), ("m", "n"), ("v", "q"), ("p", "w"))
            loads[i] = [
                pltpu.make_async_copy(get(source, i), get(target, i), r.isem.at[i, k])
                for k, (source, target) in enumerate(moves)
            ]
            for copy in loads[i]:
                copy.start()
        norms = jnp.sqrt(r.norms[...])
        r.trust[...] = norms[:17, :2]
        ratio = r.rates[3] * norms[:, 0:1] / norms[:, 1:2]

        def send(i, name, target, k):
            copy = pltpu.make_async_copy(get(name, i), get(target, i), r.osem.at[i, k])
            copy.start()
            stores.append(copy)

        for i in order:
            for copy in loads[i]:
                copy.wait()
            send(i, "h", "og", 0)
            step = tile_rows(shapes[i])
            offset = piece_rows(shapes)[i]
            for p in range(shapes[i][0]):
                scale = ratio[offset + p : offset + p + 1, :]

                def tile(j, p=p, i=i, step=step, scale=scale):
                    rs = pl.ds(pl.multiple_of(j * step, step), step)
                    master = get("w", i)[0, p, rs, :]
                    mean, square = moments_of(
                        get("h", i)[p, rs, :], get("n", i)[p, rs, :], get("q", i)[p, rs, :], r.rates
                    )
                    move = direction_of(mean, square, master, r.rates, entries[i][3])
                    master = master - scale * move
                    average = get("w", i)[1, p, rs, :]
                    average = r.rates[2] * average + (1.0 - r.rates[2]) * master
                    get("n", i)[p, rs, :] = mean
                    get("q", i)[p, rs, :] = square
                    get("w", i)[0, p, rs, :] = master
                    get("w", i)[1, p, rs, :] = average
                    get("b", i)[0, p, rs, :] = master.astype(BF16)
                    get("b", i)[1, p, rs, :] = average.astype(BF16)

                loop(shapes[i][-2] // step, tile)
            send(i, "n", "om", 1)
            send(i, "q", "ov", 2)
            send(i, "w", "ow", 3)
            send(i, "b", "ob", 4)
        for copy in stores:
            copy.wait()

    return call(body, ins, outs, scratch, None)


def shards(
    dims,
    frames_input,
    out_grad,
    lengths,
    step_count,
    rates,
    expand_params,
    expand_first,
    expand_second,
    shrink_params,
    shrink_first,
    shrink_second,
    project_params,
    project_first,
    project_second,
    mixing_params,
    mixing_first,
    mixing_second,
    gating_params,
    gating_first,
    gating_second,
    kernel_params,
    kernel_first,
    kernel_second,
    merging_params,
    merging_first,
    merging_second,
    gains_params,
    gains_first,
    gains_second,
):
    local_rows, width = frames_input.shape
    shard_rows = expand_params.shape[2]
    dims = SimpleNamespace(
        L=local_rows,
        D=width,
        S=local_rows * dims.ny * 2,
        F=expand_params.shape[3],
        H=project_params.shape[3],
        C=gating_params.shape[3],
        **vars(dims),
    )
    tensor_rank = lax.axis_index("tensor")
    data_rank = lax.axis_index("dp")
    block_y = tensor_rank // 2
    live_keys = jnp.arange(dims.S, dtype=jnp.int32) < lengths[0]
    live = live_keys.astype(F32).reshape(-1, 1)
    bias = jnp.where(live_keys, 0.0, MASKED).reshape(-1, 1)
    live_local = lax.dynamic_slice_in_dim(live, tensor_rank * local_rows, local_rows, 0)
    taps = kernel_params[0]
    gain = [gains_params[0, i : i + 1] for i in range(5)]

    expand_shard = expand_params[0].astype(BF16)
    shrink_shard = jnp.swapaxes(shrink_params[0].astype(BF16), 1, 2)
    attention_shard = jnp.concatenate(
        [project_params[0, 0], project_params[0, 1], project_params[0, 2], mixing_params[0].T], axis=1
    ).astype(BF16)
    conv_shard = jnp.concatenate(
        [gating_params[0, 0], gating_params[0, 1], merging_params[0].T], axis=1
    ).astype(BF16)
    cotangent = (out_grad.astype(F32) * live_local).astype(BF16)

    head = head_kernel(
        dims, 0, frames_input, cotangent, gain[0], expand_shard[0], shrink_shard[0]
    )
    n1, h0, expand0, shrink0 = head["n"], head["xh"], head["bo0"], head["bo1"]
    first = front_kernel(
        dims, 1, n1, expand0, shrink0, h0, gain[1], gain[2], bias, attention_shard, conv_shard,
        expand_shard[1],
    )
    middle = middle_kernel(
        dims, 2, first, taps, live, head["ogh"], gain[2:], shrink_shard[1], shard_rows
    )
    last = last_kernel(
        dims, 4, first, middle, n1, expand0, shrink0, h0, bias, gain[:2], shard_rows
    )

    frames_out = lax.dynamic_index_in_dim(middle["fo"], block_y, 0, False)

    steps_done = step_count[0].astype(F32)
    scalars = jnp.concatenate(
        [rates, 1.0 / (1.0 - rates[:2] ** steps_done), jnp.zeros((2,), F32)]
    )
    entries = []
    triples = (
        (expand_params, expand_first, expand_second),
        (shrink_params, shrink_first, shrink_second),
        (project_params, project_first, project_second),
        (mixing_params, mixing_first, mixing_second),
        (gating_params, gating_first, gating_second),
        (kernel_params, kernel_first, kernel_second),
        (merging_params, merging_first, merging_second),
        (gains_params, gains_first, gains_second),
    )
    for place in PLACES:
        params, first, second = triples[place]
        if first.ndim == 2:
            at = 1 if place == 7 else 0
            params = jnp.expand_dims(params, at + 1)
            first, second = jnp.expand_dims(first, at), jnp.expand_dims(second, at)
        entries.append((params, first, second, 0.0 if place == 7 else DECAY_RATE))
    summed = gradient_kernel(
        dims, 3, scalars, entries, [last["de"], last["dr"]],
        [middle["oute"], middle["outr"], last["sa"], last["sc"]],
        [last["dg0"], last["dg1"], middle["dg2"], middle["dg3"], middle["dg4"]], middle["dk"],
    )
    updated = update_kernel(
        dims, scalars, summed["norms"], entries, [summed["g" + str(i)] for i in range(8)]
    )
    results = []
    for place in range(8):
        tag = str(PLACES.index(place))
        like = triples[place][1].shape
        results += [updated[name + tag].reshape(like) for name in ("og", "om", "ov")]
        results += [updated[name + tag].reshape((2,) + like) for name in ("ow", "ob")]
    return (frames_out, last["gin"], *results, updated["trust"])


def solution(mesh):
    slow = math.gcd(mesh.shape["dp"], 4)
    dims = SimpleNamespace(na=slow, nb=mesh.shape["dp"] // slow, ny=mesh.shape["tensor"] // 2)
    return jax.shard_map(
        functools.partial(shards, dims),
        mesh=mesh,
        in_specs=(
            P(("dp", "tensor"), None),
            P(("dp", "tensor"), None),
            P("dp"),
            P(),
            P(),
            P(None, None, "dp", "tensor"),
            P(None, "dp", "tensor"),
            P(None, "dp", "tensor"),
            P(None, None, "tensor", "dp"),
            P(None, "tensor", "dp"),
            P(None, "tensor", "dp"),
            P(None, None, "dp", "tensor"),
            P(None, "dp", "tensor"),
            P(None, "dp", "tensor"),
            P(None, "tensor", "dp"),
            P("tensor", "dp"),
            P("tensor", "dp"),
            P(None, None, "dp", "tensor"),
            P(None, "dp", "tensor"),
            P(None, "dp", "tensor"),
            P(None, None, "tensor"),
            P(None, "tensor"),
            P(None, "tensor"),
            P(None, "tensor", "dp"),
            P("tensor", "dp"),
            P("tensor", "dp"),
            P(),
            P(),
            P(),
        ),
        out_specs=(
            P(("dp", "tensor"), None),
            P(("dp", "tensor"), None),
            P(None, "dp", "tensor"),
            P(None, "dp", "tensor"),
            P(None, "dp", "tensor"),
            P(None, None, "dp", "tensor"),
            P(None, None, "dp", "tensor"),
            P(None, "tensor", "dp"),
            P(None, "tensor", "dp"),
            P(None, "tensor", "dp"),
            P(None, None, "tensor", "dp"),
            P(None, None, "tensor", "dp"),
            P(None, "dp", "tensor"),
            P(None, "dp", "tensor"),
            P(None, "dp", "tensor"),
            P(None, None, "dp", "tensor"),
            P(None, None, "dp", "tensor"),
            P("tensor", "dp"),
            P("tensor", "dp"),
            P("tensor", "dp"),
            P(None, "tensor", "dp"),
            P(None, "tensor", "dp"),
            P(None, "dp", "tensor"),
            P(None, "dp", "tensor"),
            P(None, "dp", "tensor"),
            P(None, None, "dp", "tensor"),
            P(None, None, "dp", "tensor"),
            P(None, "tensor"),
            P(None, "tensor"),
            P(None, "tensor"),
            P(None, None, "tensor"),
            P(None, None, "tensor"),
            P("tensor", "dp"),
            P("tensor", "dp"),
            P("tensor", "dp"),
            P(None, "tensor", "dp"),
            P(None, "tensor", "dp"),
            P(),
            P(),
            P(),
            P(),
            P(),
            P(),
        ),
        check_vma=False,
    )
```

```python
import functools
import math
from types import SimpleNamespace

import jax
import jax.numpy as jnp
from jax import lax
from jax.experimental import pallas as pl
from jax.experimental.pallas import tpu as pltpu
from jax.sharding import PartitionSpec as P

HEAD_DIM = 64
KERNEL = 31

EPSILON = 1e-05
ADAM_EPS = 1e-06
DECAY_RATE = 0.01
MASKED = -1000000000.0

F32 = jnp.float32
BF16 = jnp.bfloat16
MESH = pl.DeviceIdType.MESH
STEP = 16
TILE = 256
GRANT = 60 * 1024 * 1024


class Spot:
    def __init__(self, dims):
        self.dims = dims
        self.d = lax.axis_index("dp")
        self.t = lax.axis_index("tensor")
        self.y = lax.div(self.t, 2)
        self.c = lax.rem(self.t, 2)
        self.a = lax.div(self.d, dims.nb)
        self.b = lax.rem(self.d, dims.nb)

    def sibling(self):
        return (self.d, self.y * 2 + 1 - self.c)

    def across(self, j):
        return (self.d, lax.rem(self.y + j, self.dims.ny) * 2 + self.c)

    def slow(self, j):
        return (lax.rem(self.a + j, self.dims.na) * self.dims.nb + self.b, self.t)

    def fast(self, j):
        return (self.a * self.dims.nb + lax.rem(self.b + j, self.dims.nb), self.t)

    def tensor_peers(self):
        return [self.sibling()] + [self.across(j) for j in range(1, self.dims.ny)]

    def data_peers(self):
        return [self.slow(j) for j in range(1, self.dims.na)] + [
            self.fast(j) for j in range(1, self.dims.nb)
        ]


def greet(peers):
    barrier = pltpu.get_barrier_semaphore()
    for peer in peers:
        pl.semaphore_signal(barrier, 1, device_id=peer, device_id_type=MESH)
    pl.semaphore_wait(barrier, len(peers))


def remote(source, target, send, recv, peer):
    return pltpu.make_async_remote_copy(
        src_ref=source,
        dst_ref=target,
        send_sem=send,
        recv_sem=recv,
        device_id=peer,
        device_id_type=MESH,
    )


def loop(count, body, unroll=1):
    def step(i, carry):
        body(i)
        return carry

    lax.fori_loop(0, count, step, 0, unroll=unroll)


def rows_of(i, step=STEP):
    return pl.ds(pl.multiple_of(i * step, step), step)


class Refs(SimpleNamespace):
    def need(self, *names):
        for name in names:
            if name in self.pending:
                self.pending.pop(name).wait()

    def done(self, *names):
        for name in names:
            copy = self.unsent.pop(name)
            copy.start()
            self.leaving.append(copy)

    def close(self):
        self.need(*list(self.pending))
        self.done(*list(self.unsent))
        for copy in self.leaving:
            copy.wait()


def call(body, ins, outs, scratch, cid):
    in_names, out_names, scratch_names = list(ins), list(outs), list(scratch)
    loads = [name for name in in_names if ins[name][1] in (LD, LD0)]
    stores = [name for name in out_names if outs[name][2] is ST]
    whole = {name: ins[name][1] is LD for name in loads}
    copies = [
        VM(ins[name][0].shape[0 if whole[name] else 1 :], ins[name][0].dtype) for name in loads
    ]
    copies += [VM(outs[name][0], outs[name][1]) for name in stores]
    sems = [SEMS((max(len(copies), 1),))]

    def place(space):
        return pl.BlockSpec(memory_space=HB if space in (LD, LD0, ST) else space)

    def kernel(*refs):
        names = in_names + out_names + scratch_names
        given = dict(zip(names, refs))
        held = refs[len(names) : -1]
        r = Refs(**given, pending={}, unsent={}, leaving=[])
        for i, name in enumerate(loads):
            source = given[name] if whole[name] else given[name].at[0]
            r.pending[name] = pltpu.make_async_copy(source, held[i], refs[-1].at[i])
            setattr(r, name, held[i])
        for i, name in enumerate(stores, len(loads)):
            r.unsent[name] = pltpu.make_async_copy(held[i], given[name], refs[-1].at[i])
            setattr(r, name, held[i])
        for copy in r.pending.values():
            copy.start()
        body(r)
        r.close()

    results = pl.pallas_call(
        kernel,
        out_shape=[jax.ShapeDtypeStruct(shape, kind) for shape, kind, _ in outs.values()],
        in_specs=[place(space) for _, space in ins.values()],
        out_specs=[place(space) for _, _, space in outs.values()],
        scratch_shapes=list(scratch.values()) + copies + sems,
        compiler_params=pltpu.CompilerParams(
            collective_id=cid, has_side_effects=cid is not None, vmem_limit_bytes=GRANT
        ),
    )(*[array for array, _ in ins.values()])
    return dict(zip(out_names, results))


LD, LD0, ST = object(), object(), object()
VM = pltpu.VMEM
HB = pl.ANY
SM = pltpu.SMEM
SEMS = pltpu.SemaphoreType.DMA


def tagged(prefix, tag, specs):
    return {prefix + name + tag: spec for name, spec in specs.items()}


def bound(refs, prefix, tag, specs):
    return SimpleNamespace(**{name: getattr(refs, prefix + name + tag) for name in specs})


class Gather:
    def __init__(self, tag, dims):
        self.tag, self.dims = tag, dims
        na, nb = dims.na, dims.nb
        m, k = max(nb - 1, 1), max(na - 1, 1)
        self.specs = dict(
            loc=SEMS,
            xs=SEMS((m,)),
            xr=SEMS((m,)),
            us=SEMS((k,)),
            ur=SEMS((k,)),
            ds=SEMS((k,)),
            dr=SEMS((k,)),
            fs=SEMS((2, k, m)),
            fr=SEMS((2, k, m)),
        )
        self.stage = 0

    def scratch(self):
        return tagged("g", self.tag, self.specs)

    def bind(self, refs, spot, source, whole, columns=None):
        self.sem = bound(refs, "g", self.tag, self.specs)
        self.spot, self.source, self.whole, self.columns = spot, source, whole, columns
        return self

    def rows(self, d):
        shard = self.source.shape[0]
        rows = pl.ds(pl.multiple_of(d * shard, shard), shard)
        return self.whole.at[rows] if self.columns is None else self.whole.at[rows, self.columns]

    def block(self, a):
        return self.rows(a * self.dims.nb + self.spot.b)

    def hop(self, way, s):
        spot, sem = self.spot, self.sem
        step = 1 if way == 0 else -1
        target = self.block(spot.a - step * (s - 1))
        source = self.source if s == 1 else target
        send, recv = (sem.us, sem.ur) if way == 0 else (sem.ds, sem.dr)
        peer = ((spot.a + step) * self.dims.nb + spot.b, spot.t)
        return remote(source, target, send.at[s - 1], recv.at[s - 1], peer)

    def sends(self, way, s):
        spot, na = self.spot, self.dims.na
        if way == 0:
            return jnp.logical_and(spot.a - (s - 1) >= 0, spot.a + 1 < na)
        return jnp.logical_and(spot.a + (s - 1) < na, spot.a - 1 >= 0)

    def has(self, way, s):
        return self.spot.a - s >= 0 if way == 0 else self.spot.a + s < self.dims.na

    def hand(self, way, s, i):
        block = self.block(self.spot.a - s if way == 0 else self.spot.a + s)
        sem = self.sem
        return remote(
            block, block, sem.fs.at[way, s - 1, i - 1], sem.fr.at[way, s - 1, i - 1], self.spot.fast(i)
        )

    def start(self):
        spot, dims, sem = self.spot, self.dims, self.sem
        mine = self.rows(spot.d)
        if dims.na > 1:
            for way in range(2):

                @pl.when(self.sends(way, 1))
                def _(way=way):
                    self.hop(way, 1).start()

        self.own = [
            remote(self.source, mine, sem.xs.at[j - 1], sem.xr.at[j - 1], spot.fast(j))
            for j in range(1, dims.nb)
        ]
        for copy in self.own:
            copy.start()
        self.local = pltpu.make_async_copy(self.source, mine, sem.loc)
        self.local.start()

    def advance(self):
        dims = self.dims
        self.stage += 1
        s = self.stage
        if s >= dims.na:
            return False
        for way in range(2):

            @pl.when(self.has(way, s))
            def _(way=way):
                self.hop(way, s).wait_recv()
                for i in range(1, dims.nb):
                    self.hand(way, s, i).start()

            if s + 1 < dims.na:

                @pl.when(self.sends(way, s + 1))
                def _(way=way):
                    self.hop(way, s + 1).start()

        return True

    def finish(self):
        dims = self.dims
        while self.advance():
            pass
        self.local.wait()
        for copy in self.own:
            copy.wait()
        for s in range(1, dims.na):
            for way in range(2):

                @pl.when(self.sends(way, s))
                def _(way=way, s=s):
                    self.hop(way, s).wait_send()

                @pl.when(self.has(way, s))
                def _(way=way, s=s):
                    for i in range(1, dims.nb):
                        self.hand(way, s, i).wait()


class Scatter:
    def __init__(self, tag, dims, rows, first, columns, into=None):
        self.tag, self.dims, self.size = tag, dims, (rows, columns)
        self.columns = pl.ds(first, columns)
        self.into = self.columns if into is None else pl.ds(into, columns)
        na, nb = dims.na, dims.nb
        m = max(nb - 1, 1)
        self.specs = dict(
            held=VM((na, rows, columns), BF16),
            one=VM((m, na, rows, columns), BF16),
            two=VM((na // 2, rows, columns), BF16),
            three=VM((rows, columns), BF16),
            loc=SEMS,
            xs=SEMS((m,)),
            xr=SEMS((m,)),
            zs=SEMS((na // 2,)),
            zr=SEMS((na // 2,)),
            ls=SEMS,
            lr=SEMS,
        )
        self.stage = 0

    def scratch(self):
        return tagged("s", self.tag, self.specs)

    def bind(self, refs, spot, source, result):
        self.r = bound(refs, "s", self.tag, self.specs)
        self.spot, self.source, self.result = spot, source, result
        self.low, self.high = lax.rem(spot.a, 2), lax.div(spot.a, 2)
        return self

    def start(self):
        spot, dims, r = self.spot, self.dims, self.r
        self.sent = []
        for j in range(1, dims.nb):
            block = lax.rem(spot.b + j, dims.nb)
            copy = remote(
                self.source.at[:, block, :, self.columns],
                r.one.at[j - 1],
                r.xs.at[j - 1],
                r.xr.at[j - 1],
                spot.fast(j),
            )
            copy.start()
            self.sent.append(copy)
        self.local = pltpu.make_async_copy(
            self.source.at[:, spot.b, :, self.columns], r.held, r.loc
        )
        self.local.start()

    def blocks(self, low):
        return [low + 2 * i for i in range(self.dims.na // 2)]

    def place(self, high, low):
        return (high * 2 + low) * self.dims.nb + self.spot.b, self.spot.t

    def advance(self):
        spot, dims, r = self.spot, self.dims, self.r
        rows, columns = self.size
        self.stage += 1
        if self.stage == 1:
            self.local.wait()
            for copy in self.sent:
                copy.wait_recv()
            for a in range(dims.na):

                def add(i, a=a):
                    rs = rows_of(i)
                    total = r.held[a, rs, :].astype(F32)
                    for j in range(dims.nb - 1):
                        total = total + r.one[j, a, rs, :].astype(F32)
                    r.held[a, rs, :] = total.astype(BF16)

                loop(rows // STEP, add, 2)
            self.pair = []
            for i, a in enumerate(self.blocks(1 - self.low)):
                copy = remote(
                    r.held.at[a], r.two.at[i], r.zs.at[i], r.zr.at[i],
                    self.place(self.high, 1 - self.low),
                )
                copy.start()
                self.pair.append(copy)
            return True
        if self.stage == 2:
            for i, a in enumerate(self.blocks(self.low)):
                self.pair[i].wait()

                def join(j, i=i, a=a):
                    rs = rows_of(j)
                    total = r.held[a, rs, :].astype(F32) + r.two[i, rs, :].astype(F32)
                    r.held[a, rs, :] = total.astype(BF16)

                loop(rows // STEP, join, 2)
            self.final = remote(
                r.held.at[(1 - self.high) * 2 + self.low], r.three, r.ls, r.lr,
                self.place(1 - self.high, self.low),
            )
            self.final.start()
            return True
        return False

    def finish(self):
        while self.advance():
            pass
        r = self.r
        rows, columns = self.size
        self.final.wait()

        def add(i):
            rs = rows_of(i)
            total = r.held[self.spot.a, rs, :].astype(F32) + r.three[rs, :].astype(F32)
            self.result[rs, self.into] = total

        loop(rows // STEP, add, 2)
        for copy in self.sent:
            copy.wait_send()


class Edge:
    def __init__(self, dims, count):
        self.dims, self.count = dims, count

    def scratch(self):
        nc, Q, D, count = self.dims.nc, self.dims.Q, self.dims.D, self.count
        m = max(self.dims.ny - 1, 1)
        return dict(
            e_own=VM((nc, Q, D), F32),
            e_give=VM((nc, Q, D), BF16),
            e_take=VM((nc, Q, D), BF16),
            e_sum=VM((nc, Q, D), BF16),
            e_far=VM((min(count, 2), m, nc, Q, D), BF16),
            e_ds=SEMS((count, nc)),
            e_dr=SEMS((count, nc)),
            e_ys=SEMS((count, m, nc)),
            e_yr=SEMS((count, m, nc)),
            e_ns=SEMS((count, nc)),
            e_nr=SEMS((count, nc)),
        )

    def bind(self, refs, spot):
        self.refs, self.spot = refs, spot
        self.near, self.far, self.handed = {}, {}, {}
        return self

    def open(self, i, k):
        if i > 0:
            self.near.pop((i - 1, k)).wait_send()

    def put(self, k, columns, part):
        Q, refs = self.dims.Q, self.refs
        low, high = part[:Q], part[Q:]
        first = self.spot.c == 0
        refs.e_own[k, :, columns] = jnp.where(first, low, high)
        refs.e_give[k, :, columns] = jnp.where(first, high, low).astype(BF16)

    def start(self, i, k):
        refs = self.refs
        copy = remote(
            refs.e_give.at[k],
            refs.e_take.at[k],
            refs.e_ds.at[i, k],
            refs.e_dr.at[i, k],
            self.spot.sibling(),
        )
        copy.start()
        self.near[i, k] = copy

    def cross(self, i, k, send=True):
        refs, dims = self.refs, self.dims
        self.near[i, k].wait_recv()
        if i > 0:
            for copy in self.far.pop((i - 1, k)):
                copy.wait_send()

        def add(j):
            rs = rows_of(j)
            total = refs.e_own[k, rs, :] + refs.e_take[k, rs, :].astype(F32)
            refs.e_own[k, rs, :] = total
            refs.e_sum[k, rs, :] = total.astype(BF16)

        loop(dims.Q // STEP, add, 2)
        if send:
            self.far[i, k] = []
            for j in range(1, dims.ny):
                copy = remote(
                    refs.e_sum.at[k],
                    refs.e_far.at[i % 2, j - 1, k],
                    refs.e_ys.at[i, j - 1, k],
                    refs.e_yr.at[i, j - 1, k],
                    self.spot.across(j),
                )
                copy.start()
                self.far[i, k].append(copy)

    def total(self, i, k, rs, slot):
        refs = self.refs
        total = refs.e_own[k, rs, :]
        for j in range(self.dims.ny - 1):
            total = total + refs.e_far[i % 2, j, slot, rs, :].astype(F32)
        return total

    def settle(self, i, k, row_fn, target):
        refs, dims, spot = self.refs, self.dims, self.spot
        for copy in self.far[i, k]:
            copy.wait_recv()
        base = (k * 2 + spot.c) * dims.Q

        def body(j):
            rs = rows_of(j)
            rows = row_fn(self.total(i, k, rs, k), k, rs)
            target[pl.ds(pl.multiple_of(base + j * STEP, STEP), STEP), :] = rows

        loop(dims.Q // STEP, body, 2)
        block = target.at[pl.ds(pl.multiple_of(base, dims.Q), dims.Q)]
        copy = remote(block, block, refs.e_ns.at[i, k], refs.e_nr.at[i, k], spot.sibling())
        copy.start()
        self.handed[i, k] = copy

    def arrived(self, i, k):
        self.handed[i, k].wait_recv()

    def drain(self):
        for copy in list(self.near.values()) + list(self.handed.values()):
            copy.wait_send()
        for copies in self.far.values():
            for copy in copies:
                copy.wait_send()


def unit(hidden):
    center = hidden - jnp.mean(hidden, axis=-1, keepdims=True)
    spread = jnp.mean(center * center, axis=-1, keepdims=True)
    inverse = lax.rsqrt(spread + EPSILON)
    return center * inverse, inverse


def unit_back(upstream, xhat, inverse, gain):
    scaled = upstream * gain
    return inverse * (
        scaled
        - jnp.mean(scaled, axis=-1, keepdims=True)
        - xhat * jnp.mean(scaled * xhat, axis=-1, keepdims=True)
    )


def fold(rows):
    return rows[:8] + rows[8:]


def chunk_rows(dims, k):
    return pl.ds(k * dims.L, dims.L)


def up_products(dims, k, normed, expand, inner, slope):
    rows = chunk_rows(dims, k)

    def column(j):
        cs = rows_of(j, TILE)
        before = jnp.dot(normed[rows, :], expand[:, cs], preferred_element_type=F32)
        gate = jax.nn.sigmoid(before)
        inner[rows, cs] = (before * gate).astype(BF16)
        slope[rows, cs] = (gate * (1.0 + before * (1.0 - gate))).astype(BF16)

    loop(dims.F // TILE, column, True)


def back_products(dims, k, upstream, shrink, slope, back):
    rows = chunk_rows(dims, k)

    def column(j):
        cs = rows_of(j, TILE)
        part = jnp.dot(upstream[rows, :], shrink[:, cs], preferred_element_type=F32)
        back[rows, cs] = (part * slope[rows, cs].astype(F32)).astype(BF16)

    loop(dims.F // TILE, column, True)


def part_product(edge, i, k, operand, matrix, first, dims):
    width = operand.shape[1]
    edge.open(i, k)

    def column(j):
        cs = rows_of(j, TILE)
        edge.put(
            k,
            cs,
            lax.dot_general(
                operand[chunk_rows(dims, k), :],
                matrix[cs, pl.ds(first, width)],
                (((1,), (1,)), ((), ())),
                preferred_element_type=F32,
            ),
        )

    loop(dims.D // TILE, column, True)
    edge.start(i, k)


def weight_part(result, first, rows_side, columns_side, dims):
    width = columns_side.shape[1]
    shard = result.shape[2]
    for i in range(dims.D // TILE):
        part = lax.dot_general(
            rows_side[:, pl.ds(i * TILE, TILE)],
            columns_side[...],
            (((0,), (0,)), ((), ())),
            preferred_element_type=F32,
        ).astype(BF16)
        for j in range(TILE // shard):
            d = i * (TILE // shard) + j
            result[d // dims.nb, d % dims.nb, :, pl.ds(first, width)] = part[
                j * shard : (j + 1) * shard
            ]


def forward_rows(hidden, scale, gain, kept):
    def rows(total, k, rs):
        after = hidden[k, rs, :].astype(F32) + scale * total
        kept[k, rs, :] = after
        xhat, _ = unit(after)
        return (xhat * gain[...]).astype(BF16)

    return rows


def backward_rows(hidden, scale, gain, grad, sums, spot):
    def rows(total, k, rs):
        xhat, inverse = unit(hidden[k, rs, :].astype(F32))
        own = jnp.where(spot.y == k // 2, 1.0, 0.0)
        sums[...] += fold(total * xhat) * own
        after = grad[k, rs, :] + unit_back(total, xhat, inverse, gain[...])
        grad[k, rs, :] = after
        return (scale * after).astype(BF16)

    return rows


QUERIES = 256
BAND = 64
MARGIN = 16


def slide(padded, base, taps, flip=False):
    window = padded[pl.ds(pl.multiple_of(base, BAND), BAND + 2 * MARGIN), :]
    total = None
    for residue in range(8):
        shifted = window[residue : residue + BAND + 24]
        for eighth in range(4):
            tap = 8 * eighth + residue - 1
            if 0 <= tap < KERNEL:
                place = KERNEL - 1 - tap if flip else tap
                term = shifted[8 * eighth : 8 * eighth + BAND] * taps[place, 0:1, :]
                total = term if total is None else total + term
    return total


def clear_margins(padded, S):
    edge = jnp.zeros((MARGIN, padded.shape[1]), F32)
    padded[pl.ds(0, MARGIN), :] = edge
    padded[pl.ds(MARGIN + S, MARGIN), :] = edge


def attend(dims, k, r):
    H, m = dims.H, dims.L
    heads = H // HEAD_DIM
    blocks = m // min(QUERIES, m)
    size = m // blocks

    def one(i):
        head = lax.div(i, blocks)
        at = pl.ds(pl.multiple_of(k * m + lax.rem(i, blocks) * size, size), size)
        scores = lax.dot_general(
            r.k[head], r.q[head, at, :], (((1,), (1,)), ((), ())), preferred_element_type=F32
        )
        scores = scores + r.column[...]
        peak = jnp.max(scores, axis=0, keepdims=True)
        exponent = jnp.exp(scores - peak)
        total = jnp.sum(exponent, axis=0, keepdims=True)
        output = jnp.dot(r.vt[head], exponent.astype(BF16), preferred_element_type=F32)
        r.lse[head, :, at] = peak + jnp.log(total)
        r.ot[pl.ds(pl.multiple_of(head * HEAD_DIM, HEAD_DIM), HEAD_DIM), at] = output / total

    loop(heads * blocks, one)
    rows = chunk_rows(dims, k)
    r.oh[rows, :] = r.ot[:, rows].T.astype(BF16)


def live_column(r, S, dead):
    place = lax.broadcasted_iota(jnp.int32, (S, 1), 0)
    live, other = (0.0, MASKED) if dead else (1.0, 0.0)
    r.column[...] = jnp.where(place < r.lengths[0], live, other)


def front_kernel(
    dims, cid, frames, cotangent, lengths, gains, expand, shrink, project, mixing, gating, merging
):
    nc, L, Q, D, S, F, H, C = (
        dims.nc, dims.L, dims.Q, dims.D, dims.S, dims.F, dims.H, dims.C
    )
    heads = H // HEAD_DIM
    shard = expand.shape[2]
    edge = Edge(dims, 2)
    gathers = [Gather(str(i), dims) for i in range(6)]
    half = F // 2
    scratch = edge.scratch() | dict(
        vt=VM((heads, HEAD_DIM, S), BF16),
        ot=VM((H, S), F32),
        column=VM((S, 1), F32),
        ogl=VM((2, Q, D), BF16),
        s0=VM((shard, F), BF16),
        s1=VM((shard, F), BF16),
        s2=VM((shard, 4 * H), BF16),
        s3=VM((shard, 3 * C), BF16),
        s4=VM((shard, F), BF16),
        s5=VM((shard, half), BF16),
        xs=SEMS((nc,)),
        xr=SEMS((nc,)),
        os=SEMS((nc,)),
        orr=SEMS((nc,)),
        ns=SEMS((nc,)),
        nr=SEMS((nc,)),
    )
    for gather in gathers:
        scratch |= gather.scratch()

    def body(r):
        spot = Spot(dims)
        others = [(spot.d, lax.rem(spot.t + j, nc)) for j in range(1, nc)]
        greet(others + spot.data_peers())
        edge.bind(r, spot)
        for i, (source, whole) in enumerate(
            ((r.s0, r.e), (r.s1, r.rt), (r.s2, r.wa), (r.s3, r.wc), (r.s4, r.e1), (r.s5, r.ra))
        ):
            gathers[i].bind(r, spot, source, whole)
        r.need("x")
        moves = []
        for j in range(1, nc):
            some = pl.ds(pl.multiple_of(lax.rem(spot.c + j, 2) * Q, Q), Q)
            copy = remote(
                r.x.at[some], r.xh.at[spot.t], r.xs.at[j - 1], r.xr.at[j - 1], others[j - 1]
            )
            copy.start()
            moves.append(copy)

        r.need("pe")
        r.s0[...] = r.pe[0].astype(BF16)
        gathers[0].start()
        r.need("pr")

        def turned(target, first, source, begin=0, count=None):
            def part(j):
                cs = pl.ds(pl.multiple_of(begin + j * 128, 128), 128)
                target[:, pl.ds(pl.multiple_of(first + j * 128, 128), 128)] = (
                    source[cs, :].T.astype(BF16)
                )

            loop((count or source.shape[0]) // 128, part, True)

        turned(r.s1, 0, r.pr.at[0])
        gathers[1].start()
        mine = pl.ds(pl.multiple_of(spot.c * Q, Q), Q)
        r.xh[spot.t] = r.x[mine, :]

        handed = []

        def normalize(t):
            base = pl.multiple_of((t * 2 + spot.c) * Q, Q)

            def rows(i):
                xhat, _ = unit(r.xh[t, rows_of(i), :].astype(F32))
                target = pl.ds(pl.multiple_of(base + i * STEP, STEP), STEP)
                r.n1[target, :] = (xhat * r.g0[...]).astype(BF16)

            loop(Q // STEP, rows, 2)
            block = r.n1.at[pl.ds(base, Q)]
            i = len(handed)
            copy = remote(block, block, r.ns.at[i], r.nr.at[i], spot.sibling())
            copy.start()
            handed.append(copy)

        normalize(spot.t)
        r.need("og")
        place = lax.broadcasted_iota(jnp.int32, (Q, 1), 0) + spot.t * L
        for i in range(2):
            live = place + i * Q < r.lengths[0]
            r.ogl[i] = jnp.where(live, r.og[pl.ds(i * Q, Q), :].astype(F32), 0.0).astype(BF16)
        for j in range(1, nc):
            copy = remote(
                r.ogl.at[lax.rem(spot.c + j, 2)], r.ogh.at[spot.t], r.os.at[j - 1], r.orr.at[j - 1],
                others[j - 1],
            )
            copy.start()
            moves.append(copy)
        r.ogh[spot.t] = r.ogl[spot.c]
        gathers[0].advance()
        gathers[1].advance()
        for j in range(1, nc):
            moves[j - 1].wait_recv()
            normalize(lax.rem(spot.t + nc - j, nc))
        gathers[0].advance()
        gathers[1].advance()

        r.need("pp", "pm", "pg", "pz")
        for i in range(3):
            r.s2[:, pl.ds(i * H, H)] = r.pp[i].astype(BF16)
        turned(r.s2, 3 * H, r.pm)
        for i in range(2):
            r.s3[:, pl.ds(i * C, C)] = r.pg[i].astype(BF16)
        turned(r.s3, 2 * C, r.pz)
        r.s4[...] = r.pe[1].astype(BF16)
        turned(r.s5, 0, r.pr.at[1], 0, half)
        turned(r.r1, 0, r.pr.at[1], half, half)
        r.done("r1")
        live_column(r, S, True)
        gathers[0].advance()
        gathers[1].advance()
        gathers[2].start()
        for copy in handed:
            copy.wait()
        gathers[0].finish()

        for k in range(nc):
            up_products(dims, k, r.n1, r.e, r.u, r.slope)
            if k == 0:
                gathers[1].finish()
            part_product(edge, 0, k, r.u, r.rt, 0, dims)
            if k > 0:
                edge.cross(0, k - 1)
        edge.cross(0, nc - 1)
        r.done("u", "slope", "n1", "e", "rt")
        gathers[2].advance()
        for k in range(nc):
            edge.settle(0, k, forward_rows(r.xh, 0.5, r.g1, r.h1), r.n2)
            if k < 2:
                gathers[2].advance()
            if k == 1:
                gathers[3].start()
        gathers[3].advance()
        r.done("h1")
        for k in range(nc):
            edge.arrived(0, k)
        r.done("n2")
        gathers[2].finish()
        gathers[4].start()
        for i, target in enumerate((r.q, r.k, r.v)):
            packed = jnp.dot(r.n2[...], r.wa[:, pl.ds(i * H, H)], preferred_element_type=F32)
            if i == 0:
                packed = packed.astype(BF16).astype(F32) * HEAD_DIM**-0.5
            for j in range(heads):
                part = packed[:, j * HEAD_DIM : (j + 1) * HEAD_DIM]
                target[j] = part.astype(BF16)
                if i == 2:
                    r.vt[j] = part.T.astype(BF16)
        r.done("q", "k", "v", "wa")

        for k in range(nc):
            attend(dims, k, r)
            part_product(edge, 1, k, r.oh, r.wa, 3 * H, dims)
            if k > 0:
                edge.cross(1, k - 1)
            gathers[3 if k < 2 else 4].advance()
            if k == 2:
                gathers[5].start()
        edge.cross(1, nc - 1)
        r.done("oh", "lse")
        for k in range(nc):
            edge.settle(1, k, forward_rows(r.h1, 1.0, r.g2, r.h2), r.n3)
            gathers[4 if k == 0 else 5].advance()
        r.done("h2")
        for k in range(nc):
            edge.arrived(1, k)
        r.done("n3")
        for copy in moves[: nc - 1]:
            copy.wait_send()
        for copy in moves[nc - 1 :]:
            copy.wait()
        edge.drain()
        for gather in gathers[3:]:
            gather.finish()

    triple = (heads, S, HEAD_DIM)
    rows_all, held = (S, D), (nc, Q, D)
    return call(
        body,
        dict(
            x=(frames, LD),
            pe=(expand, LD0),
            pr=(shrink, LD0),
            og=(cotangent, LD),
            pp=(project, LD0),
            pm=(mixing, LD0),
            pg=(gating, LD0),
            pz=(merging, LD0),
            lengths=(lengths, SM),
            g0=(gains[0], VM),
            g1=(gains[1], VM),
            g2=(gains[2], VM),
        ),
        dict(
            xh=(held, BF16, ST),
            ogh=(held, BF16, ST),
            n1=(rows_all, BF16, ST),
            e=((D, F), BF16, ST),
            rt=((D, F), BF16, ST),
            u=((S, F), BF16, ST),
            slope=((S, F), BF16, ST),
            h1=(held, F32, ST),
            n2=(rows_all, BF16, ST),
            q=(triple, BF16, ST),
            k=(triple, BF16, ST),
            v=(triple, BF16, ST),
            oh=((S, H), BF16, ST),
            lse=((heads, 1, S), F32, ST),
            h2=(held, F32, ST),
            n3=(rows_all, BF16, ST),
            wa=((D, 4 * H), BF16, ST),
            r1=((shard, half), BF16, ST),
            ra=((D, half), BF16, HB),
            wc=((D, 3 * C), BF16, HB),
            e1=((D, F), BF16, HB),
        ),
        scratch,
        cid,
    )


def middle_kernel(dims, cid, kept, lengths, taps, gains, shard):
    nc, Q, D, S, F, C = dims.nc, dims.Q, dims.D, dims.S, dims.F, dims.C
    m = dims.L
    edge = Edge(dims, 4)
    gather = Gather("0", dims)
    half = F // 2
    scatters = [Scatter(str(j), dims, shard, half * (j % 2), half) for j in range(3)]
    four = (dims.na, dims.nb, shard)
    scratch = edge.scratch() | gather.scratch()
    scratch |= dict(
        rt=VM((D, F), BF16),
        n4=VM((S, D), BF16),
        h3=VM((nc, Q, D), F32),
        fall=VM((nc, Q, D), BF16),
        column=VM((S, 1), F32),
        rsem=SEMS,
        fsem=SEMS((3,)),
        u=VM((S, F), BF16),
        slope=VM((S, F), BF16),
        w4=VM((S, D), BF16),
        dr=VM(four + (F,), BF16),
        w3=VM((S, D), BF16),
        z=VM((S, C), BF16),
        zslope=VM((S, C), F32),
        ga=VM((S, C), F32),
        gb=VM((S, C), F32),
        glu=VM((S + 2 * MARGIN, C), F32),
        back=VM((S + 2 * MARGIN, C), F32),
        pair=VM((S, 2 * C), BF16),
        sums=VM((KERNEL, 8, C), F32),
    )
    for scatter in scatters:
        scratch |= scatter.scratch()

    def body(r):
        spot = Spot(dims)
        greet(spot.tensor_peers() + spot.data_peers())
        edge.bind(r, spot)
        gather.bind(r, spot, r.sr, r.rt, pl.ds(half, half)).start()
        early = pltpu.make_async_copy(r.ra, r.rt.at[:, pl.ds(0, half)], r.rsem)
        early.start()
        for scatter in scatters[:2]:
            scatter.bind(r, spot, r.dr, r.outr)
        scatters[2].bind(r, spot, r.de, r.oute)
        for sums in (r.dg2, r.dg3, r.dg4):
            sums[...] = jnp.zeros_like(sums)

        clear_margins(r.glu, S)
        clear_margins(r.back, S)
        live_column(r, S, False)
        r.need("n", "wc")

        def gated(i):
            rows = rows_of(i, 256)
            values = jnp.dot(r.n[rows, :], r.wc[:, pl.ds(0, C)], preferred_element_type=F32)
            gate = jax.nn.sigmoid(
                jnp.dot(r.n[rows, :], r.wc[:, pl.ds(C, C)], preferred_element_type=F32)
            )
            open_gate = gate * r.column[rows, :]
            product = values * open_gate
            r.ga[rows, :] = open_gate
            r.gb[rows, :] = product * (1.0 - gate)
            r.glu[pl.ds(pl.multiple_of(i * 256 + MARGIN, MARGIN), 256), :] = product

        loop(S // 256, gated)
        for k in range(nc):

            def band(i, k=k):
                base = k * m + i * BAND
                mixed = slide(r.glu, base, r.taps)
                gate = jax.nn.sigmoid(mixed)
                rows = pl.ds(pl.multiple_of(base, BAND), BAND)
                r.z[rows, :] = (mixed * gate).astype(BF16)
                r.zslope[rows, :] = gate * (1.0 + mixed * (1.0 - gate))

            loop(m // BAND, band)
            part_product(edge, 0, k, r.z, r.wc, 2 * C, dims)
            if k > 0:
                edge.cross(0, k - 1)
            if k % 2 == 1:
                gather.advance()
        edge.cross(0, nc - 1)
        gather.advance()

        r.need("h", "e")
        for k in range(nc):
            edge.settle(0, k, forward_rows(r.h, 1.0, r.g3, r.h3), r.n4)
            edge.arrived(0, k)
            up_products(dims, k, r.n4, r.e, r.u, r.slope)
            if k == 0:
                early.wait()
                gather.finish()
            part_product(edge, 1, k, r.u, r.rt, 0, dims)
            edge.cross(1, k)

        def turn(total, k, rs):
            xhat, inverse = unit(r.h3[k, rs, :] + 0.5 * total)
            r.fall[k, rs, :] = (xhat * r.g4[...]).astype(BF16)
            upstream = r.og[k, rs, :].astype(F32)
            own = jnp.where(spot.y == k // 2, 1.0, 0.0)
            r.dg4[...] += fold(upstream * xhat) * own
            grad = unit_back(upstream, xhat, inverse, r.g4[...])
            r.gh[k, rs, :] = grad
            return (0.5 * grad).astype(BF16)

        r.need("og")
        for k in range(nc):
            edge.settle(1, k, turn, r.w4)
            edge.arrived(1, k)
            back_products(dims, k, r.w4, r.rt, r.slope, r.slope)
            part_product(edge, 2, k, r.slope, r.e, 0, dims)
            edge.cross(2, k)
        keep = pltpu.make_async_copy(r.fall.at[spot.t], r.fo.at[spot.c], r.fsem.at[2])
        keep.start()
        other = spot.y * 2 + 1 - spot.c
        give = remote(
            r.fall.at[other], r.fo.at[spot.c], r.fsem.at[0], r.fsem.at[1], spot.sibling()
        )
        give.start()
        weight_part(r.dr, 0, r.w4, r.u, dims)
        for scatter in scatters[:2]:
            scatter.start()
        weight_part(r.de, 0, r.n4, r.slope, dims)
        scatters[2].start()
        r.done("de")

        finished = 0
        for k in range(nc):
            edge.settle(2, k, backward_rows(r.h3, 1.0, r.g3, r.gh, r.dg3, spot), r.w3)
            edge.arrived(2, k)
            rows = chunk_rows(dims, k)
            inner = jnp.dot(r.w3[rows, :], r.wc[:, pl.ds(2 * C, C)], preferred_element_type=F32)
            r.back[pl.ds(k * m + MARGIN, m), :] = inner * r.zslope[rows, :]
            until = (k + 1) * m // BAND - (1 if k < nc - 1 else 0)

            def band(i, finished=finished):
                base = (i + finished) * BAND
                rows = pl.ds(pl.multiple_of(base, BAND), BAND)
                mixed = slide(r.back, base, r.taps, True)
                r.pair[rows, pl.ds(0, C)] = (mixed * r.ga[rows, :]).astype(BF16)
                r.pair[rows, pl.ds(C, C)] = (mixed * r.gb[rows, :]).astype(BF16)

            loop(until - finished, band)
            finished = until
            if k == 2:
                scatters[0].advance()
            if k > 0:
                part_product(edge, 3, k - 1, r.pair, r.wc, 0, dims)
            if k > 1:
                edge.cross(3, k - 2)
        edge.cross(3, nc - 2)
        part_product(edge, 3, nc - 1, r.pair, r.wc, 0, dims)
        edge.cross(3, nc - 1)
        scatters[1].advance()
        weight_part(r.dw, 0, r.n, r.pair, dims)
        weight_part(r.dw, 2 * C, r.w3, r.z, dims)
        r.done("dw")
        scatters[0].advance()
        r.sums[...] = jnp.zeros_like(r.sums)

        def tap_sums(i):
            base = i * BAND
            window = r.glu[pl.ds(pl.multiple_of(base, BAND), BAND + 2 * MARGIN), :]
            slope = r.back[pl.ds(pl.multiple_of(base + MARGIN, MARGIN), BAND), :]
            for residue in range(8):
                shifted = window[residue : residue + BAND + 24]
                for eighth in range(4):
                    tap = 8 * eighth + residue - 1
                    if 0 <= tap < KERNEL:
                        term = shifted[8 * eighth : 8 * eighth + BAND] * slope
                        r.sums[tap] += term.reshape(BAND // 8, 8, C).sum(axis=0)

        loop(S // BAND, tap_sums)
        for tap in range(KERNEL):
            r.dk[tap : tap + 1, :] = jnp.sum(r.sums[tap], axis=0, keepdims=True)
        for k in range(nc):
            edge.settle(3, k, backward_rows(r.h, 1.0, r.g2, r.gh, r.dg2, spot), r.w2)
            if k == 0:
                scatters[2].advance()
            elif k == 1:
                scatters[1].advance()
            elif k == 2:
                scatters[0].finish()
                scatters[2].advance()
        r.done("gh")
        for k in range(nc):
            edge.arrived(3, k)
        r.done("w2")
        keep.wait()
        give.wait()
        edge.drain()
        for scatter in scatters[1:]:
            scatter.finish()

    return call(
        body,
        dict(
            n=(kept["n3"], LD),
            wc=(kept["wc"], LD),
            e=(kept["e1"], LD),
            h=(kept["h2"], LD),
            og=(kept["ogh"], LD),
            taps=(taps, VM),
            lengths=(lengths, SM),
            g2=(gains[2], VM),
            g3=(gains[3], VM),
            g4=(gains[4], VM),
            sr=(kept["r1"], HB),
            ra=(kept["ra"], HB),
        ),
        dict(
            fo=((2, Q, D), BF16, HB),
            gh=((nc, Q, D), F32, ST),
            w2=((S, D), BF16, ST),
            dw=(four + (3 * C,), BF16, ST),
            de=(four + (F,), BF16, ST),
            outr=((shard, F), F32, VM),
            oute=((shard, half), F32, VM),
            dk=((KERNEL, C), F32, VM),
            dg2=((8, D), F32, VM),
            dg3=((8, D), F32, VM),
            dg4=((8, D), F32, VM),
        ),
        scratch,
        cid,
    )


def last_kernel(dims, cid, kept, middle, lengths, gains, shard):
    nc, Q, D, S, F, H, C = dims.nc, dims.Q, dims.D, dims.S, dims.F, dims.H, dims.C
    heads = H // HEAD_DIM
    edge = Edge(dims, 2)
    four = (dims.na, dims.nb, shard)
    scatters = [Scatter("0", dims, shard, 0, 3 * C), Scatter("1", dims, shard, F // 2, F // 2, 0)]
    scatters += [Scatter(str(2 + j), dims, shard, j * 2 * H, 2 * H) for j in range(2)]
    triple = (heads, S, HEAD_DIM)
    scratch = edge.scratch() | dict(
        da=VM(triple, BF16),
        kt=VM((heads, HEAD_DIM, S), BF16),
        delta=VM((heads, 1, S), F32),
        gk=VM(triple, F32),
        gv=VM(triple, F32),
        dqt=VM((H, S), F32),
        pack=VM((S, 3 * H), BF16),
        dw=VM(four + (4 * H,), BF16),
        w1=VM((S, D), BF16),
        column=VM((S, 1), F32),
        psem=SEMS,
        gsem=SEMS,
    )
    for scatter in scatters:
        scratch |= scatter.scratch()

    def body(r):
        spot = Spot(dims)
        greet(spot.tensor_peers() + spot.data_peers())
        edge.bind(r, spot)
        scatters[0].bind(r, spot, r.cw, r.sc).start()
        scatters[1].bind(r, spot, r.dei, r.oute).start()
        for scatter in scatters[2:]:
            scatter.bind(r, spot, r.dw, r.sa)
        live_column(r, S, True)
        for sums in (r.dg1, r.gk, r.gv):
            sums[...] = jnp.zeros_like(sums)

        ghc = pltpu.make_async_copy(r.ghi, r.gh, r.gsem)
        ghc.start()

        r.need("w", "wa", "oh", "k")
        mixed = jnp.dot(r.w[...], r.wa[:, pl.ds(3 * H, H)], preferred_element_type=F32).astype(BF16)
        inner = (mixed.astype(F32) * r.oh[...].astype(F32)).T
        for j in range(heads):
            some = slice(j * HEAD_DIM, (j + 1) * HEAD_DIM)
            r.da[j] = mixed[:, some]
            r.delta[j] = jnp.sum(inner[some], axis=0, keepdims=True)
            r.kt[j] = r.k[j].astype(F32).T.astype(BF16)
        blocks = S // min(2 * QUERIES, S)
        size = S // blocks
        r.need("q", "v", "lse")

        def one(i):
            head = lax.div(i, blocks)
            at = pl.ds(pl.multiple_of(lax.rem(i, blocks) * size, size), size)
            query, outer = r.q[head, at, :], r.da[head, at, :]
            scores = lax.dot_general(
                r.k[head], query, (((1,), (1,)), ((), ())), preferred_element_type=F32
            )
            prob = jnp.exp(scores + (r.column[...] - r.lse[head, :, at]))
            r.gv[head] += jnp.dot(prob.astype(BF16), outer, preferred_element_type=F32)
            back = lax.dot_general(
                r.v[head], outer, (((1,), (1,)), ((), ())), preferred_element_type=F32
            )
            slope = (prob * (back - r.delta[head, :, at])).astype(BF16)
            r.gk[head] += jnp.dot(slope, query, preferred_element_type=F32)
            r.dqt[pl.ds(pl.multiple_of(head * HEAD_DIM, HEAD_DIM), HEAD_DIM), at] = (
                jnp.dot(r.kt[head], slope, preferred_element_type=F32) * HEAD_DIM**-0.5
            )

        loop(heads * blocks, one)
        r.pack[:, pl.ds(0, H)] = r.dqt[...].T.astype(BF16)
        for j, source in ((1, r.gk), (2, r.gv)):
            r.pack[:, pl.ds(j * H, H)] = jnp.concatenate(
                [source[i] for i in range(heads)], axis=1
            ).astype(BF16)
        for k in range(nc):
            part_product(edge, 0, k, r.pack, r.wa, 0, dims)
            if k > 0:
                edge.cross(0, k - 1)
        edge.cross(0, nc - 1)
        r.need("n2")
        weight_part(r.dw, 0, r.n2, r.pack, dims)
        weight_part(r.dw, 3 * H, r.w, r.oh, dims)
        for scatter in scatters[2:]:
            scatter.start()
        scatters[0].advance()

        ghc.wait()
        r.need("h1", "rt", "slope", "e")
        for k in range(nc):
            edge.settle(0, k, backward_rows(r.h1, 0.5, r.g1, r.gh, r.dg1, spot), r.w1)
            edge.arrived(0, k)
            back_products(dims, k, r.w1, r.rt, r.slope, r.slope)
            part_product(edge, 1, k, r.slope, r.e, 0, dims)
            if k > 0:
                edge.cross(1, k - 1, send=False)
            if k == 0:
                scatters[1].advance()
            elif k == 1:
                scatters[0].advance()
            elif k == 2:
                scatters[1].advance()
            elif k == 3:
                scatters[2].advance()
                scatters[0].finish()
        r.done("gh")
        r.need("n1", "u")
        weight_part(r.dr, 0, r.w1, r.u, dims)
        r.done("dr")
        edge.cross(1, nc - 1, send=False)
        part = pltpu.make_async_copy(r.e_sum, r.part, r.psem)
        part.start()
        weight_part(r.de, 0, r.n1, r.slope, dims)
        r.done("de")
        scatters[1].finish()
        scatters[3].advance()
        scatters[2].advance()
        part.wait()
        edge.drain()
        scatters[3].advance()
        scatters[2].finish()
        scatters[3].finish()

    return call(
        body,
        dict(
            w=(middle["w2"], LD),
            wa=(kept["wa"], LD),
            oh=(kept["oh"], LD),
            k=(kept["k"], LD),
            q=(kept["q"], LD),
            v=(kept["v"], LD),
            lse=(kept["lse"], LD),
            n2=(kept["n2"], LD),
            ghi=(middle["gh"], HB),
            h1=(kept["h1"], LD),
            rt=(kept["rt"], LD),
            slope=(kept["slope"], LD),
            e=(kept["e"], LD),
            n1=(kept["n1"], LD),
            u=(kept["u"], LD),
            lengths=(lengths, SM),
            g1=(gains[1], VM),
            cw=(middle["dw"], HB),
            dei=(middle["de"], HB),
        ),
        dict(
            part=((nc, Q, D), BF16, HB),
            gh=((nc, Q, D), F32, ST),
            de=(four + (F,), BF16, ST),
            dr=(four + (F,), BF16, ST),
            sc=((shard, 3 * C), F32, VM),
            sa=((shard, 4 * H), F32, VM),
            oute=((shard, F // 2), F32, VM),
            dg1=((8, D), F32, VM),
        ),
        scratch,
        cid,
    )


def direction_of(mean, square, master, rates, decay):
    return mean * rates[4] / (jnp.sqrt(square * rates[5]) + ADAM_EPS) + decay * master


def moments_of(grad, mean, square, rates):
    return (
        rates[0] * mean + (1.0 - rates[0]) * grad,
        rates[1] * square + (1.0 - rates[1]) * grad * grad,
    )


def tile_rows(shape):
    rows, columns = shape[-2:]
    step = min(rows, max(8, 16384 // max(columns, 128)))
    return step if rows % step == 0 and step % 8 == 0 else rows


def eighths(tile):
    rows, columns = tile.shape
    return tile.reshape(rows // 8, 8, columns).sum(axis=0) if rows % 8 == 0 else tile


def flip(result, source, dims):
    def part(j):
        cs = rows_of(j, 128)
        result[cs, :] = source[:, cs].T

    loop(source.shape[1] // 128, part)


PLACES = (0, 1, 2, 3, 4, 6, 5, 7)


def piece_rows(shapes):
    rows, total = {}, 0
    for i in PLACES:
        rows[i] = total
        total += shapes[i][0]
    return rows


class Relay:
    def __init__(self, tag, count, shape):
        self.tag, self.count = tag, count
        k = max(count - 1, 1)
        self.specs = dict(slots=VM((count,) + shape, F32), s=SEMS((k,)), r=SEMS((k,)))

    def scratch(self):
        return tagged("r", self.tag, self.specs)

    def start(self, refs, place, peers, value):
        self.r = bound(refs, "r", self.tag, self.specs)
        r = self.r
        r.slots[place] = value
        self.copies = []
        for j, peer in enumerate(peers):
            copy = remote(r.slots.at[place], r.slots.at[place], r.s.at[j], r.r.at[j], peer)
            copy.start()
            self.copies.append(copy)

    def finish(self):
        for copy in self.copies:
            copy.wait()
        total = self.r.slots[0]
        for i in range(1, self.count):
            total = total + self.r.slots[i]
        return total


def gradient_kernel(
    dims, cid, rates, entries, scatter, sums, gain_parts, kernel_part, part, grad, hidden, gain
):
    D, F, H, C, Q, ny = dims.D, dims.F, dims.H, dims.C, dims.Q, dims.ny
    shard = scatter[0].shape[2]
    pieces = 4
    width = F // pieces
    jobs = [
        Scatter(str(pieces * i + j), dims, shard, j * width, width)
        for i in range(2)
        for j in range(pieces)
    ]
    count_t, count_d = dims.ny * 2, dims.na * dims.nb
    gains_relays = [
        Relay("0", 2, (8, D)), Relay("1", ny, (8, D)),
        Relay("2", dims.na, (8, D)), Relay("3", dims.nb, (8, D)),
    ]
    taps_relays = [Relay("4", dims.na, (KERNEL, C)), Relay("5", dims.nb, (KERNEL, C))]
    norm_relays = [Relay("6", count_t, (24, 128)), Relay("7", count_d, (24, 128))]
    relays = gains_relays + taps_relays + norm_relays
    count = len(entries)
    m = max(ny - 1, 1)
    shapes = [entry[1].shape for entry in entries]
    scratch = dict(
        nrm=VM((24, 128), F32),
        gains=VM((8, D), F32),
        dg0=VM((8, D), F32),
        shr0=VM((shard, F), F32),
        shr1=VM((shard, F), F32),
        mix=VM((shard, H), F32),
        mer=VM((shard, C), F32),
        far=VM((m, 2, Q, D), BF16),
        sum=VM((dims.nc, Q, D), BF16),
        gh=VM((2, Q, D), F32),
        h=VM((2, Q, D), BF16),
        both=VM((2, Q, D), BF16),
        gsem=SEMS((10,)),
        psem=SEMS((4,)),
        fsem=SEMS((m, 2)),
        bsem=SEMS((2,)),
        isem=SEMS((count, 3)),
    )
    ins = dict(
        rates=(rates, SM),
        kp=(kernel_part, VM),
        sp=(part, HB),
        ghp=(grad, HB),
        hp=(hidden, HB),
        g=(gain, VM),
        src0=(scatter[0], HB),
        src1=(scatter[1], HB),
    )
    outs = dict(norms=((24, 128), F32, VM), gin=((2, Q, D), BF16, HB))
    for i, (params, mean, square, _) in enumerate(entries):
        tag = str(i)
        held = shapes[i] if i < 6 else params.shape
        ins |= {"p" + tag: (params, HB), "m" + tag: (mean, HB), "v" + tag: (square, HB)}
        scratch |= {"w" + tag: VM(held, F32), "n" + tag: VM(shapes[i], F32)}
        scratch |= {"q" + tag: VM(shapes[i], F32)}
        outs |= {"g" + tag: (shapes[i], F32, VM)}
    for i, array in enumerate(gain_parts):
        ins |= {"d" + str(i): (array, VM)}
    for i, array in enumerate(sums):
        ins |= {"s" + str(i): (array, HB)}
    for item in relays + jobs:
        scratch |= item.scratch()

    def body(r):
        spot = Spot(dims)
        everyone = [(spot.d, lax.rem(spot.t + j, count_t)) for j in range(1, count_t)]
        items = [(lax.rem(spot.d + j, count_d), spot.t) for j in range(1, count_d)]
        greet(everyone + items)
        get = lambda name, i: getattr(r, name + str(i))
        for i, job in enumerate(jobs):
            job.bind(r, spot, r.src1 if i >= pieces else r.src0, r.g0.at[0] if i >= pieces else r.shr0)
            job.start()
        mine = pl.ds(spot.y * 2, 2)
        totals = [
            pltpu.make_async_copy(r.sp, r.sum, r.psem.at[0]),
            pltpu.make_async_copy(r.ghp.at[mine], r.gh, r.psem.at[1]),
            pltpu.make_async_copy(r.hp.at[mine], r.h, r.psem.at[2]),
        ]
        for copy in totals:
            copy.start()
        grads = [
            pltpu.make_async_copy(r.s0, r.g0.at[1, :, pl.ds(0, F // 2)], r.gsem.at[0]),
            pltpu.make_async_copy(r.s4, r.g0.at[1, :, pl.ds(F // 2, F // 2)], r.gsem.at[9]),
            pltpu.make_async_copy(r.s1, r.shr1, r.gsem.at[1]),
            pltpu.make_async_copy(r.s2.at[:, pl.ds(3 * H, H)], r.mix, r.gsem.at[2]),
            pltpu.make_async_copy(r.s3.at[:, pl.ds(2 * C, C)], r.mer, r.gsem.at[3]),
        ]
        grads += [
            pltpu.make_async_copy(r.s2.at[:, pl.ds(k * H, H)], r.g2.at[k], r.gsem.at[4 + k])
            for k in range(3)
        ]
        grads += [
            pltpu.make_async_copy(r.s3.at[:, pl.ds(k * C, C)], r.g4.at[k], r.gsem.at[7 + k])
            for k in range(2)
        ]
        for copy in grads:
            copy.start()
        loads = []
        for i in range(count):
            master = get("p", i).at[0] if i < 6 else get("p", i)
            triple = [
                pltpu.make_async_copy(master, get("w", i), r.isem.at[i, 0]),
                pltpu.make_async_copy(get("m", i), get("n", i), r.isem.at[i, 1]),
                pltpu.make_async_copy(get("v", i), get("q", i), r.isem.at[i, 2]),
            ]
            for copy in triple:
                copy.start()
            loads.append(triple)

        totals[0].wait()
        crossing = []
        for j in range(1, ny):
            other = lax.rem(spot.y + j, ny) * 2
            copy = remote(
                r.sum.at[pl.ds(other, 2)], r.far.at[j - 1], r.fsem.at[j - 1, 0], r.fsem.at[j - 1, 1],
                spot.across(j),
            )
            copy.start()
            crossing.append(copy)

        r.nrm[...] = jnp.zeros_like(r.nrm)
        row = lax.broadcasted_iota(jnp.int32, (24, 128), 0)
        lane = lax.broadcasted_iota(jnp.int32, (24, 128), 1)
        first_piece = piece_rows(shapes)
        loaded = set()

        def load(i):
            if i not in loaded:
                loaded.add(i)
                for copy in loads[i]:
                    copy.wait()

        def small_norm(i, weight):
            load(i)
            master = get("w", i)[:, 0, :]
            mean, square = moments_of(get("g", i)[0], get("n", i)[0], get("q", i)[0], r.rates)
            move = direction_of(mean, square, master, r.rates, entries[i][3])
            for column, values in enumerate((master, move)):
                value = jnp.sum(values * values, axis=1, keepdims=True) * weight
                if i == 6:
                    value = jnp.sum(value, axis=0, keepdims=True)
                at = first_piece[i]
                r.nrm[at : at + value.shape[0], column : column + 1] = value

        def norm(i, p):
            load(i)
            step = tile_rows(shapes[i])
            zero = jnp.zeros((8, shapes[i][-1]), F32)

            def tile(j, carry):
                rs = pl.ds(pl.multiple_of(j * step, step), step)
                master = get("w", i)[p, rs, :]
                mean, square = moments_of(
                    get("g", i)[p, rs, :], get("n", i)[p, rs, :], get("q", i)[p, rs, :], r.rates
                )
                move = direction_of(mean, square, master, r.rates, entries[i][3])
                return (carry[0] + eighths(master * master), carry[1] + eighths(move * move))

            sums_of = lax.fori_loop(0, shapes[i][-2] // step, tile, (zero, zero))
            here = row == first_piece[i] + p
            for column, total in enumerate(sums_of):
                value = jnp.sum(jnp.sum(total, axis=0, keepdims=True), axis=1, keepdims=True)
                r.nrm[...] += jnp.where(jnp.logical_and(here, lane == column), value, 0.0)

        slow = [spot.slow(j) for j in range(1, dims.na)]
        fast = [spot.fast(j) for j in range(1, dims.nb)]
        taps_relays[0].start(r, spot.a, slow, r.kp[...])
        for copy in grads:
            copy.wait()
        flip(r.g3.at[0], r.mix, dims)
        flip(r.g5.at[0], r.mer, dims)
        jobs[0].advance()

        for copy in totals[1:]:
            copy.wait()
        for p in range(3):
            norm(2, p)
        for copy in crossing:
            copy.wait_recv()
        jobs[1].advance()
        r.dg0[...] = jnp.zeros_like(r.dg0)
        for i in range(2):

            def rows(j, i=i):
                rs = rows_of(j)
                total = r.sum[spot.y * 2 + i, rs, :].astype(F32)
                for other in range(ny - 1):
                    total = total + r.far[other, i, rs, :].astype(F32)
                xhat, inverse = unit(r.h[i, rs, :].astype(F32))
                r.dg0[...] += fold(total * xhat)
                back = r.gh[i, rs, :] + unit_back(total, xhat, inverse, r.g[...])
                r.both[i, rs, :] = back.astype(BF16)

            loop(Q // STEP, rows, 2)
        keep = pltpu.make_async_copy(r.both.at[spot.c], r.gin.at[spot.c], r.psem.at[3])
        keep.start()
        give = remote(
            r.both.at[1 - spot.c], r.gin.at[spot.c], r.bsem.at[0], r.bsem.at[1], spot.sibling()
        )
        give.start()

        r.gains[...] = jnp.zeros_like(r.gains)
        for k, ref in enumerate((r.dg0, r.d0, r.d1, r.d2, r.d3)):
            r.gains[k : k + 1, :] = jnp.sum(ref[...], axis=0, keepdims=True)
        gains_relays[0].start(r, spot.c, [spot.sibling()], r.gains[...])
        jobs[0].advance()
        jobs[2].advance()
        total = gains_relays[0].finish()
        gains_relays[1].start(r, spot.y, [spot.across(j) for j in range(1, ny)], total)
        norm(3, 0)
        for p in range(2):
            norm(4, p)
        norm(5, 0)
        jobs[1].advance()
        total = gains_relays[1].finish()
        gains_relays[2].start(r, spot.a, slow, total)
        total = taps_relays[0].finish()
        taps_relays[1].start(r, spot.b, fast, total)
        jobs[3].advance()
        flip(r.g1.at[1], r.shr1, dims)
        norm(1, 1)
        jobs[2].advance()
        total = gains_relays[2].finish()
        gains_relays[3].start(r, spot.b, fast, total)
        norm(0, 1)
        jobs[0].finish()
        jobs[4].advance()
        jobs[3].advance()
        r.g6[0] = taps_relays[1].finish()
        owner = jnp.where(spot.d == 0, 1.0, 0.0)
        small_norm(6, owner)
        jobs[1].finish()
        jobs[5].advance()
        jobs[4].advance()
        r.gains[...] = gains_relays[3].finish()
        owner = jnp.where(spot.t == 0, owner, 0.0)
        r.g7[0] = r.gains[0:5, :]
        small_norm(7, owner)
        jobs[2].finish()
        jobs[6].advance()
        jobs[5].advance()
        jobs[3].finish()
        flip(r.g1.at[0], r.shr0, dims)
        norm(1, 0)
        jobs[7].advance()
        jobs[6].advance()
        jobs[4].finish()
        jobs[5].finish()
        jobs[7].advance()
        jobs[6].finish()
        jobs[7].finish()
        norm(0, 0)
        norm_relays[0].start(r, spot.t, everyone, r.nrm[...])
        total = norm_relays[0].finish()
        norm_relays[1].start(r, spot.d, items, total)
        r.norms[...] = norm_relays[1].finish()
        keep.wait()
        give.wait()
        for copy in crossing:
            copy.wait_send()

    return call(body, ins, outs, scratch, cid)


def update_kernel(dims, rates, norms, entries, grads, frames, frames_grad):
    count = len(entries)
    shapes = [entry[1].shape for entry in entries]
    like = (dims.L, dims.D)
    ins = dict(
        rates=(rates, SM),
        norms=(norms, VM),
        fo=(frames.reshape(like), HB),
        fg=(frames_grad.reshape(like), HB),
    )
    outs = dict(trust=((2, 17), F32, VM), frames=(like, BF16, HB), gin=(like, BF16, HB))
    scratch = dict(isem=SEMS((count, 4)), osem=SEMS((count, 5)), fsem=SEMS((4,)), rows=VM((2,) + like, BF16))
    for i, (params, mean, square, _) in enumerate(entries):
        tag = str(i)
        shape = shapes[i]
        pair = params.shape
        ins |= {"p" + tag: (params, HB), "m" + tag: (mean, HB), "v" + tag: (square, HB)}
        ins |= {"g" + tag: (grads[i], HB)}
        scratch |= {"w" + tag: VM(pair, F32), "n" + tag: VM(shape, F32)}
        scratch |= {"q" + tag: VM(shape, F32), "h" + tag: VM(shape, F32)}
        scratch |= {"b" + tag: VM(pair, BF16)}
        outs |= {"og" + tag: (shape, F32, HB), "om" + tag: (shape, F32, HB)}
        outs |= {"ov" + tag: (shape, F32, HB), "ow" + tag: (pair, F32, HB)}
        outs |= {"ob" + tag: (pair, BF16, HB)}
    order = [2, 4, 3, 5, 7, 6, 1, 0]

    def body(r):
        get = lambda name, i: getattr(r, name + str(i))
        loads, stores = {}, []
        for i in order:
            moves = (("g", "h"), ("m", "n"), ("v", "q"), ("p", "w"))
            loads[i] = [
                pltpu.make_async_copy(get(source, i), get(target, i), r.isem.at[i, k])
                for k, (source, target) in enumerate(moves)
            ]
            for copy in loads[i]:
                copy.start()
        staged = []
        for k, source in enumerate((r.fo, r.fg)):
            staged.append(pltpu.make_async_copy(source, r.rows.at[k], r.fsem.at[k]))
            staged[k].start()
        norms = jnp.sqrt(r.norms[...])
        r.trust[...] = norms.T[:2, :17]
        ratio = r.rates[3] * norms[:, 0:1] / norms[:, 1:2]

        def send(i, name, target, k):
            copy = pltpu.make_async_copy(get(name, i), get(target, i), r.osem.at[i, k])
            copy.start()
            stores.append(copy)

        def update(i, grad, mean, square, master, average, scale):
            mean, square = moments_of(grad, mean, square, r.rates)
            move = direction_of(mean, square, master, r.rates, entries[i][3])
            master = master - scale * move
            average = r.rates[2] * average + (1.0 - r.rates[2]) * master
            return mean, square, master, average

        for i in order:
            for copy in loads[i]:
                copy.wait()
            send(i, "h", "og", 0)
            offset = piece_rows(shapes)[i]
            if i > 5:
                weights = get("w", i)
                scale = ratio[offset : offset + (1 if i == 6 else shapes[i][1]), :]
                mean, square, master, average = update(
                    i, get("h", i)[0], get("n", i)[0], get("q", i)[0], weights[:, 0, :],
                    weights[:, 1, :], scale,
                )
                get("n", i)[0] = mean
                get("q", i)[0] = square
                for slot, values in enumerate((master, average)):
                    weights[:, slot, :] = values
                get("b", i)[...] = weights[...].astype(BF16)
            else:
                step = tile_rows(shapes[i])
                for p in range(shapes[i][0]):
                    scale = ratio[offset + p : offset + p + 1, :]

                    def tile(j, p=p, i=i, step=step, scale=scale):
                        rs = pl.ds(pl.multiple_of(j * step, step), step)
                        mean, square, master, average = update(
                            i, get("h", i)[p, rs, :], get("n", i)[p, rs, :], get("q", i)[p, rs, :],
                            get("w", i)[0, p, rs, :], get("w", i)[1, p, rs, :], scale,
                        )
                        get("n", i)[p, rs, :] = mean
                        get("q", i)[p, rs, :] = square
                        get("w", i)[0, p, rs, :] = master
                        get("w", i)[1, p, rs, :] = average
                        get("b", i)[0, p, rs, :] = master.astype(BF16)
                        get("b", i)[1, p, rs, :] = average.astype(BF16)

                    loop(shapes[i][-2] // step, tile)
            send(i, "n", "om", 1)
            send(i, "q", "ov", 2)
            send(i, "w", "ow", 3)
            send(i, "b", "ob", 4)
            if i == order[0]:
                for k, target in enumerate((r.frames, r.gin)):
                    staged[k].wait()
                    copy = pltpu.make_async_copy(r.rows.at[k], target, r.fsem.at[2 + k])
                    copy.start()
                    stores.append(copy)
        for copy in stores:
            copy.wait()

    return call(body, ins, outs, scratch, None)


def shards(
    dims,
    frames_input,
    out_grad,
    lengths,
    step_count,
    rates,
    expand_params,
    expand_first,
    expand_second,
    shrink_params,
    shrink_first,
    shrink_second,
    project_params,
    project_first,
    project_second,
    mixing_params,
    mixing_first,
    mixing_second,
    gating_params,
    gating_first,
    gating_second,
    kernel_params,
    kernel_first,
    kernel_second,
    merging_params,
    merging_first,
    merging_second,
    gains_params,
    gains_first,
    gains_second,
):
    local_rows, width = frames_input.shape
    shard_rows = expand_params.shape[2]
    dims = SimpleNamespace(
        L=local_rows,
        D=width,
        S=local_rows * dims.ny * 2,
        F=expand_params.shape[3],
        H=project_params.shape[3],
        C=gating_params.shape[3],
        Q=local_rows // 2,
        nc=dims.ny * 2,
        **vars(dims),
    )
    gain = [gains_params[0, i : i + 1] for i in range(5)]
    taps = jnp.swapaxes(kernel_params, 0, 1)
    front = front_kernel(
        dims, 1, frames_input, out_grad, lengths, gain, expand_params, shrink_params,
        project_params, mixing_params, gating_params, merging_params,
    )
    middle = middle_kernel(dims, 2, front, lengths, taps, gain, shard_rows)
    last = last_kernel(dims, 4, front, middle, lengths, gain, shard_rows)

    steps_done = step_count[0].astype(F32)
    scalars = jnp.concatenate(
        [rates, 1.0 / (1.0 - rates[:2] ** steps_done), jnp.zeros((2,), F32)]
    )
    one = lambda params, first, second: (params[:, None], first[None], second[None], DECAY_RATE)
    entries = [
        (expand_params, expand_first, expand_second, DECAY_RATE),
        (shrink_params, shrink_first, shrink_second, DECAY_RATE),
        (project_params, project_first, project_second, DECAY_RATE),
        one(mixing_params, mixing_first, mixing_second),
        (gating_params, gating_first, gating_second, DECAY_RATE),
        one(merging_params, merging_first, merging_second),
        (taps, kernel_first[None], kernel_second[None], DECAY_RATE),
        (jnp.swapaxes(gains_params, 0, 1), gains_first[None], gains_second[None], 0.0),
    ]
    summed = gradient_kernel(
        dims, 3, scalars, entries, [last["dr"], last["de"]],
        [middle["oute"], middle["outr"], last["sa"], last["sc"], last["oute"]],
        [last["dg1"], middle["dg2"], middle["dg3"], middle["dg4"]], middle["dk"],
        last["part"], last["gh"], front["xh"], gain[0],
    )
    updated = update_kernel(
        dims, scalars, summed["norms"], entries, [summed["g" + str(i)] for i in range(8)],
        middle["fo"], summed["gin"],
    )
    results = []
    firsts = (
        expand_first, shrink_first, project_first, mixing_first, gating_first, kernel_first,
        merging_first, gains_first,
    )
    for place in range(8):
        entry = PLACES.index(place)
        like = firsts[place].shape
        tag = str(entry)
        results += [updated[name + tag].reshape(like) for name in ("og", "om", "ov")]
        for name in ("ow", "ob"):
            pair = updated[name + tag]
            results.append(jnp.swapaxes(pair, 0, 1) if entry > 5 else pair.reshape((2,) + like))
    return (updated["frames"], updated["gin"], *results, updated["trust"].T)


def solution(mesh):
    slow = math.gcd(mesh.shape["dp"], 4)
    dims = SimpleNamespace(na=slow, nb=mesh.shape["dp"] // slow, ny=mesh.shape["tensor"] // 2)
    return jax.shard_map(
        functools.partial(shards, dims),
        mesh=mesh,
        in_specs=(
            P(("dp", "tensor"), None),
            P(("dp", "tensor"), None),
            P("dp"),
            P(),
            P(),
            P(None, None, "dp", "tensor"),
            P(None, "dp", "tensor"),
            P(None, "dp", "tensor"),
            P(None, None, "tensor", "dp"),
            P(None, "tensor", "dp"),
            P(None, "tensor", "dp"),
            P(None, None, "dp", "tensor"),
            P(None, "dp", "tensor"),
            P(None, "dp", "tensor"),
            P(None, "tensor", "dp"),
            P("tensor", "dp"),
            P("tensor", "dp"),
            P(None, None, "dp", "tensor"),
            P(None, "dp", "tensor"),
            P(None, "dp", "tensor"),
            P(None, None, "tensor"),
            P(None, "tensor"),
            P(None, "tensor"),
            P(None, "tensor", "dp"),
            P("tensor", "dp"),
            P("tensor", "dp"),
            P(),
            P(),
            P(),
        ),
        out_specs=(
            P(("dp", "tensor"), None),
            P(("dp", "tensor"), None),
            P(None, "dp", "tensor"),
            P(None, "dp", "tensor"),
            P(None, "dp", "tensor"),
            P(None, None, "dp", "tensor"),
            P(None, None, "dp", "tensor"),
            P(None, "tensor", "dp"),
            P(None, "tensor", "dp"),
            P(None, "tensor", "dp"),
            P(None, None, "tensor", "dp"),
            P(None, None, "tensor", "dp"),
            P(None, "dp", "tensor"),
            P(None, "dp", "tensor"),
            P(None, "dp", "tensor"),
            P(None, None, "dp", "tensor"),
            P(None, None, "dp", "tensor"),
            P("tensor", "dp"),
            P("tensor", "dp"),
            P("tensor", "dp"),
            P(None, "tensor", "dp"),
            P(None, "tensor", "dp"),
            P(None, "dp", "tensor"),
            P(None, "dp", "tensor"),
            P(None, "dp", "tensor"),
            P(None, None, "dp", "tensor"),
            P(None, None, "dp", "tensor"),
            P(None, "tensor"),
            P(None, "tensor"),
            P(None, "tensor"),
            P(None, None, "tensor"),
            P(None, None, "tensor"),
            P("tensor", "dp"),
            P("tensor", "dp"),
            P("tensor", "dp"),
            P(None, "tensor", "dp"),
            P(None, "tensor", "dp"),
            P(),
            P(),
            P(),
            P(),
            P(),
            P(),
        ),
        check_vma=False,
    )
```

```python
import functools
import math
from types import SimpleNamespace

import jax
import jax.numpy as jnp
from jax import lax
from jax.experimental import pallas as pl
from jax.experimental.pallas import tpu as pltpu
from jax.sharding import PartitionSpec as P

HEAD_DIM = 64
KERNEL = 31

EPSILON = 1e-05
ADAM_EPS = 1e-06
DECAY_RATE = 0.01
MASKED = -1000000000.0

F32 = jnp.float32
BF16 = jnp.bfloat16
MESH = pl.DeviceIdType.MESH
STEP = 16
TILE = 256
GRANT = 60 * 1024 * 1024


class Spot:
    def __init__(self, dims):
        self.dims = dims
        self.d = lax.axis_index("dp")
        self.t = lax.axis_index("tensor")
        self.y = lax.div(self.t, 2)
        self.c = lax.rem(self.t, 2)
        self.a = lax.div(self.d, dims.nb)
        self.b = lax.rem(self.d, dims.nb)

    def sibling(self):
        return (self.d, self.y * 2 + 1 - self.c)

    def across(self, j):
        return (self.d, lax.rem(self.y + j, self.dims.ny) * 2 + self.c)

    def slow(self, j):
        return (lax.rem(self.a + j, self.dims.na) * self.dims.nb + self.b, self.t)

    def fast(self, j):
        return (self.a * self.dims.nb + lax.rem(self.b + j, self.dims.nb), self.t)

    def tensor_peers(self):
        return [self.sibling()] + [self.across(j) for j in range(1, self.dims.ny)]

    def data_peers(self):
        return [self.slow(j) for j in range(1, self.dims.na)] + [
            self.fast(j) for j in range(1, self.dims.nb)
        ]


def greet(peers):
    barrier = pltpu.get_barrier_semaphore()
    for peer in peers:
        pl.semaphore_signal(barrier, 1, device_id=peer, device_id_type=MESH)
    pl.semaphore_wait(barrier, len(peers))


def remote(source, target, send, recv, peer):
    return pltpu.make_async_remote_copy(
        src_ref=source,
        dst_ref=target,
        send_sem=send,
        recv_sem=recv,
        device_id=peer,
        device_id_type=MESH,
    )


def loop(count, body, unroll=1):
    def step(i, carry):
        body(i)
        return carry

    lax.fori_loop(0, count, step, 0, unroll=unroll)


def rows_of(i, step=STEP):
    return pl.ds(pl.multiple_of(i * step, step), step)


class Refs(SimpleNamespace):
    def need(self, *names):
        for name in names:
            if name in self.pending:
                self.pending.pop(name).wait()

    def done(self, *names):
        for name in names:
            copy = self.unsent.pop(name)
            copy.start()
            self.leaving.append(copy)

    def close(self):
        self.need(*list(self.pending))
        self.done(*list(self.unsent))
        for copy in self.leaving:
            copy.wait()


def call(body, ins, outs, scratch, cid):
    in_names, out_names, scratch_names = list(ins), list(outs), list(scratch)
    loads = [name for name in in_names if ins[name][1] in (LD, LD0)]
    stores = [name for name in out_names if outs[name][2] is ST]
    whole = {name: ins[name][1] is LD for name in loads}
    copies = [
        VM(ins[name][0].shape[0 if whole[name] else 1 :], ins[name][0].dtype) for name in loads
    ]
    copies += [VM(outs[name][0], outs[name][1]) for name in stores]
    sems = [SEMS((max(len(copies), 1),))]

    def place(space):
        return pl.BlockSpec(memory_space=HB if space in (LD, LD0, ST) else space)

    def kernel(*refs):
        names = in_names + out_names + scratch_names
        given = dict(zip(names, refs))
        held = refs[len(names) : -1]
        r = Refs(**given, pending={}, unsent={}, leaving=[])
        for i, name in enumerate(loads):
            source = given[name] if whole[name] else given[name].at[0]
            r.pending[name] = pltpu.make_async_copy(source, held[i], refs[-1].at[i])
            setattr(r, name, held[i])
        for i, name in enumerate(stores, len(loads)):
            r.unsent[name] = pltpu.make_async_copy(held[i], given[name], refs[-1].at[i])
            setattr(r, name, held[i])
        for copy in r.pending.values():
            copy.start()
        body(r)
        r.close()

    results = pl.pallas_call(
        kernel,
        out_shape=[jax.ShapeDtypeStruct(shape, kind) for shape, kind, _ in outs.values()],
        in_specs=[place(space) for _, space in ins.values()],
        out_specs=[place(space) for _, _, space in outs.values()],
        scratch_shapes=list(scratch.values()) + copies + sems,
        compiler_params=pltpu.CompilerParams(
            collective_id=cid, has_side_effects=cid is not None, vmem_limit_bytes=GRANT
        ),
    )(*[array for array, _ in ins.values()])
    return dict(zip(out_names, results))


LD, LD0, ST = object(), object(), object()
VM = pltpu.VMEM
HB = pl.ANY
SM = pltpu.SMEM
SEMS = pltpu.SemaphoreType.DMA


def tagged(prefix, tag, specs):
    return {prefix + name + tag: spec for name, spec in specs.items()}


def bound(refs, prefix, tag, specs):
    return SimpleNamespace(**{name: getattr(refs, prefix + name + tag) for name in specs})


class Gather:
    def __init__(self, tag, dims):
        self.tag, self.dims = tag, dims
        na, nb = dims.na, dims.nb
        m, k = max(nb - 1, 1), max(na - 1, 1)
        self.specs = dict(
            loc=SEMS,
            xs=SEMS((m,)),
            xr=SEMS((m,)),
            us=SEMS((k,)),
            ur=SEMS((k,)),
            ds=SEMS((k,)),
            dr=SEMS((k,)),
            fs=SEMS((2, k, m)),
            fr=SEMS((2, k, m)),
        )
        self.stage = 0

    def scratch(self):
        return tagged("g", self.tag, self.specs)

    def bind(self, refs, spot, source, whole, columns=None):
        self.sem = bound(refs, "g", self.tag, self.specs)
        self.spot, self.source, self.whole, self.columns = spot, source, whole, columns
        return self

    def rows(self, d):
        shard = self.source.shape[0]
        rows = pl.ds(pl.multiple_of(d * shard, shard), shard)
        return self.whole.at[rows] if self.columns is None else self.whole.at[rows, self.columns]

    def block(self, a):
        return self.rows(a * self.dims.nb + self.spot.b)

    def hop(self, way, s):
        spot, sem = self.spot, self.sem
        step = 1 if way == 0 else -1
        target = self.block(spot.a - step * (s - 1))
        source = self.source if s == 1 else target
        send, recv = (sem.us, sem.ur) if way == 0 else (sem.ds, sem.dr)
        peer = ((spot.a + step) * self.dims.nb + spot.b, spot.t)
        return remote(source, target, send.at[s - 1], recv.at[s - 1], peer)

    def sends(self, way, s):
        spot, na = self.spot, self.dims.na
        if way == 0:
            return jnp.logical_and(spot.a - (s - 1) >= 0, spot.a + 1 < na)
        return jnp.logical_and(spot.a + (s - 1) < na, spot.a - 1 >= 0)

    def has(self, way, s):
        return self.spot.a - s >= 0 if way == 0 else self.spot.a + s < self.dims.na

    def hand(self, way, s, i):
        block = self.block(self.spot.a - s if way == 0 else self.spot.a + s)
        sem = self.sem
        return remote(
            block, block, sem.fs.at[way, s - 1, i - 1], sem.fr.at[way, s - 1, i - 1], self.spot.fast(i)
        )

    def start(self):
        spot, dims, sem = self.spot, self.dims, self.sem
        mine = self.rows(spot.d)
        if dims.na > 1:
            for way in range(2):

                @pl.when(self.sends(way, 1))
                def _(way=way):
                    self.hop(way, 1).start()

        self.own = [
            remote(self.source, mine, sem.xs.at[j - 1], sem.xr.at[j - 1], spot.fast(j))
            for j in range(1, dims.nb)
        ]
        for copy in self.own:
            copy.start()
        self.local = pltpu.make_async_copy(self.source, mine, sem.loc)
        self.local.start()

    def advance(self):
        dims = self.dims
        self.stage += 1
        s = self.stage
        if s >= dims.na:
            return False
        for way in range(2):

            @pl.when(self.has(way, s))
            def _(way=way):
                self.hop(way, s).wait_recv()
                for i in range(1, dims.nb):
                    self.hand(way, s, i).start()

            if s + 1 < dims.na:

                @pl.when(self.sends(way, s + 1))
                def _(way=way):
                    self.hop(way, s + 1).start()

        return True

    def finish(self):
        dims = self.dims
        while self.advance():
            pass
        self.local.wait()
        for copy in self.own:
            copy.wait()
        for s in range(1, dims.na):
            for way in range(2):

                @pl.when(self.sends(way, s))
                def _(way=way, s=s):
                    self.hop(way, s).wait_send()

                @pl.when(self.has(way, s))
                def _(way=way, s=s):
                    for i in range(1, dims.nb):
                        self.hand(way, s, i).wait()


class FastGather(Gather):
    def block(self, a):
        rows = self.source.shape[0] * self.dims.nb
        at = pl.ds(pl.multiple_of(a * rows, rows), rows)
        return self.whole.at[at] if self.columns is None else self.whole.at[at, self.columns]

    def hop(self, way, s):
        spot, sem = self.spot, self.sem
        step = 1 if way == 0 else -1
        block = self.block(spot.a - step * (s - 1))
        send, recv = (sem.us, sem.ur) if way == 0 else (sem.ds, sem.dr)
        peer = ((spot.a + step) * self.dims.nb + spot.b, spot.t)
        return remote(block, block, send.at[s - 1], recv.at[s - 1], peer)

    def start(self):
        spot, dims, sem = self.spot, self.dims, self.sem
        mine = self.rows(spot.d)
        self.own = [
            remote(self.source, mine, sem.xs.at[j - 1], sem.xr.at[j - 1], spot.fast(j))
            for j in range(1, dims.nb)
        ]
        self.local = pltpu.make_async_copy(self.source, mine, sem.loc)
        for copy in self.own + [self.local]:
            copy.start()
        self.stage = -1

    def advance(self):
        dims = self.dims
        self.stage += 1
        s = self.stage
        if s >= dims.na:
            return False
        if s == 0:
            self.local.wait()
            for copy in self.own:
                copy.wait_recv()
        for way in range(2):
            if s > 0:

                @pl.when(self.has(way, s))
                def _(way=way):
                    self.hop(way, s).wait_recv()

            if s + 1 < dims.na:

                @pl.when(self.sends(way, s + 1))
                def _(way=way):
                    self.hop(way, s + 1).start()

        return True

    def finish(self):
        while self.advance():
            pass
        for copy in self.own:
            copy.wait_send()
        for s in range(1, self.dims.na):
            for way in range(2):

                @pl.when(self.sends(way, s))
                def _(way=way, s=s):
                    self.hop(way, s).wait_send()


class Scatter:
    def __init__(self, tag, dims, rows, first, columns, into=None, slow_first=False):
        self.tag, self.dims, self.size = tag, dims, (rows, columns)
        self.columns = pl.ds(first, columns)
        self.into = self.columns if into is None else pl.ds(into, columns)
        self.slow_first = slow_first
        na, nb = dims.na, dims.nb
        m, half = max(nb - 1, 1), na // 2
        one = (half, nb) if slow_first else (m, na)
        two = (m, half) if slow_first else (half,)
        self.specs = dict(
            held=VM(((half, nb) if slow_first else (na,)) + self.size, BF16),
            one=VM(one + self.size, BF16),
            two=VM(two + self.size, BF16),
            three=VM(self.size, BF16),
            loc=SEMS((half,)),
            xs=SEMS((m,)),
            xr=SEMS((m,)),
            zs=SEMS((half,)),
            zr=SEMS((half,)),
            ls=SEMS,
            lr=SEMS,
        )
        self.stage = 0

    def scratch(self):
        return tagged("s", self.tag, self.specs)

    def bind(self, refs, spot, source, result):
        self.r = bound(refs, "s", self.tag, self.specs)
        self.spot, self.source, self.result = spot, source, result
        self.low, self.high = lax.rem(spot.a, 2), lax.div(spot.a, 2)
        return self

    def blocks(self, low):
        return [low + 2 * i for i in range(self.dims.na // 2)]

    def place(self, high, low):
        return (high * 2 + low) * self.dims.nb + self.spot.b, self.spot.t

    def neighbour(self):
        return self.place(self.high, 1 - self.low)

    def sum_rows(self, target, *parts):
        def add(i):
            rs = rows_of(i)
            total = target[rs, :].astype(F32)
            for part in parts:
                total = total + part[rs, :].astype(F32)
            target[rs, :] = total.astype(BF16)

        loop(self.size[0] // STEP, add, 2)

    def start(self):
        spot, dims, r = self.spot, self.dims, self.r
        self.sent, self.local = [], []
        if self.slow_first:
            for i, a in enumerate(self.blocks(1 - self.low)):
                self.sent.append(
                    remote(
                        self.source.at[a, :, :, self.columns], r.one.at[i], r.zs.at[i], r.zr.at[i],
                        self.neighbour(),
                    )
                )
            for i, a in enumerate(self.blocks(self.low)):
                self.local.append(
                    pltpu.make_async_copy(
                        self.source.at[a, :, :, self.columns], r.held.at[i], r.loc.at[i]
                    )
                )
        else:
            for j in range(1, dims.nb):
                block = lax.rem(spot.b + j, dims.nb)
                self.sent.append(
                    remote(
                        self.source.at[:, block, :, self.columns], r.one.at[j - 1], r.xs.at[j - 1],
                        r.xr.at[j - 1], spot.fast(j),
                    )
                )
            self.local.append(
                pltpu.make_async_copy(
                    self.source.at[:, spot.b, :, self.columns], r.held, r.loc.at[0]
                )
            )
        for copy in self.sent + self.local:
            copy.start()

    def advance(self):
        spot, dims, r = self.spot, self.dims, self.r
        half = dims.na // 2
        self.stage += 1
        if self.stage == 1:
            for copy in self.local:
                copy.wait()
            for copy in self.sent:
                copy.wait_recv()
            self.pair = []
            if self.slow_first:
                for i in range(half):
                    for b in range(dims.nb):
                        self.sum_rows(r.held.at[i, b], r.one.at[i, b])
                for j in range(1, dims.nb):
                    block = lax.rem(spot.b + j, dims.nb)
                    self.pair.append(
                        remote(
                            r.held.at[:, block], r.two.at[j - 1], r.xs.at[j - 1], r.xr.at[j - 1],
                            spot.fast(j),
                        )
                    )
            else:
                for a in range(dims.na):
                    self.sum_rows(r.held.at[a], *[r.one.at[j, a] for j in range(dims.nb - 1)])
                for i, a in enumerate(self.blocks(1 - self.low)):
                    self.pair.append(
                        remote(r.held.at[a], r.two.at[i], r.zs.at[i], r.zr.at[i], self.neighbour())
                    )
            for copy in self.pair:
                copy.start()
            return True
        if self.stage == 2:
            for copy in self.pair:
                copy.wait()
            if self.slow_first:
                for i in range(half):
                    self.sum_rows(
                        r.held.at[i, spot.b], *[r.two.at[j, i] for j in range(dims.nb - 1)]
                    )
                away, self.mine = r.held.at[1 - self.high, spot.b], r.held.at[self.high, spot.b]
            else:
                for i, a in enumerate(self.blocks(self.low)):
                    self.sum_rows(r.held.at[a], r.two.at[i])
                away = r.held.at[(1 - self.high) * 2 + self.low]
                self.mine = r.held.at[spot.a]
            self.final = remote(away, r.three, r.ls, r.lr, self.place(1 - self.high, self.low))
            self.final.start()
            return True
        return False

    def finish(self):
        while self.advance():
            pass
        r = self.r
        self.final.wait()

        def add(i):
            rs = rows_of(i)
            total = self.mine[rs, :].astype(F32) + r.three[rs, :].astype(F32)
            self.result[rs, self.into] = total

        loop(self.size[0] // STEP, add, 2)
        for copy in self.sent:
            copy.wait_send()


class Edge:
    def __init__(self, dims, count):
        self.dims, self.count = dims, count

    def scratch(self):
        nc, Q, D, count = self.dims.nc, self.dims.Q, self.dims.D, self.count
        m = max(self.dims.ny - 1, 1)
        return dict(
            e_own=VM((nc, Q, D), F32),
            e_give=VM((nc, Q, D), BF16),
            e_take=VM((nc, Q, D), BF16),
            e_sum=VM((nc, Q, D), BF16),
            e_far=VM((min(count, 2), m, nc, Q, D), BF16),
            e_ds=SEMS((count, nc)),
            e_dr=SEMS((count, nc)),
            e_ys=SEMS((count, m, nc)),
            e_yr=SEMS((count, m, nc)),
            e_ns=SEMS((count, nc)),
            e_nr=SEMS((count, nc)),
        )

    def bind(self, refs, spot):
        self.refs, self.spot = refs, spot
        self.near, self.far, self.handed = {}, {}, {}
        return self

    def open(self, i, k):
        if i > 0:
            self.near.pop((i - 1, k)).wait_send()

    def put(self, k, columns, part):
        Q, refs = self.dims.Q, self.refs
        low, high = part[:Q], part[Q:]
        first = self.spot.c == 0
        refs.e_own[k, :, columns] = jnp.where(first, low, high)
        refs.e_give[k, :, columns] = jnp.where(first, high, low).astype(BF16)

    def start(self, i, k):
        refs = self.refs
        copy = remote(
            refs.e_give.at[k],
            refs.e_take.at[k],
            refs.e_ds.at[i, k],
            refs.e_dr.at[i, k],
            self.spot.sibling(),
        )
        copy.start()
        self.near[i, k] = copy

    def cross(self, i, k, send=True):
        refs, dims = self.refs, self.dims
        self.near[i, k].wait_recv()
        if i > 0:
            for copy in self.far.pop((i - 1, k)):
                copy.wait_send()

        def add(j):
            rs = rows_of(j)
            total = refs.e_own[k, rs, :] + refs.e_take[k, rs, :].astype(F32)
            refs.e_own[k, rs, :] = total
            refs.e_sum[k, rs, :] = total.astype(BF16)

        loop(dims.Q // STEP, add, 2)
        if send:
            self.far[i, k] = []
            for j in range(1, dims.ny):
                copy = remote(
                    refs.e_sum.at[k],
                    refs.e_far.at[i % 2, j - 1, k],
                    refs.e_ys.at[i, j - 1, k],
                    refs.e_yr.at[i, j - 1, k],
                    self.spot.across(j),
                )
                copy.start()
                self.far[i, k].append(copy)

    def total(self, i, k, rs, slot):
        refs = self.refs
        total = refs.e_own[k, rs, :]
        for j in range(self.dims.ny - 1):
            total = total + refs.e_far[i % 2, j, slot, rs, :].astype(F32)
        return total

    def settle(self, i, k, row_fn, target):
        refs, dims, spot = self.refs, self.dims, self.spot
        for copy in self.far[i, k]:
            copy.wait_recv()
        base = (k * 2 + spot.c) * dims.Q

        def body(j):
            rs = rows_of(j)
            rows = row_fn(self.total(i, k, rs, k), k, rs)
            target[pl.ds(pl.multiple_of(base + j * STEP, STEP), STEP), :] = rows

        loop(dims.Q // STEP, body, 2)
        block = target.at[pl.ds(pl.multiple_of(base, dims.Q), dims.Q)]
        copy = remote(block, block, refs.e_ns.at[i, k], refs.e_nr.at[i, k], spot.sibling())
        copy.start()
        self.handed[i, k] = copy

    def arrived(self, i, k):
        self.handed[i, k].wait_recv()

    def drain(self):
        for copy in list(self.near.values()) + list(self.handed.values()):
            copy.wait_send()
        for copies in self.far.values():
            for copy in copies:
                copy.wait_send()


def unit(hidden):
    center = hidden - jnp.mean(hidden, axis=-1, keepdims=True)
    spread = jnp.mean(center * center, axis=-1, keepdims=True)
    inverse = lax.rsqrt(spread + EPSILON)
    return center * inverse, inverse


def unit_back(upstream, xhat, inverse, gain):
    scaled = upstream * gain
    return inverse * (
        scaled
        - jnp.mean(scaled, axis=-1, keepdims=True)
        - xhat * jnp.mean(scaled * xhat, axis=-1, keepdims=True)
    )


def fold(rows):
    return rows[:8] + rows[8:]


def chunk_rows(dims, k):
    return pl.ds(k * dims.L, dims.L)


def up_products(dims, k, normed, expand, inner, slope):
    rows = chunk_rows(dims, k)

    def column(j):
        cs = rows_of(j, TILE)
        before = jnp.dot(normed[rows, :], expand[:, cs], preferred_element_type=F32)
        gate = jax.nn.sigmoid(before)
        inner[rows, cs] = (before * gate).astype(BF16)
        slope[rows, cs] = (gate * (1.0 + before * (1.0 - gate))).astype(BF16)

    loop(dims.F // TILE, column, True)


def back_products(dims, k, upstream, shrink, slope, back):
    rows = chunk_rows(dims, k)

    def column(j):
        cs = rows_of(j, TILE)
        part = jnp.dot(upstream[rows, :], shrink[:, cs], preferred_element_type=F32)
        back[rows, cs] = (part * slope[rows, cs].astype(F32)).astype(BF16)

    loop(dims.F // TILE, column, True)


def part_product(edge, i, k, operand, matrix, first, dims):
    width = operand.shape[1]
    edge.open(i, k)

    def column(j):
        cs = rows_of(j, TILE)
        edge.put(
            k,
            cs,
            lax.dot_general(
                operand[chunk_rows(dims, k), :],
                matrix[cs, pl.ds(first, width)],
                (((1,), (1,)), ((), ())),
                preferred_element_type=F32,
            ),
        )

    loop(dims.D // TILE, column, True)
    edge.start(i, k)


def weight_part(result, first, rows_side, columns_side, dims):
    width = columns_side.shape[1]
    shard = result.shape[2]
    for i in range(dims.D // TILE):
        part = lax.dot_general(
            rows_side[:, pl.ds(i * TILE, TILE)],
            columns_side[...],
            (((0,), (0,)), ((), ())),
            preferred_element_type=F32,
        ).astype(BF16)
        for j in range(TILE // shard):
            d = i * (TILE // shard) + j
            result[d // dims.nb, d % dims.nb, :, pl.ds(first, width)] = part[
                j * shard : (j + 1) * shard
            ]


def forward_rows(hidden, scale, gain, kept):
    def rows(total, k, rs):
        after = hidden[k, rs, :].astype(F32) + scale * total
        kept[k, rs, :] = after
        xhat, _ = unit(after)
        return (xhat * gain[...]).astype(BF16)

    return rows


def backward_rows(hidden, scale, gain, grad, sums, spot):
    def rows(total, k, rs):
        xhat, inverse = unit(hidden[k, rs, :].astype(F32))
        own = jnp.where(spot.y == k // 2, 1.0, 0.0)
        sums[...] += fold(total * xhat) * own
        after = grad[k, rs, :] + unit_back(total, xhat, inverse, gain[...])
        grad[k, rs, :] = after
        return (scale * after).astype(BF16)

    return rows


QUERIES = 256
BAND = 64
MARGIN = 16


def slide(padded, base, taps, flip=False):
    window = padded[pl.ds(pl.multiple_of(base, BAND), BAND + 2 * MARGIN), :]
    total = None
    for residue in range(8):
        shifted = window[residue : residue + BAND + 24]
        for eighth in range(4):
            tap = 8 * eighth + residue - 1
            if 0 <= tap < KERNEL:
                place = KERNEL - 1 - tap if flip else tap
                term = shifted[8 * eighth : 8 * eighth + BAND] * taps[place, 0:1, :]
                total = term if total is None else total + term
    return total


def clear_margins(padded, S):
    edge = jnp.zeros((MARGIN, padded.shape[1]), F32)
    padded[pl.ds(0, MARGIN), :] = edge
    padded[pl.ds(MARGIN + S, MARGIN), :] = edge


def attend(dims, k, r):
    H, m = dims.H, dims.L
    heads = H // HEAD_DIM
    blocks = m // min(QUERIES, m)
    size = m // blocks

    def one(i):
        head = lax.div(i, blocks)
        at = pl.ds(pl.multiple_of(k * m + lax.rem(i, blocks) * size, size), size)
        scores = lax.dot_general(
            r.k[head], r.q[head, at, :], (((1,), (1,)), ((), ())), preferred_element_type=F32
        )
        scores = scores + r.column[...]
        peak = jnp.max(scores, axis=0, keepdims=True)
        exponent = jnp.exp(scores - peak)
        total = jnp.sum(exponent, axis=0, keepdims=True)
        output = jnp.dot(r.vt[head], exponent.astype(BF16), preferred_element_type=F32)
        r.lse[head, :, at] = peak + jnp.log(total)
        r.ot[pl.ds(pl.multiple_of(head * HEAD_DIM, HEAD_DIM), HEAD_DIM), at] = output / total

    loop(heads * blocks, one)
    rows = chunk_rows(dims, k)
    r.oh[rows, :] = r.ot[:, rows].T.astype(BF16)


def live_column(r, S, dead):
    place = lax.broadcasted_iota(jnp.int32, (S, 1), 0)
    live, other = (0.0, MASKED) if dead else (1.0, 0.0)
    r.column[...] = jnp.where(place < r.lengths[0], live, other)


def front_kernel(
    dims, cid, frames, cotangent, lengths, gains, expand, shrink, project, mixing, gating, merging
):
    nc, L, Q, D, S, F, H, C = (
        dims.nc, dims.L, dims.Q, dims.D, dims.S, dims.F, dims.H, dims.C
    )
    heads = H // HEAD_DIM
    shard = expand.shape[2]
    edge = Edge(dims, 2)
    gathers = [Gather(str(i), dims) for i in range(5)] + [FastGather(str(5), dims)]
    half = F // 4
    scratch = edge.scratch() | dict(
        vt=VM((heads, HEAD_DIM, S), BF16),
        ot=VM((H, S), F32),
        column=VM((S, 1), F32),
        ogl=VM((2, Q, D), BF16),
        s0=VM((shard, F), BF16),
        s1=VM((shard, F), BF16),
        s2=VM((shard, 4 * H), BF16),
        s3=VM((shard, 3 * C), BF16),
        s4=VM((shard, F), BF16),
        s5=VM((shard, half), BF16),
        xs=SEMS((nc,)),
        xr=SEMS((nc,)),
        os=SEMS((nc,)),
        orr=SEMS((nc,)),
        ns=SEMS((nc,)),
        nr=SEMS((nc,)),
    )
    for gather in gathers:
        scratch |= gather.scratch()

    def body(r):
        spot = Spot(dims)
        others = [(spot.d, lax.rem(spot.t + j, nc)) for j in range(1, nc)]
        greet(others + spot.data_peers())
        edge.bind(r, spot)
        for i, (source, whole) in enumerate(
            ((r.s0, r.e), (r.s1, r.rt), (r.s2, r.wa), (r.s3, r.wc), (r.s4, r.e1), (r.s5, r.ra))
        ):
            gathers[i].bind(r, spot, source, whole)
        r.need("x")
        moves = []
        for j in range(1, nc):
            some = pl.ds(pl.multiple_of(lax.rem(spot.c + j, 2) * Q, Q), Q)
            copy = remote(
                r.x.at[some], r.xh.at[spot.t], r.xs.at[j - 1], r.xr.at[j - 1], others[j - 1]
            )
            copy.start()
            moves.append(copy)

        r.need("pe")
        r.s0[...] = r.pe[0].astype(BF16)
        gathers[0].start()
        r.need("pr")

        def turned(target, first, source, begin=0, count=None):
            def part(j):
                cs = pl.ds(pl.multiple_of(begin + j * 128, 128), 128)
                target[:, pl.ds(pl.multiple_of(first + j * 128, 128), 128)] = (
                    source[cs, :].T.astype(BF16)
                )

            loop((count or source.shape[0]) // 128, part, True)

        turned(r.s1, 0, r.pr.at[0])
        gathers[1].start()
        mine = pl.ds(pl.multiple_of(spot.c * Q, Q), Q)
        r.xh[spot.t] = r.x[mine, :]

        handed = []

        def normalize(t):
            base = pl.multiple_of((t * 2 + spot.c) * Q, Q)

            def rows(i):
                xhat, _ = unit(r.xh[t, rows_of(i), :].astype(F32))
                target = pl.ds(pl.multiple_of(base + i * STEP, STEP), STEP)
                r.n1[target, :] = (xhat * r.g0[...]).astype(BF16)

            loop(Q // STEP, rows, 2)
            block = r.n1.at[pl.ds(base, Q)]
            i = len(handed)
            copy = remote(block, block, r.ns.at[i], r.nr.at[i], spot.sibling())
            copy.start()
            handed.append(copy)

        normalize(spot.t)
        r.need("og")
        place = lax.broadcasted_iota(jnp.int32, (Q, 1), 0) + spot.t * L
        for i in range(2):
            live = place + i * Q < r.lengths[0]
            r.ogl[i] = jnp.where(live, r.og[pl.ds(i * Q, Q), :].astype(F32), 0.0).astype(BF16)
        for j in range(1, nc):
            copy = remote(
                r.ogl.at[lax.rem(spot.c + j, 2)], r.ogh.at[spot.t], r.os.at[j - 1], r.orr.at[j - 1],
                others[j - 1],
            )
            copy.start()
            moves.append(copy)
        r.ogh[spot.t] = r.ogl[spot.c]
        gathers[0].advance()
        gathers[1].advance()
        for j in range(1, nc):
            moves[j - 1].wait_recv()
            normalize(lax.rem(spot.t + nc - j, nc))
        gathers[0].advance()
        gathers[1].advance()

        r.need("pp", "pm", "pg", "pz")
        for i in range(3):
            r.s2[:, pl.ds(i * H, H)] = r.pp[i].astype(BF16)
        turned(r.s2, 3 * H, r.pm)
        for i in range(2):
            r.s3[:, pl.ds(i * C, C)] = r.pg[i].astype(BF16)
        turned(r.s3, 2 * C, r.pz)
        r.s4[...] = r.pe[1].astype(BF16)
        turned(r.s5, 0, r.pr.at[1], 0, half)
        turned(r.r1, 0, r.pr.at[1], half, F - half)
        r.done("r1")
        live_column(r, S, True)
        gathers[0].advance()
        gathers[1].advance()
        gathers[2].start()
        for copy in handed:
            copy.wait()
        gathers[0].finish()

        for k in range(nc):
            up_products(dims, k, r.n1, r.e, r.u, r.slope)
            if k == 0:
                gathers[1].finish()
            part_product(edge, 0, k, r.u, r.rt, 0, dims)
            if k > 0:
                edge.cross(0, k - 1)
        edge.cross(0, nc - 1)
        r.done("u", "slope", "n1", "e", "rt")
        gathers[2].advance()
        for k in range(nc):
            edge.settle(0, k, forward_rows(r.xh, 0.5, r.g1, r.h1), r.n2)
            if k < 2:
                gathers[2].advance()
            if k == 1:
                gathers[3].start()
        gathers[3].advance()
        r.done("h1")
        for k in range(nc):
            edge.arrived(0, k)
        r.done("n2")
        gathers[2].finish()
        gathers[4].start()
        for i, target in enumerate((r.q, r.k, r.v)):
            packed = jnp.dot(r.n2[...], r.wa[:, pl.ds(i * H, H)], preferred_element_type=F32)
            if i == 0:
                packed = packed.astype(BF16).astype(F32) * HEAD_DIM**-0.5
            for j in range(heads):
                part = packed[:, j * HEAD_DIM : (j + 1) * HEAD_DIM]
                target[j] = part.astype(BF16)
                if i == 2:
                    r.vt[j] = part.T.astype(BF16)
        r.done("q", "k", "v", "wa")

        for k in range(nc):
            attend(dims, k, r)
            part_product(edge, 1, k, r.oh, r.wa, 3 * H, dims)
            if k > 0:
                edge.cross(1, k - 1)
            gathers[3 if k < 2 else 4].advance()
            if k == 1:
                gathers[5].start()
            elif k == 3:
                gathers[5].advance()
        edge.cross(1, nc - 1)
        r.done("oh", "lse")
        for k in range(nc):
            edge.settle(1, k, forward_rows(r.h1, 1.0, r.g2, r.h2), r.n3)
            gathers[4 if k == 0 else 5].advance()
        r.done("h2")
        for k in range(nc):
            edge.arrived(1, k)
        r.done("n3")
        for copy in moves[: nc - 1]:
            copy.wait_send()
        for copy in moves[nc - 1 :]:
            copy.wait()
        edge.drain()
        for gather in gathers[3:]:
            gather.finish()

    triple = (heads, S, HEAD_DIM)
    rows_all, held = (S, D), (nc, Q, D)
    return call(
        body,
        dict(
            x=(frames, LD),
            pe=(expand, LD0),
            pr=(shrink, LD0),
            og=(cotangent, LD),
            pp=(project, LD0),
            pm=(mixing, LD0),
            pg=(gating, LD0),
            pz=(merging, LD0),
            lengths=(lengths, SM),
            g0=(gains[0], VM),
            g1=(gains[1], VM),
            g2=(gains[2], VM),
        ),
        dict(
            xh=(held, BF16, ST),
            ogh=(held, BF16, ST),
            n1=(rows_all, BF16, ST),
            e=((D, F), BF16, ST),
            rt=((D, F), BF16, ST),
            u=((S, F), BF16, ST),
            slope=((S, F), BF16, ST),
            h1=(held, F32, ST),
            n2=(rows_all, BF16, ST),
            q=(triple, BF16, ST),
            k=(triple, BF16, ST),
            v=(triple, BF16, ST),
            oh=((S, H), BF16, ST),
            lse=((heads, 1, S), F32, ST),
            h2=(held, F32, ST),
            n3=(rows_all, BF16, ST),
            wa=((D, 4 * H), BF16, ST),
            r1=((shard, F - half), BF16, ST),
            ra=((D, half), BF16, HB),
            wc=((D, 3 * C), BF16, HB),
            e1=((D, F), BF16, HB),
        ),
        scratch,
        cid,
    )


def middle_kernel(dims, cid, kept, lengths, taps, gains, shard):
    nc, Q, D, S, F, C = dims.nc, dims.Q, dims.D, dims.S, dims.F, dims.C
    m = dims.L
    edge = Edge(dims, 4)
    gather = Gather("0", dims)
    half = F // 2
    scatters = [Scatter(str(j), dims, shard, half * (j % 2), half) for j in range(3)]
    four = (dims.na, dims.nb, shard)
    scratch = edge.scratch() | gather.scratch()
    scratch |= dict(
        rt=VM((D, F), BF16),
        n4=VM((S, D), BF16),
        h3=VM((nc, Q, D), F32),
        fall=VM((nc, Q, D), BF16),
        column=VM((S, 1), F32),
        rsem=SEMS,
        fsem=SEMS((3,)),
        u=VM((S, F), BF16),
        slope=VM((S, F), BF16),
        w4=VM((S, D), BF16),
        dr=VM(four + (F,), BF16),
        w3=VM((S, D), BF16),
        z=VM((S, C), BF16),
        zslope=VM((S, C), F32),
        ga=VM((S, C), F32),
        gb=VM((S, C), F32),
        glu=VM((S + 2 * MARGIN, C), F32),
        back=VM((S + 2 * MARGIN, C), F32),
        pair=VM((S, 2 * C), BF16),
        sums=VM((KERNEL, 8, C), F32),
    )
    for scatter in scatters:
        scratch |= scatter.scratch()

    def body(r):
        spot = Spot(dims)
        greet(spot.tensor_peers() + spot.data_peers())
        edge.bind(r, spot)
        begin = F // 4
        gather.bind(r, spot, r.sr, r.rt, pl.ds(begin, F - begin)).start()
        early = pltpu.make_async_copy(r.ra, r.rt.at[:, pl.ds(0, begin)], r.rsem)
        early.start()
        for scatter in scatters[:2]:
            scatter.bind(r, spot, r.dr, r.outr)
        scatters[2].bind(r, spot, r.de, r.oute)
        for sums in (r.dg2, r.dg3, r.dg4):
            sums[...] = jnp.zeros_like(sums)

        clear_margins(r.glu, S)
        clear_margins(r.back, S)
        live_column(r, S, False)
        r.need("n", "wc")

        def gated(i):
            rows = rows_of(i, 256)
            values = jnp.dot(r.n[rows, :], r.wc[:, pl.ds(0, C)], preferred_element_type=F32)
            gate = jax.nn.sigmoid(
                jnp.dot(r.n[rows, :], r.wc[:, pl.ds(C, C)], preferred_element_type=F32)
            )
            open_gate = gate * r.column[rows, :]
            product = values * open_gate
            r.ga[rows, :] = open_gate
            r.gb[rows, :] = product * (1.0 - gate)
            r.glu[pl.ds(pl.multiple_of(i * 256 + MARGIN, MARGIN), 256), :] = product

        loop(S // 256, gated)
        for k in range(nc):

            def band(i, k=k):
                base = k * m + i * BAND
                mixed = slide(r.glu, base, r.taps)
                gate = jax.nn.sigmoid(mixed)
                rows = pl.ds(pl.multiple_of(base, BAND), BAND)
                r.z[rows, :] = (mixed * gate).astype(BF16)
                r.zslope[rows, :] = gate * (1.0 + mixed * (1.0 - gate))

            loop(m // BAND, band)
            part_product(edge, 0, k, r.z, r.wc, 2 * C, dims)
            if k > 0:
                edge.cross(0, k - 1)
            if k == 1:
                gather.advance()
        edge.cross(0, nc - 1)
        gather.advance()

        r.need("h", "e")
        for k in range(nc):
            edge.settle(0, k, forward_rows(r.h, 1.0, r.g3, r.h3), r.n4)
            if k == 0:
                gather.advance()
            edge.arrived(0, k)
            up_products(dims, k, r.n4, r.e, r.u, r.slope)
            if k == 0:
                early.wait()
                gather.finish()
            part_product(edge, 1, k, r.u, r.rt, 0, dims)
            edge.cross(1, k)

        def turn(total, k, rs):
            xhat, inverse = unit(r.h3[k, rs, :] + 0.5 * total)
            r.fall[k, rs, :] = (xhat * r.g4[...]).astype(BF16)
            upstream = r.og[k, rs, :].astype(F32)
            own = jnp.where(spot.y == k // 2, 1.0, 0.0)
            r.dg4[...] += fold(upstream * xhat) * own
            grad = unit_back(upstream, xhat, inverse, r.g4[...])
            r.gh[k, rs, :] = grad
            return (0.5 * grad).astype(BF16)

        r.need("og")
        for k in range(nc):
            edge.settle(1, k, turn, r.w4)
            edge.arrived(1, k)
            back_products(dims, k, r.w4, r.rt, r.slope, r.slope)
            part_product(edge, 2, k, r.slope, r.e, 0, dims)
            edge.cross(2, k)
        keep = pltpu.make_async_copy(r.fall.at[spot.t], r.fo.at[spot.c], r.fsem.at[2])
        keep.start()
        other = spot.y * 2 + 1 - spot.c
        give = remote(
            r.fall.at[other], r.fo.at[spot.c], r.fsem.at[0], r.fsem.at[1], spot.sibling()
        )
        give.start()
        weight_part(r.dr, 0, r.w4, r.u, dims)
        for scatter in scatters[:2]:
            scatter.start()
        weight_part(r.de, 0, r.n4, r.slope, dims)
        scatters[2].start()
        r.done("de")

        finished = 0
        for k in range(nc):
            edge.settle(2, k, backward_rows(r.h3, 1.0, r.g3, r.gh, r.dg3, spot), r.w3)
            edge.arrived(2, k)
            rows = chunk_rows(dims, k)
            inner = jnp.dot(r.w3[rows, :], r.wc[:, pl.ds(2 * C, C)], preferred_element_type=F32)
            r.back[pl.ds(k * m + MARGIN, m), :] = inner * r.zslope[rows, :]
            until = (k + 1) * m // BAND - (1 if k < nc - 1 else 0)

            def band(i, finished=finished):
                base = (i + finished) * BAND
                rows = pl.ds(pl.multiple_of(base, BAND), BAND)
                mixed = slide(r.back, base, r.taps, True)
                r.pair[rows, pl.ds(0, C)] = (mixed * r.ga[rows, :]).astype(BF16)
                r.pair[rows, pl.ds(C, C)] = (mixed * r.gb[rows, :]).astype(BF16)

            loop(until - finished, band)
            finished = until
            if k == 2:
                scatters[0].advance()
            if k > 0:
                part_product(edge, 3, k - 1, r.pair, r.wc, 0, dims)
            if k > 1:
                edge.cross(3, k - 2)
        edge.cross(3, nc - 2)
        part_product(edge, 3, nc - 1, r.pair, r.wc, 0, dims)
        edge.cross(3, nc - 1)
        scatters[1].advance()
        weight_part(r.dw, 0, r.n, r.pair, dims)
        weight_part(r.dw, 2 * C, r.w3, r.z, dims)
        r.done("dw")
        scatters[0].advance()
        r.sums[...] = jnp.zeros_like(r.sums)

        def tap_sums(i):
            base = i * BAND
            window = r.glu[pl.ds(pl.multiple_of(base, BAND), BAND + 2 * MARGIN), :]
            slope = r.back[pl.ds(pl.multiple_of(base + MARGIN, MARGIN), BAND), :]
            for residue in range(8):
                shifted = window[residue : residue + BAND + 24]
                for eighth in range(4):
                    tap = 8 * eighth + residue - 1
                    if 0 <= tap < KERNEL:
                        term = shifted[8 * eighth : 8 * eighth + BAND] * slope
                        r.sums[tap] += term.reshape(BAND // 8, 8, C).sum(axis=0)

        loop(S // BAND, tap_sums)
        for tap in range(KERNEL):
            r.dk[tap : tap + 1, :] = jnp.sum(r.sums[tap], axis=0, keepdims=True)
        for k in range(nc):
            edge.settle(3, k, backward_rows(r.h, 1.0, r.g2, r.gh, r.dg2, spot), r.w2)
            if k == 0:
                scatters[2].advance()
            elif k == 1:
                scatters[1].advance()
            elif k == 2:
                scatters[0].finish()
                scatters[2].advance()
        r.done("gh")
        for k in range(nc):
            edge.arrived(3, k)
        r.done("w2")
        keep.wait()
        give.wait()
        edge.drain()
        for scatter in scatters[1:]:
            scatter.finish()

    return call(
        body,
        dict(
            n=(kept["n3"], LD),
            wc=(kept["wc"], LD),
            e=(kept["e1"], LD),
            h=(kept["h2"], LD),
            og=(kept["ogh"], LD),
            taps=(taps, VM),
            lengths=(lengths, SM),
            g2=(gains[2], VM),
            g3=(gains[3], VM),
            g4=(gains[4], VM),
            sr=(kept["r1"], HB),
            ra=(kept["ra"], HB),
        ),
        dict(
            fo=((2, Q, D), BF16, HB),
            gh=((nc, Q, D), F32, ST),
            w2=((S, D), BF16, ST),
            dw=(four + (3 * C,), BF16, ST),
            de=(four + (F,), BF16, ST),
            outr=((shard, F), F32, VM),
            oute=((shard, half), F32, VM),
            dk=((KERNEL, C), F32, VM),
            dg2=((8, D), F32, VM),
            dg3=((8, D), F32, VM),
            dg4=((8, D), F32, VM),
        ),
        scratch,
        cid,
    )


def last_kernel(dims, cid, kept, middle, lengths, gains, shard):
    nc, Q, D, S, F, H, C = dims.nc, dims.Q, dims.D, dims.S, dims.F, dims.H, dims.C
    heads = H // HEAD_DIM
    edge = Edge(dims, 2)
    four = (dims.na, dims.nb, shard)
    some = 3 * H // 2 if H % 256 == 0 else 3 * H
    scatters = [
        Scatter("0", dims, shard, 0, 3 * C),
        Scatter("1", dims, shard, F // 2, F // 2, 0, True),
        Scatter("2", dims, shard, 3 * H, H),
    ]
    scatters += [
        Scatter(str(3 + j), dims, shard, j * some, some) for j in range(3 * H // some)
    ]
    triple = (heads, S, HEAD_DIM)
    scratch = edge.scratch() | dict(
        da=VM(triple, BF16),
        kt=VM((heads, HEAD_DIM, S), BF16),
        delta=VM((heads, 1, S), F32),
        gk=VM(triple, F32),
        gv=VM(triple, F32),
        dqt=VM((H, S), F32),
        pack=VM((S, 3 * H), BF16),
        dw=VM(four + (4 * H,), BF16),
        w1=VM((S, D), BF16),
        column=VM((S, 1), F32),
        psem=SEMS,
        gsem=SEMS,
    )
    for scatter in scatters:
        scratch |= scatter.scratch()

    def body(r):
        spot = Spot(dims)
        greet(spot.tensor_peers() + spot.data_peers())
        edge.bind(r, spot)
        scatters[0].bind(r, spot, r.cw, r.sc).start()
        scatters[1].bind(r, spot, r.dei, r.oute).start()
        for scatter in scatters[2:]:
            scatter.bind(r, spot, r.dw, r.sa)
        live_column(r, S, True)
        for sums in (r.dg1, r.gk, r.gv):
            sums[...] = jnp.zeros_like(sums)

        ghc = pltpu.make_async_copy(r.ghi, r.gh, r.gsem)
        ghc.start()

        r.need("w", "oh")
        weight_part(r.dw, 3 * H, r.w, r.oh, dims)
        scatters[2].start()
        r.need("wa", "k")
        mixed = jnp.dot(r.w[...], r.wa[:, pl.ds(3 * H, H)], preferred_element_type=F32).astype(BF16)
        inner = (mixed.astype(F32) * r.oh[...].astype(F32)).T
        for j in range(heads):
            some = slice(j * HEAD_DIM, (j + 1) * HEAD_DIM)
            r.da[j] = mixed[:, some]
            r.delta[j] = jnp.sum(inner[some], axis=0, keepdims=True)
            r.kt[j] = r.k[j].astype(F32).T.astype(BF16)
        blocks = S // min(2 * QUERIES, S)
        size = S // blocks
        r.need("q", "v", "lse")

        def one(i):
            head = lax.div(i, blocks)
            at = pl.ds(pl.multiple_of(lax.rem(i, blocks) * size, size), size)
            query, outer = r.q[head, at, :], r.da[head, at, :]
            scores = lax.dot_general(
                r.k[head], query, (((1,), (1,)), ((), ())), preferred_element_type=F32
            )
            prob = jnp.exp(scores + (r.column[...] - r.lse[head, :, at]))
            r.gv[head] += jnp.dot(prob.astype(BF16), outer, preferred_element_type=F32)
            back = lax.dot_general(
                r.v[head], outer, (((1,), (1,)), ((), ())), preferred_element_type=F32
            )
            slope = (prob * (back - r.delta[head, :, at])).astype(BF16)
            r.gk[head] += jnp.dot(slope, query, preferred_element_type=F32)
            r.dqt[pl.ds(pl.multiple_of(head * HEAD_DIM, HEAD_DIM), HEAD_DIM), at] = (
                jnp.dot(r.kt[head], slope, preferred_element_type=F32) * HEAD_DIM**-0.5
            )

        loop(heads * blocks, one)
        scatters[1].advance()
        r.pack[:, pl.ds(0, H)] = r.dqt[...].T.astype(BF16)
        for j, source in ((1, r.gk), (2, r.gv)):
            r.pack[:, pl.ds(j * H, H)] = jnp.concatenate(
                [source[i] for i in range(heads)], axis=1
            ).astype(BF16)
        for k in range(nc):
            part_product(edge, 0, k, r.pack, r.wa, 0, dims)
            if k > 0:
                edge.cross(0, k - 1)
        edge.cross(0, nc - 1)
        r.need("n2")
        scatters[0].advance()
        weight_part(r.dw, 0, r.n2, r.pack, dims)
        for scatter in scatters[3:]:
            scatter.start()

        ghc.wait()
        r.need("h1", "rt", "slope", "e")
        for k in range(nc):
            edge.settle(0, k, backward_rows(r.h1, 0.5, r.g1, r.gh, r.dg1, spot), r.w1)
            edge.arrived(0, k)
            back_products(dims, k, r.w1, r.rt, r.slope, r.slope)
            part_product(edge, 1, k, r.slope, r.e, 0, dims)
            if k > 0:
                edge.cross(1, k - 1, send=False)
            if k == 0:
                scatters[2].advance()
            elif k == 1:
                scatters[1].advance()
                scatters[0].advance()
            elif k == 2:
                scatters[2].advance()
                scatters[3].advance()
            elif k == 3:
                scatters[0].finish()
                scatters[-1].advance()
        r.done("gh")
        r.need("n1", "u")
        weight_part(r.dr, 0, r.w1, r.u, dims)
        r.done("dr")
        scatters[3].advance()
        edge.cross(1, nc - 1, send=False)
        part = pltpu.make_async_copy(r.e_sum, r.part, r.psem)
        part.start()
        weight_part(r.de, 0, r.n1, r.slope, dims)
        r.done("de")
        scatters[-1].advance()
        scatters[1].finish()
        scatters[2].finish()
        part.wait()
        edge.drain()
        for scatter in scatters[3:]:
            scatter.finish()

    return call(
        body,
        dict(
            w=(middle["w2"], LD),
            wa=(kept["wa"], LD),
            oh=(kept["oh"], LD),
            k=(kept["k"], LD),
            q=(kept["q"], LD),
            v=(kept["v"], LD),
            lse=(kept["lse"], LD),
            n2=(kept["n2"], LD),
            ghi=(middle["gh"], HB),
            h1=(kept["h1"], LD),
            rt=(kept["rt"], LD),
            slope=(kept["slope"], LD),
            e=(kept["e"], LD),
            n1=(kept["n1"], LD),
            u=(kept["u"], LD),
            lengths=(lengths, SM),
            g1=(gains[1], VM),
            cw=(middle["dw"], HB),
            dei=(middle["de"], HB),
        ),
        dict(
            part=((nc, Q, D), BF16, HB),
            gh=((nc, Q, D), F32, ST),
            de=(four + (F,), BF16, ST),
            dr=(four + (F,), BF16, ST),
            sc=((shard, 3 * C), F32, VM),
            sa=((shard, 4 * H), F32, VM),
            oute=((shard, F // 2), F32, VM),
            dg1=((8, D), F32, VM),
        ),
        scratch,
        cid,
    )


def direction_of(mean, square, master, rates, decay):
    return mean * rates[4] / (jnp.sqrt(square * rates[5]) + ADAM_EPS) + decay * master


def moments_of(grad, mean, square, rates):
    return (
        rates[0] * mean + (1.0 - rates[0]) * grad,
        rates[1] * square + (1.0 - rates[1]) * grad * grad,
    )


def tile_rows(shape):
    rows, columns = shape[-2:]
    step = min(rows, max(8, 16384 // max(columns, 128)))
    return step if rows % step == 0 and step % 8 == 0 else rows


def eighths(tile):
    rows, columns = tile.shape
    return tile.reshape(rows // 8, 8, columns).sum(axis=0) if rows % 8 == 0 else tile


def flip(result, source, dims):
    def part(j):
        cs = rows_of(j, 128)
        result[cs, :] = source[:, cs].T

    loop(source.shape[1] // 128, part)


PLACES = (0, 1, 2, 3, 4, 6, 5, 7)


def piece_rows(shapes):
    rows, total = {}, 0
    for i in PLACES:
        rows[i] = total
        total += shapes[i][0]
    return rows


class Relay:
    def __init__(self, tag, count, shape):
        self.tag, self.count = tag, count
        k = max(count - 1, 1)
        self.specs = dict(slots=VM((count,) + shape, F32), s=SEMS((k,)), r=SEMS((k,)))

    def scratch(self):
        return tagged("r", self.tag, self.specs)

    def start(self, refs, place, peers, value):
        self.r = bound(refs, "r", self.tag, self.specs)
        r = self.r
        r.slots[place] = value
        self.copies = []
        for j, peer in enumerate(peers):
            copy = remote(r.slots.at[place], r.slots.at[place], r.s.at[j], r.r.at[j], peer)
            copy.start()
            self.copies.append(copy)

    def finish(self):
        for copy in self.copies:
            copy.wait()
        total = self.r.slots[0]
        for i in range(1, self.count):
            total = total + self.r.slots[i]
        return total


def gradient_kernel(
    dims, cid, rates, entries, scatter, sums, gain_parts, kernel_part, part, grad, hidden, gain
):
    D, F, H, C, Q, ny = dims.D, dims.F, dims.H, dims.C, dims.Q, dims.ny
    shard = scatter[0].shape[2]
    pieces = 4
    width = F // pieces
    jobs = [
        Scatter(str(pieces * i + j), dims, shard, j * width, width, None, pieces * i + j > 5)
        for i in range(2)
        for j in range(pieces)
    ]
    count_t, count_d = dims.ny * 2, dims.na * dims.nb
    gains_relays = [
        Relay("0", 2, (8, D)), Relay("1", ny, (8, D)),
        Relay("2", dims.na, (8, D)), Relay("3", dims.nb, (8, D)),
    ]
    taps_relays = [Relay("4", dims.na, (KERNEL, C)), Relay("5", dims.nb, (KERNEL, C))]
    norm_relays = [Relay("6", count_t, (24, 128)), Relay("7", count_d, (24, 128))]
    relays = gains_relays + taps_relays + norm_relays
    count = len(entries)
    m = max(ny - 1, 1)
    shapes = [entry[1].shape for entry in entries]
    scratch = dict(
        nrm=VM((24, 128), F32),
        gains=VM((8, D), F32),
        dg0=VM((8, D), F32),
        shr0=VM((shard, F), F32),
        shr1=VM((shard, F), F32),
        mix=VM((shard, H), F32),
        mer=VM((shard, C), F32),
        far=VM((m, 2, Q, D), BF16),
        sum=VM((dims.nc, Q, D), BF16),
        gh=VM((2, Q, D), F32),
        h=VM((2, Q, D), BF16),
        both=VM((2, Q, D), BF16),
        gsem=SEMS((10,)),
        psem=SEMS((4,)),
        fsem=SEMS((m, 2)),
        bsem=SEMS((2,)),
        isem=SEMS((count, 3)),
    )
    ins = dict(
        rates=(rates, SM),
        kp=(kernel_part, VM),
        sp=(part, HB),
        ghp=(grad, HB),
        hp=(hidden, HB),
        g=(gain, VM),
        src0=(scatter[0], HB),
        src1=(scatter[1], HB),
    )
    outs = dict(norms=((24, 128), F32, VM), gin=((2, Q, D), BF16, HB))
    for i, (params, mean, square, _) in enumerate(entries):
        tag = str(i)
        held = shapes[i] if i < 6 else params.shape
        ins |= {"p" + tag: (params, HB), "m" + tag: (mean, HB), "v" + tag: (square, HB)}
        scratch |= {"w" + tag: VM(held, F32), "n" + tag: VM(shapes[i], F32)}
        scratch |= {"q" + tag: VM(shapes[i], F32)}
        outs |= {"g" + tag: (shapes[i], F32, VM)}
    for i, array in enumerate(gain_parts):
        ins |= {"d" + str(i): (array, VM)}
    for i, array in enumerate(sums):
        ins |= {"s" + str(i): (array, HB)}
    for item in relays + jobs:
        scratch |= item.scratch()

    def body(r):
        spot = Spot(dims)
        everyone = [(spot.d, lax.rem(spot.t + j, count_t)) for j in range(1, count_t)]
        items = [(lax.rem(spot.d + j, count_d), spot.t) for j in range(1, count_d)]
        greet(everyone + items)
        get = lambda name, i: getattr(r, name + str(i))
        for i, job in enumerate(jobs):
            early = i < pieces
            job.bind(r, spot, r.src0 if early else r.src1, r.shr0 if early else r.g0.at[0])
        for i in (6, 0, 7, 1, 2, 3, 4, 5):
            jobs[i].start()
        mine = pl.ds(spot.y * 2, 2)
        totals = [
            pltpu.make_async_copy(r.sp, r.sum, r.psem.at[0]),
            pltpu.make_async_copy(r.ghp.at[mine], r.gh, r.psem.at[1]),
            pltpu.make_async_copy(r.hp.at[mine], r.h, r.psem.at[2]),
        ]
        for copy in totals:
            copy.start()
        grads = [
            pltpu.make_async_copy(r.s0, r.g0.at[1, :, pl.ds(0, F // 2)], r.gsem.at[0]),
            pltpu.make_async_copy(r.s4, r.g0.at[1, :, pl.ds(F // 2, F // 2)], r.gsem.at[9]),
            pltpu.make_async_copy(r.s1, r.shr1, r.gsem.at[1]),
            pltpu.make_async_copy(r.s2.at[:, pl.ds(3 * H, H)], r.mix, r.gsem.at[2]),
            pltpu.make_async_copy(r.s3.at[:, pl.ds(2 * C, C)], r.mer, r.gsem.at[3]),
        ]
        grads += [
            pltpu.make_async_copy(r.s2.at[:, pl.ds(k * H, H)], r.g2.at[k], r.gsem.at[4 + k])
            for k in range(3)
        ]
        grads += [
            pltpu.make_async_copy(r.s3.at[:, pl.ds(k * C, C)], r.g4.at[k], r.gsem.at[7 + k])
            for k in range(2)
        ]
        for copy in grads:
            copy.start()
        loads = []
        for i in range(count):
            master = get("p", i).at[0] if i < 6 else get("p", i)
            triple = [
                pltpu.make_async_copy(master, get("w", i), r.isem.at[i, 0]),
                pltpu.make_async_copy(get("m", i), get("n", i), r.isem.at[i, 1]),
                pltpu.make_async_copy(get("v", i), get("q", i), r.isem.at[i, 2]),
            ]
            for copy in triple:
                copy.start()
            loads.append(triple)

        totals[0].wait()
        crossing = []
        for j in range(1, ny):
            other = lax.rem(spot.y + j, ny) * 2
            copy = remote(
                r.sum.at[pl.ds(other, 2)], r.far.at[j - 1], r.fsem.at[j - 1, 0], r.fsem.at[j - 1, 1],
                spot.across(j),
            )
            copy.start()
            crossing.append(copy)

        r.nrm[...] = jnp.zeros_like(r.nrm)
        row = lax.broadcasted_iota(jnp.int32, (24, 128), 0)
        lane = lax.broadcasted_iota(jnp.int32, (24, 128), 1)
        first_piece = piece_rows(shapes)
        loaded = set()

        def load(i):
            if i not in loaded:
                loaded.add(i)
                for copy in loads[i]:
                    copy.wait()

        def small_norm(i, weight):
            load(i)
            master = get("w", i)[:, 0, :]
            mean, square = moments_of(get("g", i)[0], get("n", i)[0], get("q", i)[0], r.rates)
            move = direction_of(mean, square, master, r.rates, entries[i][3])
            for column, values in enumerate((master, move)):
                value = jnp.sum(values * values, axis=1, keepdims=True) * weight
                if i == 6:
                    value = jnp.sum(value, axis=0, keepdims=True)
                at = first_piece[i]
                r.nrm[at : at + value.shape[0], column : column + 1] = value

        def norm(i, p):
            load(i)
            step = tile_rows(shapes[i])
            zero = jnp.zeros((8, shapes[i][-1]), F32)

            def tile(j, carry):
                rs = pl.ds(pl.multiple_of(j * step, step), step)
                master = get("w", i)[p, rs, :]
                mean, square = moments_of(
                    get("g", i)[p, rs, :], get("n", i)[p, rs, :], get("q", i)[p, rs, :], r.rates
                )
                move = direction_of(mean, square, master, r.rates, entries[i][3])
                return (carry[0] + eighths(master * master), carry[1] + eighths(move * move))

            sums_of = lax.fori_loop(0, shapes[i][-2] // step, tile, (zero, zero))
            here = row == first_piece[i] + p
            for column, total in enumerate(sums_of):
                value = jnp.sum(jnp.sum(total, axis=0, keepdims=True), axis=1, keepdims=True)
                r.nrm[...] += jnp.where(jnp.logical_and(here, lane == column), value, 0.0)

        slow = [spot.slow(j) for j in range(1, dims.na)]
        fast = [spot.fast(j) for j in range(1, dims.nb)]
        taps_relays[0].start(r, spot.a, slow, r.kp[...])
        for copy in grads:
            copy.wait()
        flip(r.g3.at[0], r.mix, dims)
        flip(r.g5.at[0], r.mer, dims)
        jobs[6].advance()
        jobs[0].advance()

        for copy in totals[1:]:
            copy.wait()
        for p in range(3):
            norm(2, p)
        for copy in crossing:
            copy.wait_recv()
        jobs[7].advance()
        jobs[1].advance()
        r.dg0[...] = jnp.zeros_like(r.dg0)
        for i in range(2):

            def rows(j, i=i):
                rs = rows_of(j)
                total = r.sum[spot.y * 2 + i, rs, :].astype(F32)
                for other in range(ny - 1):
                    total = total + r.far[other, i, rs, :].astype(F32)
                xhat, inverse = unit(r.h[i, rs, :].astype(F32))
                r.dg0[...] += fold(total * xhat)
                back = r.gh[i, rs, :] + unit_back(total, xhat, inverse, r.g[...])
                r.both[i, rs, :] = back.astype(BF16)

            loop(Q // STEP, rows, 2)
        keep = pltpu.make_async_copy(r.both.at[spot.c], r.gin.at[spot.c], r.psem.at[3])
        keep.start()
        give = remote(
            r.both.at[1 - spot.c], r.gin.at[spot.c], r.bsem.at[0], r.bsem.at[1], spot.sibling()
        )
        give.start()

        r.gains[...] = jnp.zeros_like(r.gains)
        for k, ref in enumerate((r.dg0, r.d0, r.d1, r.d2, r.d3)):
            r.gains[k : k + 1, :] = jnp.sum(ref[...], axis=0, keepdims=True)
        gains_relays[0].start(r, spot.c, [spot.sibling()], r.gains[...])
        jobs[0].advance()
        jobs[2].advance()
        total = gains_relays[0].finish()
        gains_relays[1].start(r, spot.y, [spot.across(j) for j in range(1, ny)], total)
        norm(3, 0)
        for p in range(2):
            norm(4, p)
        norm(5, 0)
        jobs[1].advance()
        jobs[3].advance()
        total = gains_relays[1].finish()
        gains_relays[2].start(r, spot.a, slow, total)
        total = taps_relays[0].finish()
        taps_relays[1].start(r, spot.b, fast, total)
        flip(r.g1.at[1], r.shr1, dims)
        norm(1, 1)
        jobs[0].finish()
        jobs[2].advance()
        jobs[4].advance()
        total = gains_relays[2].finish()
        gains_relays[3].start(r, spot.b, fast, total)
        norm(0, 1)
        jobs[1].finish()
        jobs[3].advance()
        jobs[5].advance()
        jobs[2].finish()
        r.g6[0] = taps_relays[1].finish()
        owner = jnp.where(spot.d == 0, 1.0, 0.0)
        small_norm(6, owner)
        jobs[4].advance()
        jobs[3].finish()
        flip(r.g1.at[0], r.shr0, dims)
        jobs[6].advance()
        r.gains[...] = gains_relays[3].finish()
        owner = jnp.where(spot.t == 0, owner, 0.0)
        r.g7[0] = r.gains[0:5, :]
        small_norm(7, owner)
        jobs[5].advance()
        jobs[7].advance()
        norm(1, 0)
        for job in jobs[4:]:
            job.finish()
        norm(0, 0)
        norm_relays[0].start(r, spot.t, everyone, r.nrm[...])
        total = norm_relays[0].finish()
        norm_relays[1].start(r, spot.d, items, total)
        r.norms[...] = norm_relays[1].finish()
        keep.wait()
        give.wait()
        for copy in crossing:
            copy.wait_send()

    return call(body, ins, outs, scratch, cid)


def update_kernel(dims, rates, norms, entries, grads, frames, frames_grad):
    count = len(entries)
    shapes = [entry[1].shape for entry in entries]
    like = (dims.L, dims.D)
    ins = dict(
        rates=(rates, SM),
        norms=(norms, VM),
        fo=(frames.reshape(like), HB),
        fg=(frames_grad.reshape(like), HB),
    )
    outs = dict(trust=((2, 17), F32, VM), frames=(like, BF16, HB), gin=(like, BF16, HB))
    scratch = dict(isem=SEMS((count, 4)), osem=SEMS((count, 5)), fsem=SEMS((4,)), rows=VM((2,) + like, BF16))
    for i, (params, mean, square, _) in enumerate(entries):
        tag = str(i)
        shape = shapes[i]
        pair = params.shape
        ins |= {"p" + tag: (params, HB), "m" + tag: (mean, HB), "v" + tag: (square, HB)}
        ins |= {"g" + tag: (grads[i], HB)}
        scratch |= {"w" + tag: VM(pair, F32), "n" + tag: VM(shape, F32)}
        scratch |= {"q" + tag: VM(shape, F32), "h" + tag: VM(shape, F32)}
        scratch |= {"b" + tag: VM(pair, BF16)}
        outs |= {"og" + tag: (shape, F32, HB), "om" + tag: (shape, F32, HB)}
        outs |= {"ov" + tag: (shape, F32, HB), "ow" + tag: (pair, F32, HB)}
        outs |= {"ob" + tag: (pair, BF16, HB)}
    order = [2, 4, 3, 5, 7, 6, 1, 0]

    def body(r):
        get = lambda name, i: getattr(r, name + str(i))
        loads, stores = {}, []
        for i in order:
            moves = (("g", "h"), ("m", "n"), ("v", "q"), ("p", "w"))
            loads[i] = [
                pltpu.make_async_copy(get(source, i), get(target, i), r.isem.at[i, k])
                for k, (source, target) in enumerate(moves)
            ]
            for copy in loads[i]:
                copy.start()
        staged = []
        for k, source in enumerate((r.fo, r.fg)):
            staged.append(pltpu.make_async_copy(source, r.rows.at[k], r.fsem.at[k]))
            staged[k].start()
        norms = jnp.sqrt(r.norms[...])
        r.trust[...] = norms.T[:2, :17]
        ratio = r.rates[3] * norms[:, 0:1] / norms[:, 1:2]

        def send(i, name, target, k):
            copy = pltpu.make_async_copy(get(name, i), get(target, i), r.osem.at[i, k])
            copy.start()
            stores.append(copy)

        def update(i, grad, mean, square, master, average, scale):
            mean, square = moments_of(grad, mean, square, r.rates)
            move = direction_of(mean, square, master, r.rates, entries[i][3])
            master = master - scale * move
            average = r.rates[2] * average + (1.0 - r.rates[2]) * master
            return mean, square, master, average

        for i in order:
            for copy in loads[i]:
                copy.wait()
            send(i, "h", "og", 0)
            offset = piece_rows(shapes)[i]
            if i > 5:
                weights = get("w", i)
                scale = ratio[offset : offset + (1 if i == 6 else shapes[i][1]), :]
                mean, square, master, average = update(
                    i, get("h", i)[0], get("n", i)[0], get("q", i)[0], weights[:, 0, :],
                    weights[:, 1, :], scale,
                )
                get("n", i)[0] = mean
                get("q", i)[0] = square
                for slot, values in enumerate((master, average)):
                    weights[:, slot, :] = values
                get("b", i)[...] = weights[...].astype(BF16)
            else:
                step = tile_rows(shapes[i])
                for p in range(shapes[i][0]):
                    scale = ratio[offset + p : offset + p + 1, :]

                    def tile(j, p=p, i=i, step=step, scale=scale):
                        rs = pl.ds(pl.multiple_of(j * step, step), step)
                        mean, square, master, average = update(
                            i, get("h", i)[p, rs, :], get("n", i)[p, rs, :], get("q", i)[p, rs, :],
                            get("w", i)[0, p, rs, :], get("w", i)[1, p, rs, :], scale,
                        )
                        get("n", i)[p, rs, :] = mean
                        get("q", i)[p, rs, :] = square
                        get("w", i)[0, p, rs, :] = master
                        get("w", i)[1, p, rs, :] = average
                        get("b", i)[0, p, rs, :] = master.astype(BF16)
                        get("b", i)[1, p, rs, :] = average.astype(BF16)

                    loop(shapes[i][-2] // step, tile)
            send(i, "n", "om", 1)
            send(i, "q", "ov", 2)
            send(i, "w", "ow", 3)
            send(i, "b", "ob", 4)
            if i == order[0]:
                for k, target in enumerate((r.frames, r.gin)):
                    staged[k].wait()
                    copy = pltpu.make_async_copy(r.rows.at[k], target, r.fsem.at[2 + k])
                    copy.start()
                    stores.append(copy)
        for copy in stores:
            copy.wait()

    return call(body, ins, outs, scratch, None)


def shards(
    dims,
    frames_input,
    out_grad,
    lengths,
    step_count,
    rates,
    expand_params,
    expand_first,
    expand_second,
    shrink_params,
    shrink_first,
    shrink_second,
    project_params,
    project_first,
    project_second,
    mixing_params,
    mixing_first,
    mixing_second,
    gating_params,
    gating_first,
    gating_second,
    kernel_params,
    kernel_first,
    kernel_second,
    merging_params,
    merging_first,
    merging_second,
    gains_params,
    gains_first,
    gains_second,
):
    local_rows, width = frames_input.shape
    shard_rows = expand_params.shape[2]
    dims = SimpleNamespace(
        L=local_rows,
        D=width,
        S=local_rows * dims.ny * 2,
        F=expand_params.shape[3],
        H=project_params.shape[3],
        C=gating_params.shape[3],
        Q=local_rows // 2,
        nc=dims.ny * 2,
        **vars(dims),
    )
    gain = [gains_params[0, i : i + 1] for i in range(5)]
    taps = jnp.swapaxes(kernel_params, 0, 1)
    front = front_kernel(
        dims, 1, frames_input, out_grad, lengths, gain, expand_params, shrink_params,
        project_params, mixing_params, gating_params, merging_params,
    )
    middle = middle_kernel(dims, 2, front, lengths, taps, gain, shard_rows)
    last = last_kernel(dims, 4, front, middle, lengths, gain, shard_rows)

    steps_done = step_count[0].astype(F32)
    scalars = jnp.concatenate(
        [rates, 1.0 / (1.0 - rates[:2] ** steps_done), jnp.zeros((2,), F32)]
    )
    one = lambda params, first, second: (params[:, None], first[None], second[None], DECAY_RATE)
    entries = [
        (expand_params, expand_first, expand_second, DECAY_RATE),
        (shrink_params, shrink_first, shrink_second, DECAY_RATE),
        (project_params, project_first, project_second, DECAY_RATE),
        one(mixing_params, mixing_first, mixing_second),
        (gating_params, gating_first, gating_second, DECAY_RATE),
        one(merging_params, merging_first, merging_second),
        (taps, kernel_first[None], kernel_second[None], DECAY_RATE),
        (jnp.swapaxes(gains_params, 0, 1), gains_first[None], gains_second[None], 0.0),
    ]
    summed = gradient_kernel(
        dims, 3, scalars, entries, [last["dr"], last["de"]],
        [middle["oute"], middle["outr"], last["sa"], last["sc"], last["oute"]],
        [last["dg1"], middle["dg2"], middle["dg3"], middle["dg4"]], middle["dk"],
        last["part"], last["gh"], front["xh"], gain[0],
    )
    updated = update_kernel(
        dims, scalars, summed["norms"], entries, [summed["g" + str(i)] for i in range(8)],
        middle["fo"], summed["gin"],
    )
    results = []
    firsts = (
        expand_first, shrink_first, project_first, mixing_first, gating_first, kernel_first,
        merging_first, gains_first,
    )
    for place in range(8):
        entry = PLACES.index(place)
        like = firsts[place].shape
        tag = str(entry)
        results += [updated[name + tag].reshape(like) for name in ("og", "om", "ov")]
        for name in ("ow", "ob"):
            pair = updated[name + tag]
            results.append(jnp.swapaxes(pair, 0, 1) if entry > 5 else pair.reshape((2,) + like))
    return (updated["frames"], updated["gin"], *results, updated["trust"].T)


def solution(mesh):
    slow = math.gcd(mesh.shape["dp"], 4)
    dims = SimpleNamespace(na=slow, nb=mesh.shape["dp"] // slow, ny=mesh.shape["tensor"] // 2)
    return jax.shard_map(
        functools.partial(shards, dims),
        mesh=mesh,
        in_specs=(
            P(("dp", "tensor"), None),
            P(("dp", "tensor"), None),
            P("dp"),
            P(),
            P(),
            P(None, None, "dp", "tensor"),
            P(None, "dp", "tensor"),
            P(None, "dp", "tensor"),
            P(None, None, "tensor", "dp"),
            P(None, "tensor", "dp"),
            P(None, "tensor", "dp"),
            P(None, None, "dp", "tensor"),
            P(None, "dp", "tensor"),
            P(None, "dp", "tensor"),
            P(None, "tensor", "dp"),
            P("tensor", "dp"),
            P("tensor", "dp"),
            P(None, None, "dp", "tensor"),
            P(None, "dp", "tensor"),
            P(None, "dp", "tensor"),
            P(None, None, "tensor"),
            P(None, "tensor"),
            P(None, "tensor"),
            P(None, "tensor", "dp"),
            P("tensor", "dp"),
            P("tensor", "dp"),
            P(),
            P(),
            P(),
        ),
        out_specs=(
            P(("dp", "tensor"), None),
            P(("dp", "tensor"), None),
            P(None, "dp", "tensor"),
            P(None, "dp", "tensor"),
            P(None, "dp", "tensor"),
            P(None, None, "dp", "tensor"),
            P(None, None, "dp", "tensor"),
            P(None, "tensor", "dp"),
            P(None, "tensor", "dp"),
            P(None, "tensor", "dp"),
            P(None, None, "tensor", "dp"),
            P(None, None, "tensor", "dp"),
            P(None, "dp", "tensor"),
            P(None, "dp", "tensor"),
            P(None, "dp", "tensor"),
            P(None, None, "dp", "tensor"),
            P(None, None, "dp", "tensor"),
            P("tensor", "dp"),
            P("tensor", "dp"),
            P("tensor", "dp"),
            P(None, "tensor", "dp"),
            P(None, "tensor", "dp"),
            P(None, "dp", "tensor"),
            P(None, "dp", "tensor"),
            P(None, "dp", "tensor"),
            P(None, None, "dp", "tensor"),
            P(None, None, "dp", "tensor"),
            P(None, "tensor"),
            P(None, "tensor"),
            P(None, "tensor"),
            P(None, None, "tensor"),
            P(None, None, "tensor"),
            P("tensor", "dp"),
            P("tensor", "dp"),
            P("tensor", "dp"),
            P(None, "tensor", "dp"),
            P(None, "tensor", "dp"),
            P(),
            P(),
            P(),
            P(),
            P(),
            P(),
        ),
        check_vma=False,
    )
```

```python
import functools
import math
from types import SimpleNamespace

import jax
import jax.numpy as jnp
from jax import lax
from jax.experimental import pallas as pl
from jax.experimental.pallas import tpu as pltpu
from jax.sharding import PartitionSpec as P

HEAD_DIM = 64
KERNEL = 31

EPSILON = 1e-05
ADAM_EPS = 1e-06
DECAY_RATE = 0.01
MASKED = -1000000000.0

F32 = jnp.float32
BF16 = jnp.bfloat16
MESH = pl.DeviceIdType.MESH
STEP = 16
TILE = 256
GRANT = 60 * 1024 * 1024


class Spot:
    def __init__(self, dims):
        self.dims = dims
        self.d = lax.axis_index("dp")
        self.t = lax.axis_index("tensor")
        self.y = lax.div(self.t, 2)
        self.c = lax.rem(self.t, 2)
        self.a = lax.div(self.d, dims.nb)
        self.b = lax.rem(self.d, dims.nb)

    def sibling(self):
        return (self.d, self.y * 2 + 1 - self.c)

    def across(self, j):
        return (self.d, lax.rem(self.y + j, self.dims.ny) * 2 + self.c)

    def slow(self, j):
        return (lax.rem(self.a + j, self.dims.na) * self.dims.nb + self.b, self.t)

    def fast(self, j):
        return (self.a * self.dims.nb + lax.rem(self.b + j, self.dims.nb), self.t)

    def tensor_peers(self):
        return [self.sibling()] + [self.across(j) for j in range(1, self.dims.ny)]

    def data_peers(self):
        return [self.slow(j) for j in range(1, self.dims.na)] + [
            self.fast(j) for j in range(1, self.dims.nb)
        ]


def greet(peers):
    barrier = pltpu.get_barrier_semaphore()
    for peer in peers:
        pl.semaphore_signal(barrier, 1, device_id=peer, device_id_type=MESH)
    pl.semaphore_wait(barrier, len(peers))


def remote(source, target, send, recv, peer):
    return pltpu.make_async_remote_copy(
        src_ref=source,
        dst_ref=target,
        send_sem=send,
        recv_sem=recv,
        device_id=peer,
        device_id_type=MESH,
    )


def loop(count, body, unroll=1):
    def step(i, carry):
        body(i)
        return carry

    lax.fori_loop(0, count, step, 0, unroll=unroll)


def rows_of(i, step=STEP):
    return pl.ds(pl.multiple_of(i * step, step), step)


class Refs(SimpleNamespace):
    def need(self, *names):
        for name in names:
            if name in self.pending:
                self.pending.pop(name).wait()

    def done(self, *names):
        for name in names:
            copy = self.unsent.pop(name)
            copy.start()
            self.leaving.append(copy)

    def close(self):
        self.need(*list(self.pending))
        self.done(*list(self.unsent))
        for copy in self.leaving:
            copy.wait()


def call(body, ins, outs, scratch, cid):
    in_names, out_names, scratch_names = list(ins), list(outs), list(scratch)
    loads = [name for name in in_names if ins[name][1] in (LD, LD0)]
    stores = [name for name in out_names if outs[name][2] is ST]
    whole = {name: ins[name][1] is LD for name in loads}
    copies = [
        VM(ins[name][0].shape[0 if whole[name] else 1 :], ins[name][0].dtype) for name in loads
    ]
    copies += [VM(outs[name][0], outs[name][1]) for name in stores]
    sems = [SEMS((max(len(copies), 1),))]

    def place(space):
        return pl.BlockSpec(memory_space=HB if space in (LD, LD0, ST) else space)

    def kernel(*refs):
        names = in_names + out_names + scratch_names
        given = dict(zip(names, refs))
        held = refs[len(names) : -1]
        r = Refs(**given, pending={}, unsent={}, leaving=[])
        for i, name in enumerate(loads):
            source = given[name] if whole[name] else given[name].at[0]
            r.pending[name] = pltpu.make_async_copy(source, held[i], refs[-1].at[i])
            setattr(r, name, held[i])
        for i, name in enumerate(stores, len(loads)):
            r.unsent[name] = pltpu.make_async_copy(held[i], given[name], refs[-1].at[i])
            setattr(r, name, held[i])
        for copy in r.pending.values():
            copy.start()
        body(r)
        r.close()

    results = pl.pallas_call(
        kernel,
        out_shape=[jax.ShapeDtypeStruct(shape, kind) for shape, kind, _ in outs.values()],
        in_specs=[place(space) for _, space in ins.values()],
        out_specs=[place(space) for _, _, space in outs.values()],
        scratch_shapes=list(scratch.values()) + copies + sems,
        compiler_params=pltpu.CompilerParams(
            collective_id=cid, has_side_effects=cid is not None, vmem_limit_bytes=GRANT
        ),
    )(*[array for array, _ in ins.values()])
    return dict(zip(out_names, results))


LD, LD0, ST = object(), object(), object()
VM = pltpu.VMEM
HB = pl.ANY
SM = pltpu.SMEM
SEMS = pltpu.SemaphoreType.DMA


def tagged(prefix, tag, specs):
    return {prefix + name + tag: spec for name, spec in specs.items()}


def bound(refs, prefix, tag, specs):
    return SimpleNamespace(**{name: getattr(refs, prefix + name + tag) for name in specs})


class Gather:
    def __init__(self, tag, dims):
        self.tag, self.dims = tag, dims
        na, nb = dims.na, dims.nb
        m, k = max(nb - 1, 1), max(na - 1, 1)
        self.specs = dict(
            loc=SEMS,
            xs=SEMS((m,)),
            xr=SEMS((m,)),
            us=SEMS((k,)),
            ur=SEMS((k,)),
            ds=SEMS((k,)),
            dr=SEMS((k,)),
            fs=SEMS((2, k, m)),
            fr=SEMS((2, k, m)),
        )
        self.stage = 0

    def scratch(self):
        return tagged("g", self.tag, self.specs)

    def bind(self, refs, spot, source, whole, columns=None):
        self.sem = bound(refs, "g", self.tag, self.specs)
        self.spot, self.source, self.whole, self.columns = spot, source, whole, columns
        return self

    def rows(self, d):
        shard = self.source.shape[0]
        rows = pl.ds(pl.multiple_of(d * shard, shard), shard)
        return self.whole.at[rows] if self.columns is None else self.whole.at[rows, self.columns]

    def block(self, a):
        return self.rows(a * self.dims.nb + self.spot.b)

    def hop(self, way, s):
        spot, sem = self.spot, self.sem
        step = 1 if way == 0 else -1
        target = self.block(spot.a - step * (s - 1))
        source = self.source if s == 1 else target
        send, recv = (sem.us, sem.ur) if way == 0 else (sem.ds, sem.dr)
        peer = ((spot.a + step) * self.dims.nb + spot.b, spot.t)
        return remote(source, target, send.at[s - 1], recv.at[s - 1], peer)

    def sends(self, way, s):
        spot, na = self.spot, self.dims.na
        if way == 0:
            return jnp.logical_and(spot.a - (s - 1) >= 0, spot.a + 1 < na)
        return jnp.logical_and(spot.a + (s - 1) < na, spot.a - 1 >= 0)

    def has(self, way, s):
        return self.spot.a - s >= 0 if way == 0 else self.spot.a + s < self.dims.na

    def hand(self, way, s, i):
        block = self.block(self.spot.a - s if way == 0 else self.spot.a + s)
        sem = self.sem
        return remote(
            block, block, sem.fs.at[way, s - 1, i - 1], sem.fr.at[way, s - 1, i - 1], self.spot.fast(i)
        )

    def start(self):
        spot, dims, sem = self.spot, self.dims, self.sem
        mine = self.rows(spot.d)
        if dims.na > 1:
            for way in range(2):

                @pl.when(self.sends(way, 1))
                def _(way=way):
                    self.hop(way, 1).start()

        self.own = [
            remote(self.source, mine, sem.xs.at[j - 1], sem.xr.at[j - 1], spot.fast(j))
            for j in range(1, dims.nb)
        ]
        for copy in self.own:
            copy.start()
        self.local = pltpu.make_async_copy(self.source, mine, sem.loc)
        self.local.start()

    def advance(self):
        dims = self.dims
        self.stage += 1
        s = self.stage
        if s >= dims.na:
            return False
        for way in range(2):

            @pl.when(self.has(way, s))
            def _(way=way):
                self.hop(way, s).wait_recv()
                for i in range(1, dims.nb):
                    self.hand(way, s, i).start()

            if s + 1 < dims.na:

                @pl.when(self.sends(way, s + 1))
                def _(way=way):
                    self.hop(way, s + 1).start()

        return True

    def finish(self):
        dims = self.dims
        while self.advance():
            pass
        self.local.wait()
        for copy in self.own:
            copy.wait()
        for s in range(1, dims.na):
            for way in range(2):

                @pl.when(self.sends(way, s))
                def _(way=way, s=s):
                    self.hop(way, s).wait_send()

                @pl.when(self.has(way, s))
                def _(way=way, s=s):
                    for i in range(1, dims.nb):
                        self.hand(way, s, i).wait()


class FastGather(Gather):
    def block(self, a):
        rows = self.source.shape[0] * self.dims.nb
        at = pl.ds(pl.multiple_of(a * rows, rows), rows)
        return self.whole.at[at] if self.columns is None else self.whole.at[at, self.columns]

    def hop(self, way, s):
        spot, sem = self.spot, self.sem
        step = 1 if way == 0 else -1
        block = self.block(spot.a - step * (s - 1))
        send, recv = (sem.us, sem.ur) if way == 0 else (sem.ds, sem.dr)
        peer = ((spot.a + step) * self.dims.nb + spot.b, spot.t)
        return remote(block, block, send.at[s - 1], recv.at[s - 1], peer)

    def start(self):
        spot, dims, sem = self.spot, self.dims, self.sem
        mine = self.rows(spot.d)
        self.own = [
            remote(self.source, mine, sem.xs.at[j - 1], sem.xr.at[j - 1], spot.fast(j))
            for j in range(1, dims.nb)
        ]
        self.local = pltpu.make_async_copy(self.source, mine, sem.loc)
        for copy in self.own + [self.local]:
            copy.start()
        self.stage = -1

    def advance(self):
        dims = self.dims
        self.stage += 1
        s = self.stage
        if s >= dims.na:
            return False
        if s == 0:
            self.local.wait()
            for copy in self.own:
                copy.wait_recv()
        for way in range(2):
            if s > 0:

                @pl.when(self.has(way, s))
                def _(way=way):
                    self.hop(way, s).wait_recv()

            if s + 1 < dims.na:

                @pl.when(self.sends(way, s + 1))
                def _(way=way):
                    self.hop(way, s + 1).start()

        return True

    def finish(self):
        while self.advance():
            pass
        for copy in self.own:
            copy.wait_send()
        for s in range(1, self.dims.na):
            for way in range(2):

                @pl.when(self.sends(way, s))
                def _(way=way, s=s):
                    self.hop(way, s).wait_send()


class Scatter:
    def __init__(self, tag, dims, rows, first, columns, into=None, slow_first=False):
        self.tag, self.dims, self.size = tag, dims, (rows, columns)
        self.columns = pl.ds(first, columns)
        self.into = self.columns if into is None else pl.ds(into, columns)
        self.slow_first = slow_first
        na, nb = dims.na, dims.nb
        m, half = max(nb - 1, 1), na // 2
        one = (half, nb) if slow_first else (m, na)
        two = (m, half) if slow_first else (half,)
        self.specs = dict(
            held=VM(((half, nb) if slow_first else (na,)) + self.size, BF16),
            one=VM(one + self.size, BF16),
            two=VM(two + self.size, BF16),
            three=VM(self.size, BF16),
            loc=SEMS((half,)),
            xs=SEMS((m,)),
            xr=SEMS((m,)),
            zs=SEMS((half,)),
            zr=SEMS((half,)),
            ls=SEMS,
            lr=SEMS,
        )
        self.stage = 0

    def scratch(self):
        return tagged("s", self.tag, self.specs)

    def bind(self, refs, spot, source, result):
        self.r = bound(refs, "s", self.tag, self.specs)
        self.spot, self.source, self.result = spot, source, result
        self.low, self.high = lax.rem(spot.a, 2), lax.div(spot.a, 2)
        return self

    def blocks(self, low):
        return [low + 2 * i for i in range(self.dims.na // 2)]

    def place(self, high, low):
        return (high * 2 + low) * self.dims.nb + self.spot.b, self.spot.t

    def neighbour(self):
        return self.place(self.high, 1 - self.low)

    def sum_rows(self, target, *parts):
        def add(i):
            rs = rows_of(i)
            total = target[rs, :].astype(F32)
            for part in parts:
                total = total + part[rs, :].astype(F32)
            target[rs, :] = total.astype(BF16)

        loop(self.size[0] // STEP, add, 2)

    def start(self):
        spot, dims, r = self.spot, self.dims, self.r
        self.sent, self.local = [], []
        if self.slow_first:
            for i, a in enumerate(self.blocks(1 - self.low)):
                self.sent.append(
                    remote(
                        self.source.at[a, :, :, self.columns], r.one.at[i], r.zs.at[i], r.zr.at[i],
                        self.neighbour(),
                    )
                )
            for i, a in enumerate(self.blocks(self.low)):
                self.local.append(
                    pltpu.make_async_copy(
                        self.source.at[a, :, :, self.columns], r.held.at[i], r.loc.at[i]
                    )
                )
        else:
            for j in range(1, dims.nb):
                block = lax.rem(spot.b + j, dims.nb)
                self.sent.append(
                    remote(
                        self.source.at[:, block, :, self.columns], r.one.at[j - 1], r.xs.at[j - 1],
                        r.xr.at[j - 1], spot.fast(j),
                    )
                )
            self.local.append(
                pltpu.make_async_copy(
                    self.source.at[:, spot.b, :, self.columns], r.held, r.loc.at[0]
                )
            )
        for copy in self.sent + self.local:
            copy.start()

    def advance(self):
        spot, dims, r = self.spot, self.dims, self.r
        half = dims.na // 2
        self.stage += 1
        if self.stage == 1:
            for copy in self.local:
                copy.wait()
            for copy in self.sent:
                copy.wait_recv()
            self.pair = []
            if self.slow_first:
                for i in range(half):
                    for b in range(dims.nb):
                        self.sum_rows(r.held.at[i, b], r.one.at[i, b])
                for j in range(1, dims.nb):
                    block = lax.rem(spot.b + j, dims.nb)
                    self.pair.append(
                        remote(
                            r.held.at[:, block], r.two.at[j - 1], r.xs.at[j - 1], r.xr.at[j - 1],
                            spot.fast(j),
                        )
                    )
            else:
                for a in range(dims.na):
                    self.sum_rows(r.held.at[a], *[r.one.at[j, a] for j in range(dims.nb - 1)])
                for i, a in enumerate(self.blocks(1 - self.low)):
                    self.pair.append(
                        remote(r.held.at[a], r.two.at[i], r.zs.at[i], r.zr.at[i], self.neighbour())
                    )
            for copy in self.pair:
                copy.start()
            return True
        if self.stage == 2:
            for copy in self.pair:
                copy.wait()
            if self.slow_first:
                for i in range(half):
                    self.sum_rows(
                        r.held.at[i, spot.b], *[r.two.at[j, i] for j in range(dims.nb - 1)]
                    )
                away, self.mine = r.held.at[1 - self.high, spot.b], r.held.at[self.high, spot.b]
            else:
                for i, a in enumerate(self.blocks(self.low)):
                    self.sum_rows(r.held.at[a], r.two.at[i])
                away = r.held.at[(1 - self.high) * 2 + self.low]
                self.mine = r.held.at[spot.a]
            self.final = remote(away, r.three, r.ls, r.lr, self.place(1 - self.high, self.low))
            self.final.start()
            return True
        return False

    def finish(self):
        while self.advance():
            pass
        r = self.r
        self.final.wait()

        def add(i):
            rs = rows_of(i)
            total = self.mine[rs, :].astype(F32) + r.three[rs, :].astype(F32)
            self.result[rs, self.into] = total

        loop(self.size[0] // STEP, add, 2)
        for copy in self.sent:
            copy.wait_send()


class Edge:
    def __init__(self, dims, count):
        self.dims, self.count = dims, count

    def scratch(self):
        nc, Q, D, count = self.dims.nc, self.dims.Q, self.dims.D, self.count
        m = max(self.dims.ny - 1, 1)
        return dict(
            e_own=VM((nc, Q, D), F32),
            e_give=VM((nc, Q, D), BF16),
            e_take=VM((nc, Q, D), BF16),
            e_sum=VM((nc, Q, D), BF16),
            e_far=VM((min(count, 2), m, nc, Q, D), BF16),
            e_ds=SEMS((count, nc)),
            e_dr=SEMS((count, nc)),
            e_ys=SEMS((count, m, nc)),
            e_yr=SEMS((count, m, nc)),
            e_ns=SEMS((count, nc)),
            e_nr=SEMS((count, nc)),
        )

    def bind(self, refs, spot):
        self.refs, self.spot = refs, spot
        self.near, self.far, self.handed = {}, {}, {}
        return self

    def open(self, i, k):
        if i > 0:
            self.near.pop((i - 1, k)).wait_send()

    def put(self, k, columns, part):
        Q, refs = self.dims.Q, self.refs
        low, high = part[:Q], part[Q:]
        first = self.spot.c == 0
        refs.e_own[k, :, columns] = jnp.where(first, low, high)
        refs.e_give[k, :, columns] = jnp.where(first, high, low).astype(BF16)

    def start(self, i, k):
        refs = self.refs
        copy = remote(
            refs.e_give.at[k],
            refs.e_take.at[k],
            refs.e_ds.at[i, k],
            refs.e_dr.at[i, k],
            self.spot.sibling(),
        )
        copy.start()
        self.near[i, k] = copy

    def cross(self, i, k, send=True):
        refs, dims = self.refs, self.dims
        self.near[i, k].wait_recv()
        if i > 0:
            for copy in self.far.pop((i - 1, k)):
                copy.wait_send()

        def add(j):
            rs = rows_of(j)
            total = refs.e_own[k, rs, :] + refs.e_take[k, rs, :].astype(F32)
            refs.e_own[k, rs, :] = total
            refs.e_sum[k, rs, :] = total.astype(BF16)

        loop(dims.Q // STEP, add, 2)
        if send:
            self.far[i, k] = []
            for j in range(1, dims.ny):
                copy = remote(
                    refs.e_sum.at[k],
                    refs.e_far.at[i % 2, j - 1, k],
                    refs.e_ys.at[i, j - 1, k],
                    refs.e_yr.at[i, j - 1, k],
                    self.spot.across(j),
                )
                copy.start()
                self.far[i, k].append(copy)

    def total(self, i, k, rs, slot):
        refs = self.refs
        total = refs.e_own[k, rs, :]
        for j in range(self.dims.ny - 1):
            total = total + refs.e_far[i % 2, j, slot, rs, :].astype(F32)
        return total

    def settle(self, i, k, row_fn, target):
        refs, dims, spot = self.refs, self.dims, self.spot
        for copy in self.far[i, k]:
            copy.wait_recv()
        base = (k * 2 + spot.c) * dims.Q

        def body(j):
            rs = rows_of(j)
            rows = row_fn(self.total(i, k, rs, k), k, rs)
            target[pl.ds(pl.multiple_of(base + j * STEP, STEP), STEP), :] = rows

        loop(dims.Q // STEP, body, 2)
        block = target.at[pl.ds(pl.multiple_of(base, dims.Q), dims.Q)]
        copy = remote(block, block, refs.e_ns.at[i, k], refs.e_nr.at[i, k], spot.sibling())
        copy.start()
        self.handed[i, k] = copy

    def arrived(self, i, k):
        self.handed[i, k].wait_recv()

    def drain(self):
        for copy in list(self.near.values()) + list(self.handed.values()):
            copy.wait_send()
        for copies in self.far.values():
            for copy in copies:
                copy.wait_send()


def unit(hidden):
    center = hidden - jnp.mean(hidden, axis=-1, keepdims=True)
    spread = jnp.mean(center * center, axis=-1, keepdims=True)
    inverse = lax.rsqrt(spread + EPSILON)
    return center * inverse, inverse


def unit_back(upstream, xhat, inverse, gain):
    scaled = upstream * gain
    return inverse * (
        scaled
        - jnp.mean(scaled, axis=-1, keepdims=True)
        - xhat * jnp.mean(scaled * xhat, axis=-1, keepdims=True)
    )


def fold(rows):
    return rows[:8] + rows[8:]


def chunk_rows(dims, k):
    return pl.ds(k * dims.L, dims.L)


def up_products(dims, k, normed, expand, inner, slope):
    rows = chunk_rows(dims, k)

    def column(j):
        cs = rows_of(j, TILE)
        before = jnp.dot(normed[rows, :], expand[:, cs], preferred_element_type=F32)
        gate = jax.nn.sigmoid(before)
        inner[rows, cs] = (before * gate).astype(BF16)
        slope[rows, cs] = (gate * (1.0 + before * (1.0 - gate))).astype(BF16)

    loop(dims.F // TILE, column, True)


def back_products(dims, k, upstream, shrink, slope, back):
    rows = chunk_rows(dims, k)

    def column(j):
        cs = rows_of(j, TILE)
        part = jnp.dot(upstream[rows, :], shrink[:, cs], preferred_element_type=F32)
        back[rows, cs] = (part * slope[rows, cs].astype(F32)).astype(BF16)

    loop(dims.F // TILE, column, True)


def part_product(edge, i, k, operand, matrix, first, dims):
    width = operand.shape[1]
    edge.open(i, k)

    def column(j):
        cs = rows_of(j, TILE)
        edge.put(
            k,
            cs,
            lax.dot_general(
                operand[chunk_rows(dims, k), :],
                matrix[cs, pl.ds(first, width)],
                (((1,), (1,)), ((), ())),
                preferred_element_type=F32,
            ),
        )

    loop(dims.D // TILE, column, True)
    edge.start(i, k)


def weight_part(result, first, rows_side, columns_side, dims):
    width = columns_side.shape[1]
    shard = result.shape[2]
    for i in range(dims.D // TILE):
        part = lax.dot_general(
            rows_side[:, pl.ds(i * TILE, TILE)],
            columns_side[...],
            (((0,), (0,)), ((), ())),
            preferred_element_type=F32,
        ).astype(BF16)
        for j in range(TILE // shard):
            d = i * (TILE // shard) + j
            result[d // dims.nb, d % dims.nb, :, pl.ds(first, width)] = part[
                j * shard : (j + 1) * shard
            ]


def forward_rows(hidden, scale, gain, kept):
    def rows(total, k, rs):
        after = hidden[k, rs, :].astype(F32) + scale * total
        kept[k, rs, :] = after
        xhat, _ = unit(after)
        return (xhat * gain[...]).astype(BF16)

    return rows


def backward_rows(hidden, scale, gain, grad, sums, spot):
    def rows(total, k, rs):
        xhat, inverse = unit(hidden[k, rs, :].astype(F32))
        own = jnp.where(spot.y == k // 2, 1.0, 0.0)
        sums[...] += fold(total * xhat) * own
        after = grad[k, rs, :] + unit_back(total, xhat, inverse, gain[...])
        grad[k, rs, :] = after
        return (scale * after).astype(BF16)

    return rows


QUERIES = 256
BAND = 64
MARGIN = 16


def slide(padded, base, taps, flip=False):
    window = padded[pl.ds(pl.multiple_of(base, BAND), BAND + 2 * MARGIN), :]
    total = None
    for residue in range(8):
        shifted = window[residue : residue + BAND + 24]
        for eighth in range(4):
            tap = 8 * eighth + residue - 1
            if 0 <= tap < KERNEL:
                place = KERNEL - 1 - tap if flip else tap
                term = shifted[8 * eighth : 8 * eighth + BAND] * taps[place, 0:1, :]
                total = term if total is None else total + term
    return total


def clear_margins(padded, S):
    edge = jnp.zeros((MARGIN, padded.shape[1]), F32)
    padded[pl.ds(0, MARGIN), :] = edge
    padded[pl.ds(MARGIN + S, MARGIN), :] = edge


def attend(dims, k, r):
    H, m = dims.H, dims.L
    heads = H // HEAD_DIM
    blocks = m // min(QUERIES, m)
    size = m // blocks

    def one(i):
        head = lax.div(i, blocks)
        at = pl.ds(pl.multiple_of(k * m + lax.rem(i, blocks) * size, size), size)
        scores = lax.dot_general(
            r.k[head], r.q[head, at, :], (((1,), (1,)), ((), ())), preferred_element_type=F32
        )
        scores = scores + r.column[...]
        peak = jnp.max(scores, axis=0, keepdims=True)
        exponent = jnp.exp(scores - peak)
        total = jnp.sum(exponent, axis=0, keepdims=True)
        output = jnp.dot(r.vt[head], exponent.astype(BF16), preferred_element_type=F32)
        r.lse[head, :, at] = peak + jnp.log(total)
        r.ot[pl.ds(pl.multiple_of(head * HEAD_DIM, HEAD_DIM), HEAD_DIM), at] = output / total

    loop(heads * blocks, one)
    rows = chunk_rows(dims, k)
    r.oh[rows, :] = r.ot[:, rows].T.astype(BF16)


def live_column(r, S, dead):
    place = lax.broadcasted_iota(jnp.int32, (S, 1), 0)
    live, other = (0.0, MASKED) if dead else (1.0, 0.0)
    r.column[...] = jnp.where(place < r.lengths[0], live, other)


def front_kernel(
    dims, cid, frames, cotangent, lengths, gains, expand, shrink, project, mixing, gating, merging
):
    nc, L, Q, D, S, F, H, C = (
        dims.nc, dims.L, dims.Q, dims.D, dims.S, dims.F, dims.H, dims.C
    )
    heads = H // HEAD_DIM
    shard = expand.shape[2]
    edge = Edge(dims, 2)
    gathers = [Gather(str(i), dims) for i in range(5)]
    gathers += [FastGather(str(i), dims) for i in (5, 6)]
    half = F // 4
    scratch = edge.scratch() | dict(
        vt=VM((heads, HEAD_DIM, S), BF16),
        ot=VM((H, S), F32),
        column=VM((S, 1), F32),
        ogl=VM((2, Q, D), BF16),
        s0=VM((shard, F), BF16),
        s1=VM((shard, F - half), BF16),
        s6=VM((shard, half), BF16),
        s2=VM((shard, 4 * H), BF16),
        s3=VM((shard, 3 * C), BF16),
        s4=VM((shard, F), BF16),
        s5=VM((shard, half), BF16),
        xs=SEMS((nc,)),
        xr=SEMS((nc,)),
        os=SEMS((nc,)),
        orr=SEMS((nc,)),
        ns=SEMS((nc,)),
        nr=SEMS((nc,)),
    )
    for gather in gathers:
        scratch |= gather.scratch()

    def body(r):
        spot = Spot(dims)
        others = [(spot.d, lax.rem(spot.t + j, nc)) for j in range(1, nc)]
        greet(others + spot.data_peers())
        edge.bind(r, spot)
        for i, (source, whole) in enumerate(
            ((r.s0, r.e), (r.s1, r.rt), (r.s2, r.wa), (r.s3, r.wc), (r.s4, r.e1), (r.s5, r.ra))
        ):
            gathers[i].bind(r, spot, source, whole)
        most = F - half
        gathers[1].bind(r, spot, r.s1, r.rt, pl.ds(0, most))
        gathers[6].bind(r, spot, r.s6, r.rt, pl.ds(most, half))
        r.need("x")
        moves = []
        for j in range(1, nc):
            some = pl.ds(pl.multiple_of(lax.rem(spot.c + j, 2) * Q, Q), Q)
            copy = remote(
                r.x.at[some], r.xh.at[spot.t], r.xs.at[j - 1], r.xr.at[j - 1], others[j - 1]
            )
            copy.start()
            moves.append(copy)

        r.need("pe")
        r.s0[...] = r.pe[0].astype(BF16)
        gathers[0].start()
        r.need("pr")

        def turned(target, first, source, begin=0, count=None):
            def part(j):
                cs = pl.ds(pl.multiple_of(begin + j * 128, 128), 128)
                target[:, pl.ds(pl.multiple_of(first + j * 128, 128), 128)] = (
                    source[cs, :].T.astype(BF16)
                )

            loop((count or source.shape[0]) // 128, part, True)

        turned(r.s6, 0, r.pr.at[0], most, half)
        gathers[6].start()
        turned(r.s1, 0, r.pr.at[0], 0, most)
        gathers[1].start()
        mine = pl.ds(pl.multiple_of(spot.c * Q, Q), Q)
        r.xh[spot.t] = r.x[mine, :]

        handed = []

        def normalize(t):
            base = pl.multiple_of((t * 2 + spot.c) * Q, Q)

            def rows(i):
                xhat, _ = unit(r.xh[t, rows_of(i), :].astype(F32))
                target = pl.ds(pl.multiple_of(base + i * STEP, STEP), STEP)
                r.n1[target, :] = (xhat * r.g0[...]).astype(BF16)

            loop(Q // STEP, rows, 2)
            block = r.n1.at[pl.ds(base, Q)]
            i = len(handed)
            copy = remote(block, block, r.ns.at[i], r.nr.at[i], spot.sibling())
            copy.start()
            handed.append(copy)

        normalize(spot.t)
        r.need("og")
        place = lax.broadcasted_iota(jnp.int32, (Q, 1), 0) + spot.t * L
        for i in range(2):
            live = place + i * Q < r.lengths[0]
            r.ogl[i] = jnp.where(live, r.og[pl.ds(i * Q, Q), :].astype(F32), 0.0).astype(BF16)
        for j in range(1, nc):
            copy = remote(
                r.ogl.at[lax.rem(spot.c + j, 2)], r.ogh.at[spot.t], r.os.at[j - 1], r.orr.at[j - 1],
                others[j - 1],
            )
            copy.start()
            moves.append(copy)
        r.ogh[spot.t] = r.ogl[spot.c]
        gathers[6].advance()
        gathers[0].advance()
        gathers[1].advance()
        for j in range(1, nc):
            moves[j - 1].wait_recv()
            normalize(lax.rem(spot.t + nc - j, nc))
        gathers[6].advance()
        gathers[0].advance()
        gathers[1].advance()

        r.need("pp", "pm", "pg", "pz")
        for i in range(3):
            r.s2[:, pl.ds(i * H, H)] = r.pp[i].astype(BF16)
        turned(r.s2, 3 * H, r.pm)
        for i in range(2):
            r.s3[:, pl.ds(i * C, C)] = r.pg[i].astype(BF16)
        turned(r.s3, 2 * C, r.pz)
        r.s4[...] = r.pe[1].astype(BF16)
        turned(r.s5, 0, r.pr.at[1], 0, half)
        turned(r.r1, 0, r.pr.at[1], half, F - half)
        r.done("r1")
        live_column(r, S, True)
        gathers[6].advance()
        gathers[0].advance()
        gathers[1].advance()
        gathers[2].start()
        for copy in handed:
            copy.wait()
        gathers[0].finish()

        for k in range(nc):
            up_products(dims, k, r.n1, r.e, r.u, r.slope)
            if k == 0:
                gathers[6].finish()
                gathers[1].finish()
            part_product(edge, 0, k, r.u, r.rt, 0, dims)
            if k > 0:
                edge.cross(0, k - 1)
        edge.cross(0, nc - 1)
        r.done("u", "slope", "n1", "e", "rt")
        gathers[2].advance()
        for k in range(nc):
            edge.settle(0, k, forward_rows(r.xh, 0.5, r.g1, r.h1), r.n2)
            if k < 2:
                gathers[2].advance()
            if k == 1:
                gathers[3].start()
        gathers[3].advance()
        r.done("h1")
        for k in range(nc):
            edge.arrived(0, k)
        r.done("n2")
        gathers[2].finish()
        gathers[4].start()
        for i, target in enumerate((r.q, r.k, r.v)):
            packed = jnp.dot(r.n2[...], r.wa[:, pl.ds(i * H, H)], preferred_element_type=F32)
            if i == 0:
                packed = packed.astype(BF16).astype(F32) * HEAD_DIM**-0.5
            for j in range(heads):
                part = packed[:, j * HEAD_DIM : (j + 1) * HEAD_DIM]
                target[j] = part.astype(BF16)
                if i == 2:
                    r.vt[j] = part.T.astype(BF16)
        r.done("q", "k", "v", "wa")

        for k in range(nc):
            attend(dims, k, r)
            part_product(edge, 1, k, r.oh, r.wa, 3 * H, dims)
            if k > 0:
                edge.cross(1, k - 1)
            gathers[3 if k < 2 else 4].advance()
            if k == 1:
                gathers[5].start()
            elif k == 3:
                gathers[5].advance()
        edge.cross(1, nc - 1)
        r.done("oh", "lse")
        for k in range(nc):
            edge.settle(1, k, forward_rows(r.h1, 1.0, r.g2, r.h2), r.n3)
            gathers[4 if k == 0 else 5].advance()
        r.done("h2")
        for k in range(nc):
            edge.arrived(1, k)
        r.done("n3")
        for copy in moves[: nc - 1]:
            copy.wait_send()
        for copy in moves[nc - 1 :]:
            copy.wait()
        edge.drain()
        for gather in gathers[3:6]:
            gather.finish()

    triple = (heads, S, HEAD_DIM)
    rows_all, held = (S, D), (nc, Q, D)
    return call(
        body,
        dict(
            x=(frames, LD),
            pe=(expand, LD0),
            pr=(shrink, LD0),
            og=(cotangent, LD),
            pp=(project, LD0),
            pm=(mixing, LD0),
            pg=(gating, LD0),
            pz=(merging, LD0),
            lengths=(lengths, SM),
            g0=(gains[0], VM),
            g1=(gains[1], VM),
            g2=(gains[2], VM),
        ),
        dict(
            xh=(held, BF16, ST),
            ogh=(held, BF16, ST),
            n1=(rows_all, BF16, ST),
            e=((D, F), BF16, ST),
            rt=((D, F), BF16, ST),
            u=((S, F), BF16, ST),
            slope=((S, F), BF16, ST),
            h1=(held, F32, ST),
            n2=(rows_all, BF16, ST),
            q=(triple, BF16, ST),
            k=(triple, BF16, ST),
            v=(triple, BF16, ST),
            oh=((S, H), BF16, ST),
            lse=((heads, 1, S), F32, ST),
            h2=(held, F32, ST),
            n3=(rows_all, BF16, ST),
            wa=((D, 4 * H), BF16, ST),
            r1=((shard, F - half), BF16, ST),
            ra=((D, half), BF16, HB),
            wc=((D, 3 * C), BF16, HB),
            e1=((D, F), BF16, HB),
        ),
        scratch,
        cid,
    )


def middle_kernel(dims, cid, kept, lengths, taps, gains, shard):
    nc, Q, D, S, F, C = dims.nc, dims.Q, dims.D, dims.S, dims.F, dims.C
    m = dims.L
    edge = Edge(dims, 4)
    gather = Gather("0", dims)
    half = F // 2
    scatters = [Scatter(str(j), dims, shard, half * (j % 2), half) for j in range(3)]
    four = (dims.na, dims.nb, shard)
    scratch = edge.scratch() | gather.scratch()
    scratch |= dict(
        rt=VM((D, F), BF16),
        n4=VM((S, D), BF16),
        h3=VM((nc, Q, D), F32),
        fall=VM((nc, Q, D), BF16),
        column=VM((S, 1), F32),
        rsem=SEMS,
        fsem=SEMS((3,)),
        u=VM((S, F), BF16),
        slope=VM((S, F), BF16),
        w4=VM((S, D), BF16),
        dr=VM(four + (F,), BF16),
        w3=VM((S, D), BF16),
        z=VM((S, C), BF16),
        zslope=VM((S, C), F32),
        ga=VM((S, C), F32),
        gb=VM((S, C), F32),
        glu=VM((S + 2 * MARGIN, C), F32),
        back=VM((S + 2 * MARGIN, C), F32),
        pair=VM((S, 2 * C), BF16),
        sums=VM((KERNEL, 8, C), F32),
    )
    for scatter in scatters:
        scratch |= scatter.scratch()

    def body(r):
        spot = Spot(dims)
        greet(spot.tensor_peers() + spot.data_peers())
        edge.bind(r, spot)
        begin = F // 4
        gather.bind(r, spot, r.sr, r.rt, pl.ds(begin, F - begin)).start()
        early = pltpu.make_async_copy(r.ra, r.rt.at[:, pl.ds(0, begin)], r.rsem)
        early.start()
        for scatter in scatters[:2]:
            scatter.bind(r, spot, r.dr, r.outr)
        scatters[2].bind(r, spot, r.de, r.oute)
        for sums in (r.dg2, r.dg3, r.dg4):
            sums[...] = jnp.zeros_like(sums)

        clear_margins(r.glu, S)
        clear_margins(r.back, S)
        live_column(r, S, False)
        r.need("n", "wc")

        def gated(i):
            rows = rows_of(i, 256)
            values = jnp.dot(r.n[rows, :], r.wc[:, pl.ds(0, C)], preferred_element_type=F32)
            gate = jax.nn.sigmoid(
                jnp.dot(r.n[rows, :], r.wc[:, pl.ds(C, C)], preferred_element_type=F32)
            )
            open_gate = gate * r.column[rows, :]
            product = values * open_gate
            r.ga[rows, :] = open_gate
            r.gb[rows, :] = product * (1.0 - gate)
            r.glu[pl.ds(pl.multiple_of(i * 256 + MARGIN, MARGIN), 256), :] = product

        loop(S // 256, gated)
        for k in range(nc):

            def band(i, k=k):
                base = k * m + i * BAND
                mixed = slide(r.glu, base, r.taps)
                gate = jax.nn.sigmoid(mixed)
                rows = pl.ds(pl.multiple_of(base, BAND), BAND)
                r.z[rows, :] = (mixed * gate).astype(BF16)
                r.zslope[rows, :] = gate * (1.0 + mixed * (1.0 - gate))

            loop(m // BAND, band)
            part_product(edge, 0, k, r.z, r.wc, 2 * C, dims)
            if k > 0:
                edge.cross(0, k - 1)
            if k == 1:
                gather.advance()
        edge.cross(0, nc - 1)
        gather.advance()

        r.need("h", "e")
        for k in range(nc):
            edge.settle(0, k, forward_rows(r.h, 1.0, r.g3, r.h3), r.n4)
            if k == 0:
                gather.advance()
            edge.arrived(0, k)
            up_products(dims, k, r.n4, r.e, r.u, r.slope)
            if k == 0:
                early.wait()
                gather.finish()
            part_product(edge, 1, k, r.u, r.rt, 0, dims)
            edge.cross(1, k)

        def turn(total, k, rs):
            xhat, inverse = unit(r.h3[k, rs, :] + 0.5 * total)
            r.fall[k, rs, :] = (xhat * r.g4[...]).astype(BF16)
            upstream = r.og[k, rs, :].astype(F32)
            own = jnp.where(spot.y == k // 2, 1.0, 0.0)
            r.dg4[...] += fold(upstream * xhat) * own
            grad = unit_back(upstream, xhat, inverse, r.g4[...])
            r.gh[k, rs, :] = grad
            return (0.5 * grad).astype(BF16)

        r.need("og")
        for k in range(nc):
            edge.settle(1, k, turn, r.w4)
            edge.arrived(1, k)
            back_products(dims, k, r.w4, r.rt, r.slope, r.slope)
            part_product(edge, 2, k, r.slope, r.e, 0, dims)
            edge.cross(2, k)
        keep = pltpu.make_async_copy(r.fall.at[spot.t], r.fo.at[spot.c], r.fsem.at[2])
        keep.start()
        other = spot.y * 2 + 1 - spot.c
        give = remote(
            r.fall.at[other], r.fo.at[spot.c], r.fsem.at[0], r.fsem.at[1], spot.sibling()
        )
        give.start()
        weight_part(r.dr, 0, r.w4, r.u, dims)
        for scatter in scatters[:2]:
            scatter.start()
        weight_part(r.de, 0, r.n4, r.slope, dims)
        scatters[2].start()
        r.done("de")

        finished = 0
        for k in range(nc):
            edge.settle(2, k, backward_rows(r.h3, 1.0, r.g3, r.gh, r.dg3, spot), r.w3)
            edge.arrived(2, k)
            rows = chunk_rows(dims, k)
            inner = jnp.dot(r.w3[rows, :], r.wc[:, pl.ds(2 * C, C)], preferred_element_type=F32)
            r.back[pl.ds(k * m + MARGIN, m), :] = inner * r.zslope[rows, :]
            until = (k + 1) * m // BAND - (1 if k < nc - 1 else 0)

            def band(i, finished=finished):
                base = (i + finished) * BAND
                rows = pl.ds(pl.multiple_of(base, BAND), BAND)
                mixed = slide(r.back, base, r.taps, True)
                r.pair[rows, pl.ds(0, C)] = (mixed * r.ga[rows, :]).astype(BF16)
                r.pair[rows, pl.ds(C, C)] = (mixed * r.gb[rows, :]).astype(BF16)

            loop(until - finished, band)
            finished = until
            if k == 2:
                scatters[0].advance()
            if k > 0:
                part_product(edge, 3, k - 1, r.pair, r.wc, 0, dims)
            if k > 1:
                edge.cross(3, k - 2)
        edge.cross(3, nc - 2)
        part_product(edge, 3, nc - 1, r.pair, r.wc, 0, dims)
        edge.cross(3, nc - 1)
        scatters[1].advance()
        weight_part(r.dw, 0, r.n, r.pair, dims)
        weight_part(r.dw, 2 * C, r.w3, r.z, dims)
        r.done("dw")
        scatters[0].advance()
        r.sums[...] = jnp.zeros_like(r.sums)

        def tap_sums(i):
            base = i * BAND
            window = r.glu[pl.ds(pl.multiple_of(base, BAND), BAND + 2 * MARGIN), :]
            slope = r.back[pl.ds(pl.multiple_of(base + MARGIN, MARGIN), BAND), :]
            for residue in range(8):
                shifted = window[residue : residue + BAND + 24]
                for eighth in range(4):
                    tap = 8 * eighth + residue - 1
                    if 0 <= tap < KERNEL:
                        term = shifted[8 * eighth : 8 * eighth + BAND] * slope
                        r.sums[tap] += term.reshape(BAND // 8, 8, C).sum(axis=0)

        loop(S // BAND, tap_sums)
        for tap in range(KERNEL):
            r.dk[tap : tap + 1, :] = jnp.sum(r.sums[tap], axis=0, keepdims=True)
        for k in range(nc):
            edge.settle(3, k, backward_rows(r.h, 1.0, r.g2, r.gh, r.dg2, spot), r.w2)
            if k == 0:
                scatters[2].advance()
            elif k == 1:
                scatters[1].advance()
            elif k == 2:
                scatters[0].finish()
                scatters[2].advance()
        r.done("gh")
        for k in range(nc):
            edge.arrived(3, k)
        r.done("w2")
        keep.wait()
        give.wait()
        edge.drain()
        for scatter in scatters[1:]:
            scatter.finish()

    return call(
        body,
        dict(
            n=(kept["n3"], LD),
            wc=(kept["wc"], LD),
            e=(kept["e1"], LD),
            h=(kept["h2"], LD),
            og=(kept["ogh"], LD),
            taps=(taps, VM),
            lengths=(lengths, SM),
            g2=(gains[2], VM),
            g3=(gains[3], VM),
            g4=(gains[4], VM),
            sr=(kept["r1"], HB),
            ra=(kept["ra"], HB),
        ),
        dict(
            fo=((2, Q, D), BF16, HB),
            gh=((nc, Q, D), F32, ST),
            w2=((S, D), BF16, ST),
            dw=(four + (3 * C,), BF16, ST),
            de=(four + (F,), BF16, ST),
            outr=((shard, F), F32, VM),
            oute=((shard, half), F32, VM),
            dk=((KERNEL, C), F32, VM),
            dg2=((8, D), F32, VM),
            dg3=((8, D), F32, VM),
            dg4=((8, D), F32, VM),
        ),
        scratch,
        cid,
    )


def last_kernel(dims, cid, kept, middle, lengths, gains, shard):
    nc, Q, D, S, F, H, C = dims.nc, dims.Q, dims.D, dims.S, dims.F, dims.H, dims.C
    heads = H // HEAD_DIM
    edge = Edge(dims, 2)
    four = (dims.na, dims.nb, shard)
    some = 3 * H // 2 if H % 256 == 0 else 3 * H
    scatters = [
        Scatter("0", dims, shard, 0, 3 * C),
        Scatter("1", dims, shard, F // 2, F // 2, 0, True),
        Scatter("2", dims, shard, 3 * H, H),
    ]
    scatters += [
        Scatter(str(3 + j), dims, shard, j * some, some) for j in range(3 * H // some)
    ]
    triple = (heads, S, HEAD_DIM)
    scratch = edge.scratch() | dict(
        da=VM(triple, BF16),
        kt=VM((heads, HEAD_DIM, S), BF16),
        delta=VM((heads, 1, S), F32),
        gk=VM(triple, F32),
        gv=VM(triple, F32),
        dqt=VM((H, S), F32),
        pack=VM((S, 3 * H), BF16),
        dw=VM(four + (4 * H,), BF16),
        w1=VM((S, D), BF16),
        column=VM((S, 1), F32),
        psem=SEMS,
        gsem=SEMS,
    )
    for scatter in scatters:
        scratch |= scatter.scratch()

    def body(r):
        spot = Spot(dims)
        greet(spot.tensor_peers() + spot.data_peers())
        edge.bind(r, spot)
        scatters[0].bind(r, spot, r.cw, r.sc).start()
        scatters[1].bind(r, spot, r.dei, r.oute).start()
        for scatter in scatters[2:]:
            scatter.bind(r, spot, r.dw, r.sa)
        live_column(r, S, True)
        for sums in (r.dg1, r.gk, r.gv):
            sums[...] = jnp.zeros_like(sums)

        ghc = pltpu.make_async_copy(r.ghi, r.gh, r.gsem)
        ghc.start()

        r.need("w", "oh")
        weight_part(r.dw, 3 * H, r.w, r.oh, dims)
        scatters[2].start()
        r.need("wa", "k")
        mixed = jnp.dot(r.w[...], r.wa[:, pl.ds(3 * H, H)], preferred_element_type=F32).astype(BF16)
        inner = (mixed.astype(F32) * r.oh[...].astype(F32)).T
        for j in range(heads):
            some = slice(j * HEAD_DIM, (j + 1) * HEAD_DIM)
            r.da[j] = mixed[:, some]
            r.delta[j] = jnp.sum(inner[some], axis=0, keepdims=True)
            r.kt[j] = r.k[j].astype(F32).T.astype(BF16)
        blocks = S // min(2 * QUERIES, S)
        size = S // blocks
        r.need("q", "v", "lse")

        def one(i):
            head = lax.div(i, blocks)
            at = pl.ds(pl.multiple_of(lax.rem(i, blocks) * size, size), size)
            query, outer = r.q[head, at, :], r.da[head, at, :]
            scores = lax.dot_general(
                r.k[head], query, (((1,), (1,)), ((), ())), preferred_element_type=F32
            )
            prob = jnp.exp(scores + (r.column[...] - r.lse[head, :, at]))
            r.gv[head] += jnp.dot(prob.astype(BF16), outer, preferred_element_type=F32)
            back = lax.dot_general(
                r.v[head], outer, (((1,), (1,)), ((), ())), preferred_element_type=F32
            )
            slope = (prob * (back - r.delta[head, :, at])).astype(BF16)
            r.gk[head] += jnp.dot(slope, query, preferred_element_type=F32)
            r.dqt[pl.ds(pl.multiple_of(head * HEAD_DIM, HEAD_DIM), HEAD_DIM), at] = (
                jnp.dot(r.kt[head], slope, preferred_element_type=F32) * HEAD_DIM**-0.5
            )

        loop(heads * blocks, one)
        scatters[1].advance()
        r.pack[:, pl.ds(0, H)] = r.dqt[...].T.astype(BF16)
        for j, source in ((1, r.gk), (2, r.gv)):
            r.pack[:, pl.ds(j * H, H)] = jnp.concatenate(
                [source[i] for i in range(heads)], axis=1
            ).astype(BF16)
        for k in range(nc):
            part_product(edge, 0, k, r.pack, r.wa, 0, dims)
            if k > 0:
                edge.cross(0, k - 1)
        edge.cross(0, nc - 1)
        r.need("n2")
        scatters[0].advance()
        weight_part(r.dw, 0, r.n2, r.pack, dims)
        for scatter in scatters[3:]:
            scatter.start()

        ghc.wait()
        r.need("h1", "rt", "slope", "e")
        for k in range(nc):
            edge.settle(0, k, backward_rows(r.h1, 0.5, r.g1, r.gh, r.dg1, spot), r.w1)
            edge.arrived(0, k)
            back_products(dims, k, r.w1, r.rt, r.slope, r.slope)
            part_product(edge, 1, k, r.slope, r.e, 0, dims)
            if k > 0:
                edge.cross(1, k - 1, send=False)
            if k == 0:
                scatters[2].advance()
            elif k == 1:
                scatters[1].advance()
                scatters[0].advance()
            elif k == 2:
                scatters[2].advance()
                scatters[3].advance()
            elif k == 3:
                scatters[0].finish()
                scatters[-1].advance()
        r.done("gh")
        r.need("n1", "u")
        weight_part(r.dr, 0, r.w1, r.u, dims)
        r.done("dr")
        scatters[3].advance()
        edge.cross(1, nc - 1, send=False)
        part = pltpu.make_async_copy(r.e_sum, r.part, r.psem)
        part.start()
        weight_part(r.de, 0, r.n1, r.slope, dims)
        r.done("de")
        scatters[-1].advance()
        scatters[1].finish()
        scatters[2].finish()
        part.wait()
        edge.drain()
        for scatter in scatters[3:]:
            scatter.finish()

    return call(
        body,
        dict(
            w=(middle["w2"], LD),
            wa=(kept["wa"], LD),
            oh=(kept["oh"], LD),
            k=(kept["k"], LD),
            q=(kept["q"], LD),
            v=(kept["v"], LD),
            lse=(kept["lse"], LD),
            n2=(kept["n2"], LD),
            ghi=(middle["gh"], HB),
            h1=(kept["h1"], LD),
            rt=(kept["rt"], LD),
            slope=(kept["slope"], LD),
            e=(kept["e"], LD),
            n1=(kept["n1"], LD),
            u=(kept["u"], LD),
            lengths=(lengths, SM),
            g1=(gains[1], VM),
            cw=(middle["dw"], HB),
            dei=(middle["de"], HB),
        ),
        dict(
            part=((nc, Q, D), BF16, HB),
            gh=((nc, Q, D), F32, ST),
            de=(four + (F,), BF16, ST),
            dr=(four + (F,), BF16, ST),
            sc=((shard, 3 * C), F32, VM),
            sa=((shard, 4 * H), F32, VM),
            oute=((shard, F // 2), F32, VM),
            dg1=((8, D), F32, VM),
        ),
        scratch,
        cid,
    )


def direction_of(mean, square, master, rates, decay):
    return mean * rates[4] / (jnp.sqrt(square * rates[5]) + ADAM_EPS) + decay * master


def moments_of(grad, mean, square, rates):
    return (
        rates[0] * mean + (1.0 - rates[0]) * grad,
        rates[1] * square + (1.0 - rates[1]) * grad * grad,
    )


def tile_rows(shape):
    rows, columns = shape[-2:]
    step = min(rows, max(8, 16384 // max(columns, 128)))
    return step if rows % step == 0 and step % 8 == 0 else rows


def eighths(tile):
    rows, columns = tile.shape
    return tile.reshape(rows // 8, 8, columns).sum(axis=0) if rows % 8 == 0 else tile


def flip(result, source, dims):
    def part(j):
        cs = rows_of(j, 128)
        result[cs, :] = source[:, cs].T

    loop(source.shape[1] // 128, part)


PLACES = (0, 1, 2, 3, 4, 6, 5, 7)


def piece_rows(shapes):
    rows, total = {}, 0
    for i in PLACES:
        rows[i] = total
        total += shapes[i][0]
    return rows


class Relay:
    def __init__(self, tag, count, shape):
        self.tag, self.count = tag, count
        k = max(count - 1, 1)
        self.specs = dict(slots=VM((count,) + shape, F32), s=SEMS((k,)), r=SEMS((k,)))

    def scratch(self):
        return tagged("r", self.tag, self.specs)

    def start(self, refs, place, peers, value):
        self.r = bound(refs, "r", self.tag, self.specs)
        r = self.r
        r.slots[place] = value
        self.copies = []
        for j, peer in enumerate(peers):
            copy = remote(r.slots.at[place], r.slots.at[place], r.s.at[j], r.r.at[j], peer)
            copy.start()
            self.copies.append(copy)

    def finish(self):
        for copy in self.copies:
            copy.wait()
        total = self.r.slots[0]
        for i in range(1, self.count):
            total = total + self.r.slots[i]
        return total


def gradient_kernel(
    dims, cid, rates, entries, scatter, sums, gain_parts, kernel_part, part, grad, hidden, gain
):
    D, F, H, C, Q, ny = dims.D, dims.F, dims.H, dims.C, dims.Q, dims.ny
    shard = scatter[0].shape[2]
    pieces = 4
    width = F // pieces
    jobs = [
        Scatter(str(pieces * i + j), dims, shard, j * width, width, None, pieces * i + j > 5)
        for i in range(2)
        for j in range(pieces)
    ]
    count_t, count_d = dims.ny * 2, dims.na * dims.nb
    gains_relays = [
        Relay("0", 2, (8, D)), Relay("1", ny, (8, D)),
        Relay("2", dims.na, (8, D)), Relay("3", dims.nb, (8, D)),
    ]
    taps_relays = [Relay("4", dims.na, (KERNEL, C)), Relay("5", dims.nb, (KERNEL, C))]
    norm_relays = [Relay("6", count_t, (24, 128)), Relay("7", count_d, (24, 128))]
    relays = gains_relays + taps_relays + norm_relays
    count = len(entries)
    m = max(ny - 1, 1)
    shapes = [entry[1].shape for entry in entries]
    scratch = dict(
        nrm=VM((24, 128), F32),
        gains=VM((8, D), F32),
        dg0=VM((8, D), F32),
        shr0=VM((shard, F), F32),
        shr1=VM((shard, F), F32),
        mix=VM((shard, H), F32),
        mer=VM((shard, C), F32),
        far=VM((m, 2, Q, D), BF16),
        sum=VM((dims.nc, Q, D), BF16),
        gh=VM((2, Q, D), F32),
        h=VM((2, Q, D), BF16),
        both=VM((2, Q, D), BF16),
        gsem=SEMS((10,)),
        psem=SEMS((4,)),
        fsem=SEMS((m, 2)),
        bsem=SEMS((2,)),
        isem=SEMS((count, 3)),
    )
    ins = dict(
        rates=(rates, SM),
        kp=(kernel_part, VM),
        sp=(part, HB),
        ghp=(grad, HB),
        hp=(hidden, HB),
        g=(gain, VM),
        src0=(scatter[0], HB),
        src1=(scatter[1], HB),
    )
    outs = dict(norms=((24, 128), F32, VM), gin=((2, Q, D), BF16, HB))
    for i, (params, mean, square, _) in enumerate(entries):
        tag = str(i)
        held = shapes[i] if i < 6 else params.shape
        ins |= {"p" + tag: (params, HB), "m" + tag: (mean, HB), "v" + tag: (square, HB)}
        scratch |= {"w" + tag: VM(held, F32), "n" + tag: VM(shapes[i], F32)}
        scratch |= {"q" + tag: VM(shapes[i], F32)}
        outs |= {"g" + tag: (shapes[i], F32, VM)}
    for i, array in enumerate(gain_parts):
        ins |= {"d" + str(i): (array, VM)}
    for i, array in enumerate(sums):
        ins |= {"s" + str(i): (array, HB)}
    for item in relays + jobs:
        scratch |= item.scratch()

    def body(r):
        spot = Spot(dims)
        everyone = [(spot.d, lax.rem(spot.t + j, count_t)) for j in range(1, count_t)]
        items = [(lax.rem(spot.d + j, count_d), spot.t) for j in range(1, count_d)]
        greet(everyone + items)
        get = lambda name, i: getattr(r, name + str(i))
        for i, job in enumerate(jobs):
            early = i < pieces
            job.bind(r, spot, r.src0 if early else r.src1, r.shr0 if early else r.g0.at[0])
        for i in (6, 0, 7, 1, 2, 3, 4, 5):
            jobs[i].start()
        mine = pl.ds(spot.y * 2, 2)
        totals = [
            pltpu.make_async_copy(r.sp, r.sum, r.psem.at[0]),
            pltpu.make_async_copy(r.ghp.at[mine], r.gh, r.psem.at[1]),
            pltpu.make_async_copy(r.hp.at[mine], r.h, r.psem.at[2]),
        ]
        for copy in totals:
            copy.start()
        grads = [
            pltpu.make_async_copy(r.s0, r.g0.at[1, :, pl.ds(0, F // 2)], r.gsem.at[0]),
            pltpu.make_async_copy(r.s4, r.g0.at[1, :, pl.ds(F // 2, F // 2)], r.gsem.at[9]),
            pltpu.make_async_copy(r.s1, r.shr1, r.gsem.at[1]),
            pltpu.make_async_copy(r.s2.at[:, pl.ds(3 * H, H)], r.mix, r.gsem.at[2]),
            pltpu.make_async_copy(r.s3.at[:, pl.ds(2 * C, C)], r.mer, r.gsem.at[3]),
        ]
        grads += [
            pltpu.make_async_copy(r.s2.at[:, pl.ds(k * H, H)], r.g2.at[k], r.gsem.at[4 + k])
            for k in range(3)
        ]
        grads += [
            pltpu.make_async_copy(r.s3.at[:, pl.ds(k * C, C)], r.g4.at[k], r.gsem.at[7 + k])
            for k in range(2)
        ]
        for copy in grads:
            copy.start()
        loads = []
        for i in range(count):
            master = get("p", i).at[0] if i < 6 else get("p", i)
            triple = [
                pltpu.make_async_copy(master, get("w", i), r.isem.at[i, 0]),
                pltpu.make_async_copy(get("m", i), get("n", i), r.isem.at[i, 1]),
                pltpu.make_async_copy(get("v", i), get("q", i), r.isem.at[i, 2]),
            ]
            for copy in triple:
                copy.start()
            loads.append(triple)

        totals[0].wait()
        crossing = []
        for j in range(1, ny):
            other = lax.rem(spot.y + j, ny) * 2
            copy = remote(
                r.sum.at[pl.ds(other, 2)], r.far.at[j - 1], r.fsem.at[j - 1, 0], r.fsem.at[j - 1, 1],
                spot.across(j),
            )
            copy.start()
            crossing.append(copy)

        r.nrm[...] = jnp.zeros_like(r.nrm)
        row = lax.broadcasted_iota(jnp.int32, (24, 128), 0)
        lane = lax.broadcasted_iota(jnp.int32, (24, 128), 1)
        first_piece = piece_rows(shapes)
        loaded = set()

        def load(i):
            if i not in loaded:
                loaded.add(i)
                for copy in loads[i]:
                    copy.wait()

        def small_norm(i, weight):
            load(i)
            master = get("w", i)[:, 0, :]
            mean, square = moments_of(get("g", i)[0], get("n", i)[0], get("q", i)[0], r.rates)
            move = direction_of(mean, square, master, r.rates, entries[i][3])
            for column, values in enumerate((master, move)):
                value = jnp.sum(values * values, axis=1, keepdims=True) * weight
                if i == 6:
                    value = jnp.sum(value, axis=0, keepdims=True)
                at = first_piece[i]
                r.nrm[at : at + value.shape[0], column : column + 1] = value

        def norm(i, p):
            load(i)
            step = tile_rows(shapes[i])
            zero = jnp.zeros((8, shapes[i][-1]), F32)

            def tile(j, carry):
                rs = pl.ds(pl.multiple_of(j * step, step), step)
                master = get("w", i)[p, rs, :]
                mean, square = moments_of(
                    get("g", i)[p, rs, :], get("n", i)[p, rs, :], get("q", i)[p, rs, :], r.rates
                )
                move = direction_of(mean, square, master, r.rates, entries[i][3])
                return (carry[0] + eighths(master * master), carry[1] + eighths(move * move))

            sums_of = lax.fori_loop(0, shapes[i][-2] // step, tile, (zero, zero))
            here = row == first_piece[i] + p
            for column, total in enumerate(sums_of):
                value = jnp.sum(jnp.sum(total, axis=0, keepdims=True), axis=1, keepdims=True)
                r.nrm[...] += jnp.where(jnp.logical_and(here, lane == column), value, 0.0)

        slow = [spot.slow(j) for j in range(1, dims.na)]
        fast = [spot.fast(j) for j in range(1, dims.nb)]
        taps_relays[0].start(r, spot.a, slow, r.kp[...])
        for copy in grads:
            copy.wait()
        flip(r.g3.at[0], r.mix, dims)
        flip(r.g5.at[0], r.mer, dims)
        jobs[6].advance()
        jobs[0].advance()

        for copy in totals[1:]:
            copy.wait()
        for p in range(3):
            norm(2, p)
        for copy in crossing:
            copy.wait_recv()
        jobs[7].advance()
        jobs[1].advance()
        r.dg0[...] = jnp.zeros_like(r.dg0)
        for i in range(2):

            def rows(j, i=i):
                rs = rows_of(j)
                total = r.sum[spot.y * 2 + i, rs, :].astype(F32)
                for other in range(ny - 1):
                    total = total + r.far[other, i, rs, :].astype(F32)
                xhat, inverse = unit(r.h[i, rs, :].astype(F32))
                r.dg0[...] += fold(total * xhat)
                back = r.gh[i, rs, :] + unit_back(total, xhat, inverse, r.g[...])
                r.both[i, rs, :] = back.astype(BF16)

            loop(Q // STEP, rows, 2)
        keep = pltpu.make_async_copy(r.both.at[spot.c], r.gin.at[spot.c], r.psem.at[3])
        keep.start()
        give = remote(
            r.both.at[1 - spot.c], r.gin.at[spot.c], r.bsem.at[0], r.bsem.at[1], spot.sibling()
        )
        give.start()

        r.gains[...] = jnp.zeros_like(r.gains)
        for k, ref in enumerate((r.dg0, r.d0, r.d1, r.d2, r.d3)):
            r.gains[k : k + 1, :] = jnp.sum(ref[...], axis=0, keepdims=True)
        gains_relays[0].start(r, spot.c, [spot.sibling()], r.gains[...])
        jobs[0].advance()
        jobs[2].advance()
        total = gains_relays[0].finish()
        gains_relays[1].start(r, spot.y, [spot.across(j) for j in range(1, ny)], total)
        norm(3, 0)
        for p in range(2):
            norm(4, p)
        norm(5, 0)
        jobs[1].advance()
        jobs[3].advance()
        total = gains_relays[1].finish()
        gains_relays[2].start(r, spot.a, slow, total)
        total = taps_relays[0].finish()
        taps_relays[1].start(r, spot.b, fast, total)
        flip(r.g1.at[1], r.shr1, dims)
        norm(1, 1)
        jobs[0].finish()
        jobs[2].advance()
        jobs[4].advance()
        total = gains_relays[2].finish()
        gains_relays[3].start(r, spot.b, fast, total)
        norm(0, 1)
        jobs[1].finish()
        jobs[3].advance()
        jobs[5].advance()
        jobs[2].finish()
        r.g6[0] = taps_relays[1].finish()
        owner = jnp.where(spot.d == 0, 1.0, 0.0)
        small_norm(6, owner)
        jobs[4].advance()
        jobs[3].finish()
        flip(r.g1.at[0], r.shr0, dims)
        jobs[6].advance()
        r.gains[...] = gains_relays[3].finish()
        owner = jnp.where(spot.t == 0, owner, 0.0)
        r.g7[0] = r.gains[0:5, :]
        small_norm(7, owner)
        jobs[5].advance()
        jobs[7].advance()
        norm(1, 0)
        for job in jobs[4:]:
            job.finish()
        norm(0, 0)
        norm_relays[0].start(r, spot.t, everyone, r.nrm[...])
        total = norm_relays[0].finish()
        norm_relays[1].start(r, spot.d, items, total)
        r.norms[...] = norm_relays[1].finish()
        keep.wait()
        give.wait()
        for copy in crossing:
            copy.wait_send()

    return call(body, ins, outs, scratch, cid)


def update_kernel(dims, rates, norms, entries, grads, frames, frames_grad):
    count = len(entries)
    shapes = [entry[1].shape for entry in entries]
    like = (dims.L, dims.D)
    ins = dict(
        rates=(rates, SM),
        norms=(norms, VM),
        fo=(frames.reshape(like), HB),
        fg=(frames_grad.reshape(like), HB),
    )
    outs = dict(trust=((2, 17), F32, VM), frames=(like, BF16, HB), gin=(like, BF16, HB))
    scratch = dict(isem=SEMS((count, 4)), osem=SEMS((count, 5)), fsem=SEMS((4,)), rows=VM((2,) + like, BF16))
    for i, (params, mean, square, _) in enumerate(entries):
        tag = str(i)
        shape = shapes[i]
        pair = params.shape
        ins |= {"p" + tag: (params, HB), "m" + tag: (mean, HB), "v" + tag: (square, HB)}
        ins |= {"g" + tag: (grads[i], HB)}
        scratch |= {"w" + tag: VM(pair, F32), "n" + tag: VM(shape, F32)}
        scratch |= {"q" + tag: VM(shape, F32), "h" + tag: VM(shape, F32)}
        scratch |= {"b" + tag: VM(pair, BF16)}
        outs |= {"og" + tag: (shape, F32, HB), "om" + tag: (shape, F32, HB)}
        outs |= {"ov" + tag: (shape, F32, HB), "ow" + tag: (pair, F32, HB)}
        outs |= {"ob" + tag: (pair, BF16, HB)}
    order = [2, 4, 3, 5, 7, 6, 1, 0]

    def body(r):
        get = lambda name, i: getattr(r, name + str(i))
        loads, stores = {}, []
        for i in order:
            moves = (("g", "h"), ("m", "n"), ("v", "q"), ("p", "w"))
            loads[i] = [
                pltpu.make_async_copy(get(source, i), get(target, i), r.isem.at[i, k])
                for k, (source, target) in enumerate(moves)
            ]
            for copy in loads[i]:
                copy.start()
        staged = []
        for k, source in enumerate((r.fo, r.fg)):
            staged.append(pltpu.make_async_copy(source, r.rows.at[k], r.fsem.at[k]))
            staged[k].start()
        norms = jnp.sqrt(r.norms[...])
        r.trust[...] = norms.T[:2, :17]
        ratio = r.rates[3] * norms[:, 0:1] / norms[:, 1:2]

        def send(i, name, target, k):
            copy = pltpu.make_async_copy(get(name, i), get(target, i), r.osem.at[i, k])
            copy.start()
            stores.append(copy)

        def update(i, grad, mean, square, master, average, scale):
            mean, square = moments_of(grad, mean, square, r.rates)
            move = direction_of(mean, square, master, r.rates, entries[i][3])
            master = master - scale * move
            average = r.rates[2] * average + (1.0 - r.rates[2]) * master
            return mean, square, master, average

        for i in order:
            for copy in loads[i]:
                copy.wait()
            send(i, "h", "og", 0)
            offset = piece_rows(shapes)[i]
            if i > 5:
                weights = get("w", i)
                scale = ratio[offset : offset + (1 if i == 6 else shapes[i][1]), :]
                mean, square, master, average = update(
                    i, get("h", i)[0], get("n", i)[0], get("q", i)[0], weights[:, 0, :],
                    weights[:, 1, :], scale,
                )
                get("n", i)[0] = mean
                get("q", i)[0] = square
                for slot, values in enumerate((master, average)):
                    weights[:, slot, :] = values
                get("b", i)[...] = weights[...].astype(BF16)
            else:
                step = tile_rows(shapes[i])
                for p in range(shapes[i][0]):
                    scale = ratio[offset + p : offset + p + 1, :]

                    def tile(j, p=p, i=i, step=step, scale=scale):
                        rs = pl.ds(pl.multiple_of(j * step, step), step)
                        mean, square, master, average = update(
                            i, get("h", i)[p, rs, :], get("n", i)[p, rs, :], get("q", i)[p, rs, :],
                            get("w", i)[0, p, rs, :], get("w", i)[1, p, rs, :], scale,
                        )
                        get("n", i)[p, rs, :] = mean
                        get("q", i)[p, rs, :] = square
                        get("w", i)[0, p, rs, :] = master
                        get("w", i)[1, p, rs, :] = average
                        get("b", i)[0, p, rs, :] = master.astype(BF16)
                        get("b", i)[1, p, rs, :] = average.astype(BF16)

                    loop(shapes[i][-2] // step, tile)
            send(i, "n", "om", 1)
            send(i, "q", "ov", 2)
            send(i, "w", "ow", 3)
            send(i, "b", "ob", 4)
            if i == order[0]:
                for k, target in enumerate((r.frames, r.gin)):
                    staged[k].wait()
                    copy = pltpu.make_async_copy(r.rows.at[k], target, r.fsem.at[2 + k])
                    copy.start()
                    stores.append(copy)
        for copy in stores:
            copy.wait()

    return call(body, ins, outs, scratch, None)


def shards(
    dims,
    frames_input,
    out_grad,
    lengths,
    step_count,
    rates,
    expand_params,
    expand_first,
    expand_second,
    shrink_params,
    shrink_first,
    shrink_second,
    project_params,
    project_first,
    project_second,
    mixing_params,
    mixing_first,
    mixing_second,
    gating_params,
    gating_first,
    gating_second,
    kernel_params,
    kernel_first,
    kernel_second,
    merging_params,
    merging_first,
    merging_second,
    gains_params,
    gains_first,
    gains_second,
):
    local_rows, width = frames_input.shape
    shard_rows = expand_params.shape[2]
    dims = SimpleNamespace(
        L=local_rows,
        D=width,
        S=local_rows * dims.ny * 2,
        F=expand_params.shape[3],
        H=project_params.shape[3],
        C=gating_params.shape[3],
        Q=local_rows // 2,
        nc=dims.ny * 2,
        **vars(dims),
    )
    gain = [gains_params[0, i : i + 1] for i in range(5)]
    taps = jnp.swapaxes(kernel_params, 0, 1)
    front = front_kernel(
        dims, 1, frames_input, out_grad, lengths, gain, expand_params, shrink_params,
        project_params, mixing_params, gating_params, merging_params,
    )
    middle = middle_kernel(dims, 2, front, lengths, taps, gain, shard_rows)
    last = last_kernel(dims, 4, front, middle, lengths, gain, shard_rows)

    steps_done = step_count[0].astype(F32)
    scalars = jnp.concatenate(
        [rates, 1.0 / (1.0 - rates[:2] ** steps_done), jnp.zeros((2,), F32)]
    )
    one = lambda params, first, second: (params[:, None], first[None], second[None], DECAY_RATE)
    entries = [
        (expand_params, expand_first, expand_second, DECAY_RATE),
        (shrink_params, shrink_first, shrink_second, DECAY_RATE),
        (project_params, project_first, project_second, DECAY_RATE),
        one(mixing_params, mixing_first, mixing_second),
        (gating_params, gating_first, gating_second, DECAY_RATE),
        one(merging_params, merging_first, merging_second),
        (taps, kernel_first[None], kernel_second[None], DECAY_RATE),
        (jnp.swapaxes(gains_params, 0, 1), gains_first[None], gains_second[None], 0.0),
    ]
    summed = gradient_kernel(
        dims, 3, scalars, entries, [last["dr"], last["de"]],
        [middle["oute"], middle["outr"], last["sa"], last["sc"], last["oute"]],
        [last["dg1"], middle["dg2"], middle["dg3"], middle["dg4"]], middle["dk"],
        last["part"], last["gh"], front["xh"], gain[0],
    )
    updated = update_kernel(
        dims, scalars, summed["norms"], entries, [summed["g" + str(i)] for i in range(8)],
        middle["fo"], summed["gin"],
    )
    results = []
    firsts = (
        expand_first, shrink_first, project_first, mixing_first, gating_first, kernel_first,
        merging_first, gains_first,
    )
    for place in range(8):
        entry = PLACES.index(place)
        like = firsts[place].shape
        tag = str(entry)
        results += [updated[name + tag].reshape(like) for name in ("og", "om", "ov")]
        for name in ("ow", "ob"):
            pair = updated[name + tag]
            results.append(jnp.swapaxes(pair, 0, 1) if entry > 5 else pair.reshape((2,) + like))
    return (updated["frames"], updated["gin"], *results, updated["trust"].T)


def solution(mesh):
    slow = math.gcd(mesh.shape["dp"], 4)
    dims = SimpleNamespace(na=slow, nb=mesh.shape["dp"] // slow, ny=mesh.shape["tensor"] // 2)
    return jax.shard_map(
        functools.partial(shards, dims),
        mesh=mesh,
        in_specs=(
            P(("dp", "tensor"), None),
            P(("dp", "tensor"), None),
            P("dp"),
            P(),
            P(),
            P(None, None, "dp", "tensor"),
            P(None, "dp", "tensor"),
            P(None, "dp", "tensor"),
            P(None, None, "tensor", "dp"),
            P(None, "tensor", "dp"),
            P(None, "tensor", "dp"),
            P(None, None, "dp", "tensor"),
            P(None, "dp", "tensor"),
            P(None, "dp", "tensor"),
            P(None, "tensor", "dp"),
            P("tensor", "dp"),
            P("tensor", "dp"),
            P(None, None, "dp", "tensor"),
            P(None, "dp", "tensor"),
            P(None, "dp", "tensor"),
            P(None, None, "tensor"),
            P(None, "tensor"),
            P(None, "tensor"),
            P(None, "tensor", "dp"),
            P("tensor", "dp"),
            P("tensor", "dp"),
            P(),
            P(),
            P(),
        ),
        out_specs=(
            P(("dp", "tensor"), None),
            P(("dp", "tensor"), None),
            P(None, "dp", "tensor"),
            P(None, "dp", "tensor"),
            P(None, "dp", "tensor"),
            P(None, None, "dp", "tensor"),
            P(None, None, "dp", "tensor"),
            P(None, "tensor", "dp"),
            P(None, "tensor", "dp"),
            P(None, "tensor", "dp"),
            P(None, None, "tensor", "dp"),
            P(None, None, "tensor", "dp"),
            P(None, "dp", "tensor"),
            P(None, "dp", "tensor"),
            P(None, "dp", "tensor"),
            P(None, None, "dp", "tensor"),
            P(None, None, "dp", "tensor"),
            P("tensor", "dp"),
            P("tensor", "dp"),
            P("tensor", "dp"),
            P(None, "tensor", "dp"),
            P(None, "tensor", "dp"),
            P(None, "dp", "tensor"),
            P(None, "dp", "tensor"),
            P(None, "dp", "tensor"),
            P(None, None, "dp", "tensor"),
            P(None, None, "dp", "tensor"),
            P(None, "tensor"),
            P(None, "tensor"),
            P(None, "tensor"),
            P(None, None, "tensor"),
            P(None, None, "tensor"),
            P("tensor", "dp"),
            P("tensor", "dp"),
            P("tensor", "dp"),
            P(None, "tensor", "dp"),
            P(None, "tensor", "dp"),
            P(),
            P(),
            P(),
            P(),
            P(),
            P(),
        ),
        check_vma=False,
    )
```
